32 devices in a mesh: row: 4 (over y, x), col: 8 (over z, core).
Axes of the slice: x: 2, y: 2, z: 4, core: 2. Of those that a mesh axis runs over, the one named last changes fastest.
Arguments:
- features: bfloat16 [4, 8, 512, 512], P(None, 'col'), may hold values from -6 to 6
- degree: int32 [4, 8, 512], P(None, 'col'), may hold values from 1 to 16
- tile_vals: bfloat16 [4, 8, 48, 256, 256], P('row', 'col'), may hold values from -0.38085938 to 0.38085938
- tile_slot: int32 [4, 8, 48], P('row', 'col'), may hold values from 0 to 127, as said below
- tile_count: int32 [4, 8], P('row', 'col'), may hold values from 24 to 48, as said below
- w_first: bfloat16 [512, 512], replicated, may hold values from -0.25 to 0.25
- w_second: bfloat16 [512, 512], replicated, may hold values from -0.25 to 0.25
- cotangent: bfloat16 [16384, 512], P(('row', 'col')), may hold values from -6 to 6
Outputs:
- logits: bfloat16 [16384, 512], P(('row', 'col'))
- grad_first: float32 [512, 512], replicated
- grad_second: float32 [512, 512], replicated
The draws below stay inside these ranges and needn't reach their ends.
Inputs may be any that keep to these rules, and one draw needn't show every extreme that they name: `tile_slot`: on each device, the used slots hold distinct positions. `tile_count`: some device uses all 48 slots.
All inputs are finite; a program needn't handle non-finite values.
Results may differ from the reference program's by a relative error of at most 0.025.
Values may be sent and summed in bfloat16 or wider, within the bound.
No kernel may reach another device: no remote copies, remote signals or barrier semaphores. Data moves between devices by JAX's collectives and lax.ppermute only.
A program may use at most 128 MiB of HBM per device.

```python
import jax
import jax.numpy as jnp
from jax import lax

F = 512
TILE = 256
PIECE = 512
TILES_DEV = 48
NODES = 16384
N_ROW = 4
N_COL = 8


def draw_tile_slot(key, part):
    spots = N_ROW * N_COL * (PIECE // TILE) * (PIECE // TILE)
    device_keys = jax.random.split(jax.random.fold_in(key, 11), N_ROW * N_COL)

    def one_device(device_key):
        return jax.random.permutation(device_key, spots)[:TILES_DEV]
    chosen = jax.vmap(one_device)(device_keys)
    return chosen.reshape(N_ROW, N_COL, TILES_DEV).astype(jnp.int32)


def draw_tile_count(key, part):
    counts = jax.random.randint(jax.random.fold_in(key, 21), (N_ROW * N_COL,), TILES_DEV // 2, TILES_DEV + 1)
    chosen = jax.random.permutation(jax.random.fold_in(key, 22), N_ROW * N_COL)
    counts = counts.at[chosen[0]].set(TILES_DEV)
    counts = counts.at[chosen[1]].set(TILES_DEV // 2)
    return counts.reshape(N_ROW, N_COL).astype(jnp.int32)


def touch_ends(values, rng, low, high):
    place = [jax.random.randint(jax.random.fold_in(rng, axis), (), 0, length) for axis, length in enumerate(values.shape)]
    main_axis = values.shape.index(max(values.shape))
    neighbour = place[:main_axis] + [(place[main_axis] + 1) % values.shape[main_axis]] + place[main_axis + 1:]
    return values.at[tuple(place)].set(low).at[tuple(neighbour)].set(high)


def with_spikes(drawn, stream_key, source, target, parts, factor):
    def block_of(axis_at):
        return (jnp.arange(drawn.shape[axis_at]) // (drawn.shape[axis_at] // parts)).reshape((-1,) + (1,) * (drawn.ndim - 1 - axis_at))

    near = jax.random.permutation(stream_key, parts)[block_of(target)]
    second = (block_of(target) + parts // 2) % parts
    return jnp.where((block_of(source) == near) | (block_of(source) == second), factor * drawn, drawn)


def steps_of(own_key, shape, pieces, least, high):
    level, own = 1.0, jax.random.fold_in(own_key, 6)
    for dim, blocks in pieces:
        draws = jnp.exp(jax.random.uniform(jax.random.fold_in(own, dim), (blocks,), jnp.float32, least / len(pieces), high / len(pieces)))
        level = level * jnp.repeat(draws, shape[dim] // blocks).reshape([-1 if axis == dim else 1 for axis in range(len(shape))])
    return level


def scatter_about(own_key, dims, scale, most, pieces=(), kind=jnp.bfloat16):
    values = jax.random.normal(own_key, dims, jnp.float32) * scale
    if len(pieces) > 0:
        values = steps_of(own_key, dims, pieces, -0.22, 0.18) * values
    return jnp.clip(values, min=-most, max=most).astype(kind)


def heavy_noise(own_key, extent, deviation, reach, shards, heavy, held_as=jnp.bfloat16):
    drawn = deviation * jax.random.normal(own_key, extent, jnp.float32)
    if shards:
        drawn = drawn * steps_of(own_key, extent, shards, -0.22, 0.18)
    return jnp.clip(with_spikes(drawn, jax.random.fold_in(own_key, 3), *heavy), -reach, reach).astype(held_as)


def setup_inputs(seed: int = 0) -> dict:
    key_list = jax.random.split(jax.random.key(seed), 9)
    features = scatter_about(key_list[0], (N_ROW, N_COL, PIECE, F), 1.0, 6.0, ((1, 8),))
    degree = touch_ends(jax.random.randint(key_list[1], (N_ROW, N_COL, PIECE), 1, 17), jax.random.fold_in(key_list[1], 1), 1, 16).astype(jnp.int32)
    tile_vals = scatter_about(key_list[2], (N_ROW, N_COL, TILES_DEV, TILE, TILE), (5.0 * (PIECE // TILE) ** 0.5 / (TILE * TILES_DEV) ** 0.5), 0.38085938, ((0, 4), (1, 8)))
    tile_slot = draw_tile_slot(jax.random.fold_in(key_list[8], 71), 0)
    tile_count = draw_tile_count(jax.random.fold_in(key_list[8], 71), 0)
    w_first = scatter_about(key_list[5], (F, F), F ** -0.5, 0.25)
    w_second = scatter_about(key_list[6], (F, F), F ** -0.5, 0.25)
    cotangent = heavy_noise(key_list[7], (NODES, F), 1.0, 6.0, ((0, 32),), (0, 1, 32, 2.75))
    return {"features": features, "degree": degree, "tile_vals": tile_vals, "tile_slot": tile_slot, "tile_count": tile_count, "w_first": w_first, "w_second": w_second, "cotangent": cotangent}


def forward_partial(tiles_here, slots_here, number, source, row_total):
    tile_edge = tiles_here.shape[-1]
    local_cols = source.shape[0] // tile_edge

    def advance(running, element):
        position, tile_now, slot_id = element
        row_start = slot_id // local_cols * tile_edge
        col_start = slot_id % local_cols * tile_edge
        segment = lax.dynamic_slice_in_dim(source, col_start, tile_edge, 0)
        product = jnp.dot(tile_now, segment, preferred_element_type=jnp.float32)
        product = jnp.where(position < number, product, jnp.zeros_like(product))
        previous = lax.dynamic_slice_in_dim(running, row_start, tile_edge, 0)
        return (lax.dynamic_update_slice_in_dim(running, previous + product, row_start, 0), None)
    zeroed = jnp.zeros((row_total, source.shape[1]), jnp.float32)
    indices = jnp.arange(tiles_here.shape[0], dtype=jnp.int32)
    result, _ = lax.scan(advance, zeroed, (indices, tiles_here, slots_here))
    return result

def backward_partial(tiles_here, slots_here, number, source, row_total):
    tile_edge = tiles_here.shape[-1]
    local_cols = row_total // tile_edge

    def advance(running, element):
        position, tile_now, slot_id = element
        row_start = slot_id % local_cols * tile_edge
        col_start = slot_id // local_cols * tile_edge
        segment = lax.dynamic_slice_in_dim(source, col_start, tile_edge, 0)
        product = lax.dot_general(tile_now, segment, (((0,), (0,)), ((), ())), preferred_element_type=jnp.float32)
        product = jnp.where(position < number, product, jnp.zeros_like(product))
        previous = lax.dynamic_slice_in_dim(running, row_start, tile_edge, 0)
        return (lax.dynamic_update_slice_in_dim(running, previous + product, row_start, 0), None)
    zeroed = jnp.zeros((row_total, source.shape[1]), jnp.float32)
    indices = jnp.arange(tiles_here.shape[0], dtype=jnp.int32)
    result, _ = lax.scan(advance, zeroed, (indices, tiles_here, slots_here))
    return result

def aggregate(tile_vals, tile_slot, tile_count, scaled):
    blocks = scaled.reshape(N_ROW, N_COL, PIECE, F)

    def per_row(row_id):

        def per_col(running, col_id):
            source = blocks[:, col_id].reshape(N_ROW * PIECE, F)
            partial_value = forward_partial(tile_vals[row_id, col_id], tile_slot[row_id, col_id], tile_count[row_id, col_id], source, N_COL * PIECE)
            return (running + lax.optimization_barrier(partial_value.astype(jnp.bfloat16)).astype(jnp.float32), None)
        zeroed = jnp.zeros((N_COL * PIECE, F), jnp.float32)
        result, _ = lax.scan(per_col, zeroed, jnp.arange(N_COL, dtype=jnp.int32))
        return result
    return lax.map(per_row, jnp.arange(N_ROW, dtype=jnp.int32)).reshape(NODES, F)

def transpose_aggregate(tile_vals, tile_slot, tile_count, scaled):
    ranges = scaled.reshape(N_ROW, N_COL * PIECE, F)

    def per_col(col_id):

        def per_row(running, row_id):
            partial_value = backward_partial(tile_vals[row_id, col_id], tile_slot[row_id, col_id], tile_count[row_id, col_id], ranges[row_id], N_ROW * PIECE)
            return (running + lax.optimization_barrier(partial_value.astype(jnp.bfloat16)).astype(jnp.float32), None)
        zeroed = jnp.zeros((N_ROW * PIECE, F), jnp.float32)
        result, _ = lax.scan(per_row, zeroed, jnp.arange(N_ROW, dtype=jnp.int32))
        return result
    result = lax.map(per_col, jnp.arange(N_COL, dtype=jnp.int32))
    result = result.reshape(N_COL, N_ROW, PIECE, F).transpose(1, 0, 2, 3)
    return result.reshape(NODES, F)

def reference(features, degree, tile_vals, tile_slot, tile_count, w_first, w_second, cotangent):
    scaling = (1.0 / jnp.sqrt(degree.astype(jnp.float32))).reshape(NODES, 1)
    inputs = features.reshape(NODES, F)
    first_in = (inputs.astype(jnp.float32) * scaling).astype(jnp.bfloat16)
    first_agg = (aggregate(tile_vals, tile_slot, tile_count, first_in) * scaling).astype(jnp.bfloat16)
    first_pre = jnp.dot(first_agg, w_first, preferred_element_type=jnp.float32)
    first_out = (jax.nn.gelu(first_pre) * scaling).astype(jnp.bfloat16)
    second_agg = (aggregate(tile_vals, tile_slot, tile_count, first_out) * scaling).astype(jnp.bfloat16)
    logits = jnp.dot(second_agg, w_second, preferred_element_type=jnp.float32).astype(jnp.bfloat16)
    grad_agg = lax.dot_general(cotangent, w_second, (((1,), (1,)), ((), ())), preferred_element_type=jnp.float32)
    grad_agg = (grad_agg * scaling).astype(jnp.bfloat16)
    grad_hidden = transpose_aggregate(tile_vals, tile_slot, tile_count, grad_agg)
    _, pullback = jax.vjp(jax.nn.gelu, first_pre)
    grad_pre = pullback(grad_hidden * scaling)[0].astype(jnp.bfloat16)
    grad_first = lax.dot_general(first_agg, grad_pre, (((0,), (0,)), ((), ())), preferred_element_type=jnp.float32)
    grad_second = lax.dot_general(second_agg, cotangent, (((0,), (0,)), ((), ())), preferred_element_type=jnp.float32)
    return (logits, grad_first, grad_second)
```

```python
import functools

import jax
import jax.numpy as jnp
from jax import lax
from jax.experimental import pallas as pl
from jax.experimental.pallas import tpu as pltpu
from jax.sharding import PartitionSpec as P

F32 = jnp.float32
BF16 = jnp.bfloat16
VMEM_BYTES = 44 * 1024 * 1024
VMEM = pl.BlockSpec(memory_space=pltpu.VMEM)
SMEM = pl.BlockSpec(memory_space=pltpu.SMEM)
ANY = pl.BlockSpec(memory_space=pl.ANY)


def nbytes(items):
    return sum(x.size * x.dtype.itemsize for x in items)


def run(body, args, specs, outs, scratch=(), flops=0, trans=0):
    return pl.pallas_call(
        body,
        out_shape=outs,
        in_specs=specs,
        out_specs=[VMEM] * len(outs),
        scratch_shapes=list(scratch),
        compiler_params=pltpu.CompilerParams(vmem_limit_bytes=VMEM_BYTES),
        cost_estimate=pl.CostEstimate(
            flops=flops, bytes_accessed=nbytes(args) + nbytes(outs), transcendentals=trans
        ),
    )(*args)


def shape(dims, dtype=BF16):
    return jax.ShapeDtypeStruct(dims, dtype)


def sort_tiles(count_ref, slot_ref, number_ref, list_ref, local_cols, groups, cap, by_row):
    def clear(g, _):
        number_ref[g] = 0
        return 0

    lax.fori_loop(0, groups, clear, 0)

    def place(s, _):
        p = slot_ref[s]
        u, v = lax.div(p, local_cols), lax.rem(p, local_cols)
        g, other = (u, v) if by_row else (v, u)
        n = number_ref[g]
        list_ref[g * cap + n] = s * 1024 + other
        number_ref[g] = n + 1
        return 0

    lax.fori_loop(0, count_ref[0], place, 0)


def tile_copy(tiles_ref, held, sems, s):
    return pltpu.make_async_copy(tiles_ref.at[s], held.at[s], sems.at[s])


def start_group(g, tiles_ref, held, sems, number_ref, list_ref, cap):
    def one(j, _):
        tile_copy(tiles_ref, held, sems, list_ref[g * cap + j] // 1024).start()
        return 0

    lax.fori_loop(0, number_ref[g], one, 0)


def sum_group(g, tiles_ref, held, sems, number_ref, list_ref, cap, total, product):
    n = number_ref[g]
    odd = lax.rem(n, 2)

    def fetch(j):
        entry = list_ref[g * cap + j]
        s = entry // 1024
        tile_copy(tiles_ref, held, sems, s).wait()
        return s, lax.rem(entry, 1024)

    @pl.when(odd == 1)
    def _():
        total[...] = product([fetch(0)])

    @pl.when(odd == 0)
    def _():
        total[...] = jnp.zeros_like(total)

    def pair(m, _):
        first = fetch(odd + 2 * m)
        second = fetch(odd + 2 * m + 1)
        total[...] += product([first, second])
        return 0

    lax.fori_loop(0, lax.div(n, 2), pair, 0)


def forward_body(scaled, half, local_cols, cap, *refs):
    count_ref, slot_ref, tiles_ref = refs[:3]
    give, keep, held, source, total, sems, source_sems, number_ref, list_ref = refs[-9:]
    inputs = refs[3:-9]
    col = lax.axis_index("col")
    parts = give.shape[0]
    sort_tiles(count_ref, slot_ref, number_ref, list_ref, local_cols, 4 * parts, cap, True)

    def block_row(i, flip):
        return (col ^ (2 * i + flip)) * 2 + half

    if scaled:
        mask = 0
    else:
        mask = lax.axis_index("row") * 2
        copies = [
            pltpu.make_async_copy(x, source.at[i], source_sems.at[i]) for i, x in enumerate(inputs)
        ]
        for copy in copies:
            copy.start()
    for flip in (1, 0):

        def start(i, _):
            start_group(block_row(i, flip), tiles_ref, held, sems, number_ref, list_ref, cap)
            return 0

        lax.fori_loop(0, parts, start, 0)
    if scaled:
        values, scale = inputs

        def fill(i, _):
            source[i] = (values[i].astype(F32) * scale[i]).astype(BF16)
            return 0

        lax.fori_loop(0, local_cols, fill, 0)
    else:
        for copy in copies:
            copy.wait()

    def product(pieces):
        lhs = [held[s] for s, _ in pieces]
        rhs = [source[v ^ mask] for _, v in pieces]
        return jnp.dot(
            jnp.concatenate(lhs, 1), jnp.concatenate(rhs, 0), preferred_element_type=F32
        )

    for flip, out in ((1, give), (0, keep)):

        def block(i, _):
            sum_group(
                block_row(i, flip), tiles_ref, held, sems, number_ref, list_ref, cap, total, product
            )
            out[i] = total[...].astype(BF16)
            return 0

        lax.fori_loop(0, parts, block, 0)


def forward(count, slots, tiles, sources, scaled, half, local_cols, n_col):
    slots_n, edge, _ = tiles.shape
    width = sources[0].shape[-1]
    outs = [shape((n_col // 2, edge, width))] * 2
    return run(
        functools.partial(forward_body, scaled, half, local_cols, local_cols),
        (count, slots, tiles, *sources),
        [SMEM, SMEM, ANY] + ([VMEM] if scaled else [ANY]) * len(sources),
        outs,
        [
            pltpu.VMEM(tiles.shape, BF16),
            pltpu.VMEM((local_cols, edge, width), BF16),
            pltpu.VMEM((edge, width), F32),
            pltpu.SemaphoreType.DMA((slots_n,)),
            pltpu.SemaphoreType.DMA((local_cols,)),
            pltpu.SMEM((2 * n_col,), jnp.int32),
            pltpu.SMEM((2 * n_col * local_cols,), jnp.int32),
        ],
        flops=slots_n * edge * edge * width,
    )


def backward_body(local_cols, cap, n_in, *refs):
    count_ref, slot_ref, tiles_ref = refs[:3]
    inputs = refs[3 : 3 + n_in]
    outs = refs[3 + n_in : -7]
    held, source, total, sems, source_sems, number_ref, list_ref = refs[-7:]
    sort_tiles(count_ref, slot_ref, number_ref, list_ref, local_cols, local_cols, cap, False)
    mask = lax.axis_index("col") * 2
    row = lax.axis_index("row")
    copies = [
        pltpu.make_async_copy(x, source.at[pl.ds(2 * i, 2)], source_sems.at[i])
        for i, x in enumerate(inputs)
    ]
    for copy in copies:
        copy.start()
    order = list(range(1, len(outs))) + [0]
    for j in order:
        for e in range(2):
            start_group(
                (row ^ j) * 2 + e, tiles_ref, held, sems, number_ref, list_ref, cap
            )
    for copy in copies:
        copy.wait()

    def product(pieces):
        lhs = [source[u ^ mask] for _, u in pieces]
        rhs = [held[s] for s, _ in pieces]
        return jnp.dot(
            jnp.concatenate(lhs, 1), jnp.concatenate(rhs, 0), preferred_element_type=F32
        )

    for j in order:

        def block(e, _):
            sum_group(
                (row ^ j) * 2 + e, tiles_ref, held, sems, number_ref, list_ref, cap, total, product
            )
            outs[j][e] = total[...].astype(BF16)
            return 0

        lax.fori_loop(0, 2, block, 0)


def backward(count, slots, tiles, sources, n_row, n_col):
    slots_n, edge, _ = tiles.shape
    _, width, _ = sources[0].shape
    local_cols, block_rows = 2 * n_row, 2 * n_col
    return run(
        functools.partial(backward_body, local_cols, block_rows, len(sources)),
        (count, slots, tiles, *sources),
        [SMEM, SMEM, ANY] + [ANY] * len(sources),
        [shape((2, width, edge))] * n_row,
        [
            pltpu.VMEM(tiles.shape, BF16),
            pltpu.VMEM((block_rows, width, edge), BF16),
            pltpu.VMEM((width, edge), F32),
            pltpu.SemaphoreType.DMA((slots_n,)),
            pltpu.SemaphoreType.DMA((len(sources),)),
            pltpu.SMEM((local_cols,), jnp.int32),
            pltpu.SMEM((block_rows * local_cols,), jnp.int32),
        ],
        flops=2 * slots_n * edge * edge * width,
    )


def pair_sum_body(n, keep, come, *outs):
    for j in range(n):
        outs[j][...] = (keep[j].astype(F32) + come[j].astype(F32)).astype(BF16)


def pair_sum(keep, come):
    n = keep.shape[0]
    return run(
        functools.partial(pair_sum_body, n),
        (keep, come),
        [VMEM] * 2,
        [shape(keep.shape[1:])] * n,
        flops=keep.size,
    )


def tree(items):
    while len(items) > 1:
        items = [a + b for a, b in zip(items[::2], items[1::2])]
    return items[0]


def first_body(n, *refs):
    scale, weight = refs[n], refs[n + 1]
    agg, pre, out = refs[n + 2 :]
    summed = tree([x[...].astype(F32) for x in refs[:n]])
    agg[...] = (summed * scale[...]).astype(BF16)
    value = jnp.dot(agg[...], weight[...], preferred_element_type=F32)
    pre[...] = value
    out[...] = (jax.nn.gelu(value) * scale[...]).astype(BF16)


def first_layer(parts, scale, weight):
    dims = parts[0].shape
    return run(
        functools.partial(first_body, len(parts)),
        (*parts, scale, weight),
        [VMEM] * (len(parts) + 2),
        [shape(dims), shape(dims, F32), shape(dims)],
        flops=2 * dims[0] * weight.size,
        trans=dims[0] * dims[1],
    )


def second_body(n, *refs):
    scale, weight, out = refs[n], refs[n + 1], refs[n + 2]
    summed = tree([x[...].astype(F32) for x in refs[:n]])
    agg = (summed * scale[...]).astype(BF16)
    out[...] = jnp.dot(agg, weight[...], preferred_element_type=F32).astype(BF16)


def second_layer(parts, scale, weight):
    dims = parts[0].shape
    return run(
        functools.partial(second_body, len(parts)),
        (*parts, scale, weight),
        [VMEM] * (len(parts) + 2),
        [shape(dims)],
        flops=2 * dims[0] * weight.size,
    )[0]


def grad_body(n, *refs):
    parts = refs[:n]
    (agg0, agg1, pre0, pre1, out0, out1, scale, weight, give, keep) = refs[n:]
    core = lax.rem(lax.axis_index("col"), 2)
    first, second = 0.0, 0.0
    for e, (agg, pre, out) in enumerate(((agg0, pre0, out0), (agg1, pre1, out1))):
        hidden = tree([x[e].astype(F32) for x in parts]).astype(BF16)
        grad_hidden = lax.dot_general(
            hidden, weight[...], (((0,), (1,)), ((), ())), preferred_element_type=F32
        )
        _, pullback = jax.vjp(jax.nn.gelu, pre[...])
        grad_pre = pullback(grad_hidden * scale[e])[0].astype(BF16)
        first += lax.dot_general(
            agg[...], grad_pre, (((0,), (0,)), ((), ())), preferred_element_type=F32
        )
        second += lax.dot_general(
            out[...], hidden, (((0,), (1,)), ((), ())), preferred_element_type=F32
        )
    keep[...] = jnp.where(core == 0, first, second).astype(BF16)
    give[...] = jnp.where(core == 0, second, first).astype(BF16)


def weight_grads(parts, aggs, pres, outs, scale, weight):
    return run(
        functools.partial(grad_body, len(parts)),
        (*parts, *aggs, *pres, *outs, scale, weight),
        [VMEM] * (len(parts) + 8),
        [shape(weight.shape)] * 2,
        flops=6 * parts[0].size * weight.shape[0],
        trans=parts[0].size,
    )


def split_body(n, keep, come, *outs):
    row = lax.axis_index("row")
    rows = keep.shape[0] // n
    for j in range(n):
        part = pl.ds(pl.multiple_of((row ^ j) * rows, rows), rows)
        outs[j][...] = (keep[part, :].astype(F32) + come[part, :].astype(F32)).astype(BF16)


def split_sum(keep, come, n):
    rows, width = keep.shape
    return run(
        functools.partial(split_body, n),
        (keep, come),
        [VMEM] * 2,
        [shape((rows // n, width))] * n,
        flops=keep.size,
    )


def sum_body(n, *refs):
    refs[n][...] = tree([x[...].astype(F32) for x in refs[:n]]).astype(BF16)


def sum_parts(parts):
    return run(
        functools.partial(sum_body, len(parts)),
        tuple(parts),
        [VMEM] * len(parts),
        [shape(parts[0].shape)],
        flops=parts[0].size * len(parts),
    )[0]


def join_body(n, *refs):
    row = lax.axis_index("row")
    rows = refs[0].shape[0]
    for j in range(n):
        refs[n][pl.ds(pl.multiple_of((row ^ j) * rows, rows), rows), :] = refs[j][...]


def join(parts):
    rows, width = parts[0].shape
    return run(
        functools.partial(join_body, len(parts)),
        tuple(parts),
        [VMEM] * len(parts),
        [shape((rows * len(parts), width))],
    )[0]


def per_device(features, degree, tile_vals, tile_slot, tile_count, w_first, w_second, cotangent):
    n_row, n_col = lax.axis_size("row"), lax.axis_size("col")
    line = n_col // 2
    piece, width = cotangent.shape
    tiles = tile_vals[0, 0]
    edge = tiles.shape[-1]
    local_cols = n_row * 2
    slots, count = tile_slot[0, 0], tile_count[0]

    def col_send(value, pairs):
        return lax.ppermute(
            value, "col", [(2 * a + k, 2 * b + k) for a, b in pairs for k in range(2)]
        )

    def line_flip(value, j):
        return col_send(value, [(a, a ^ j) for a in range(line)])

    def core_flip(value):
        return lax.ppermute(value, "col", [(a, a ^ 1) for a in range(n_col)])

    def row_flip(value, j):
        return lax.ppermute(value, "row", [(a, a ^ j) for a in range(n_row)])

    def scatter_col(give, keep):
        own = pair_sum(keep, core_flip(give))
        if line != 4:
            return [own[0]] + [line_flip(own[j], j) for j in range(1, line)]
        inward = col_send(own[3], [(0, 1), (3, 2)])
        middle = col_send(own[3], [(1, 2), (2, 1)])
        near = line_flip(own[1], 1)
        far = line_flip((own[2].astype(F32) + inward.astype(F32)).astype(BF16), 2)
        return [own[0], near, middle, far]

    def gather_line(own):
        if line != 4:
            return [own] + [line_flip(own, j) for j in range(1, line)]
        position = lax.axis_index("col") // 2
        at_end = jnp.logical_or(position == 0, position == line - 1)
        near = line_flip(own, 1)
        middle = col_send(own, [(1, 2), (2, 1)])
        across = col_send(near, [(1, 2), (2, 1)])
        out_two = col_send(middle, [(1, 0), (2, 3)])
        out_three = col_send(across, [(1, 0), (2, 3)])
        return [
            own,
            near,
            jnp.where(at_end, out_two, across),
            jnp.where(at_end, out_three, middle),
        ]

    col_scale = (1.0 / jnp.sqrt(degree.astype(F32))).reshape(local_cols, edge, 1)
    own_scale = lax.dynamic_slice_in_dim(col_scale, lax.axis_index("row") * 2, 2, 0)
    halves = piece // edge

    scaled = (
        (cotangent.astype(F32) * own_scale.reshape(piece, 1))
        .astype(BF16)
        .reshape(halves, edge, width)
        .transpose(0, 2, 1)
    )
    gathered = gather_line(scaled)
    ranged = [x for g in gathered for x in (g, core_flip(g))]

    values = features[:, 0].reshape(local_cols, edge, width)
    aggs, pres, outs, spread = [], [], [], []
    for half in range(halves):
        give, keep = forward(
            count, slots, tiles, (values, col_scale), True, half, local_cols, n_col
        )
        agg, pre, out = first_layer(scatter_col(give, keep), own_scale[half], w_first)
        aggs.append(agg)
        pres.append(pre)
        outs.append(out)
        spread.append([out] + [row_flip(out, j) for j in range(1, n_row)])
    sources = [spread[e][j] for j in range(n_row) for e in range(halves)]

    partials = backward(count, slots, tiles, ranged, n_row, n_col)
    hidden = [partials[0]] + [row_flip(partials[j], j) for j in range(1, n_row)]
    give, keep = weight_grads(hidden, aggs, pres, outs, own_scale, w_second)
    parts = split_sum(keep, core_flip(give), n_row)
    part = sum_parts([parts[0]] + [row_flip(parts[j], j) for j in range(1, n_row)])
    part = sum_parts([part] + [line_flip(part, j) for j in range(1, line)])
    mine = join([part] + [row_flip(part, j) for j in range(1, n_row)])
    other = core_flip(mine)
    core = lax.rem(lax.axis_index("col"), 2)
    grad_first = jnp.where(core == 0, mine, other).astype(F32)
    grad_second = jnp.where(core == 0, other, mine).astype(F32)

    logits = []
    for half in range(halves):
        give, keep = forward(count, slots, tiles, sources, False, half, local_cols, n_col)
        logits.append(second_layer(scatter_col(give, keep), own_scale[half], w_second))
    return jnp.concatenate(logits, 0), grad_first, grad_second


def solution(mesh):
    return jax.shard_map(
        per_device,
        mesh=mesh,
        in_specs=(
            P(None, "col", None, None),
            P(None, "col", None),
            P("row", "col", None, None, None),
            P("row", "col", None),
            P("row", "col"),
            P(),
            P(),
            P(("row", "col"), None),
        ),
        out_specs=(P(("row", "col"), None), P(), P()),
        check_vma=False,
    )
```

```python
import functools

import jax
import jax.numpy as jnp
from jax import lax
from jax.experimental import pallas as pl
from jax.experimental.pallas import tpu as pltpu
from jax.sharding import PartitionSpec as P

F32 = jnp.float32
BF16 = jnp.bfloat16
MIB = 1024 * 1024
VMEM = pl.BlockSpec(memory_space=pltpu.VMEM)
SMEM = pl.BlockSpec(memory_space=pltpu.SMEM)
ANY = pl.BlockSpec(memory_space=pl.ANY)


def nbytes(items):
    return sum(x.size * x.dtype.itemsize for x in items)


def run(body, args, specs, outs, scratch=(), flops=0, trans=0, mib=8, after=()):
    n, extra = len(args), len(after)

    def whole(*refs):
        body(*refs[:n], *refs[n + extra :])

    return pl.pallas_call(
        whole,
        out_shape=outs,
        in_specs=specs + [ANY] * extra,
        out_specs=[VMEM] * len(outs),
        scratch_shapes=list(scratch),
        compiler_params=pltpu.CompilerParams(vmem_limit_bytes=mib * MIB),
        cost_estimate=pl.CostEstimate(
            flops=flops, bytes_accessed=nbytes(args) + nbytes(outs), transcendentals=trans
        ),
    )(*args, *after)


def shape(dims, dtype=BF16):
    return jax.ShapeDtypeStruct(dims, dtype)


def sort_tiles(count_ref, slot_ref, number_ref, list_ref, local_cols, groups, cap, by_row):
    def clear(g, _):
        number_ref[g] = 0
        return 0

    lax.fori_loop(0, groups, clear, 0)

    def place(s, _):
        p = slot_ref[s]
        u, v = lax.div(p, local_cols), lax.rem(p, local_cols)
        g, other = (u, v) if by_row else (v, u)
        n = number_ref[g]
        list_ref[g * cap + n] = s * 1024 + other
        number_ref[g] = n + 1
        return 0

    lax.fori_loop(0, count_ref[0], place, 0)


def tile_copy(tiles_ref, held, sems, s):
    return pltpu.make_async_copy(tiles_ref.at[s], held.at[s], sems.at[s])


def start_group(g, tiles_ref, held, sems, number_ref, list_ref, cap):
    def one(j, _):
        tile_copy(tiles_ref, held, sems, list_ref[g * cap + j] // 1024).start()
        return 0

    lax.fori_loop(0, number_ref[g], one, 0)


def sum_group(g, tiles_ref, held, sems, number_ref, list_ref, cap, total, product):
    n = number_ref[g]
    odd = lax.rem(n, 2)

    def fetch(j):
        entry = list_ref[g * cap + j]
        s = entry // 1024
        tile_copy(tiles_ref, held, sems, s).wait()
        return s, lax.rem(entry, 1024)

    @pl.when(odd == 1)
    def _():
        total[...] = product([fetch(0)])

    @pl.when(odd == 0)
    def _():
        total[...] = jnp.zeros_like(total)

    def pair(m, _):
        first = fetch(odd + 2 * m)
        second = fetch(odd + 2 * m + 1)
        total[...] += product([first, second])
        return 0

    lax.fori_loop(0, lax.div(n, 2), pair, 0)


def forward_body(scaled, half, local_cols, cap, *refs):
    count_ref, slot_ref, tiles_ref = refs[:3]
    give, keep, held, source, total, sems, source_sems, number_ref, list_ref = refs[-9:]
    inputs = refs[3:-9]
    col = lax.axis_index("col")
    parts = give.shape[0]
    sort_tiles(count_ref, slot_ref, number_ref, list_ref, local_cols, 4 * parts, cap, True)

    def block_row(i, flip):
        return (col ^ (2 * i + flip)) * 2 + half

    row = lax.axis_index("row")
    n_row = local_cols // 2
    if not scaled:
        copies = [
            pltpu.make_async_copy(x, source.at[pl.ds(i * n_row, n_row)], source_sems.at[i])
            for i, x in enumerate(inputs)
        ]
        for copy in copies:
            copy.start()

    def locate(v):
        return v if scaled else lax.rem(v, 2) * n_row + (lax.div(v, 2) ^ row)

    for flip in (1, 0):

        def start(i, _):
            start_group(block_row(i, flip), tiles_ref, held, sems, number_ref, list_ref, cap)
            return 0

        lax.fori_loop(0, parts, start, 0)
    if scaled:
        values, scale = inputs

        def fill(i, _):
            source[i] = (values[i].astype(F32) * scale[i]).astype(BF16)
            return 0

        lax.fori_loop(0, local_cols, fill, 0)
    else:
        for copy in copies:
            copy.wait()

    def product(pieces):
        lhs = [held[s] for s, _ in pieces]
        rhs = [source[locate(v)] for _, v in pieces]
        return jnp.dot(
            jnp.concatenate(lhs, 1), jnp.concatenate(rhs, 0), preferred_element_type=F32
        )

    for flip, out in ((1, give), (0, keep)):

        def block(i, _):
            sum_group(
                block_row(i, flip), tiles_ref, held, sems, number_ref, list_ref, cap, total, product
            )
            out[i] = total[...].astype(BF16)
            return 0

        lax.fori_loop(0, parts, block, 0)


def forward(count, slots, tiles, sources, scaled, half, local_cols, n_col, after):
    slots_n, edge, _ = tiles.shape
    width = sources[0].shape[-1]
    outs = [shape((n_col // 2, edge, width))] * 2
    return run(
        functools.partial(forward_body, scaled, half, local_cols, local_cols),
        (count, slots, tiles, *sources),
        [SMEM, SMEM, ANY] + ([VMEM] if scaled else [ANY]) * len(sources),
        outs,
        [
            pltpu.VMEM(tiles.shape, BF16),
            pltpu.VMEM((local_cols, edge, width), BF16),
            pltpu.VMEM((edge, width), F32),
            pltpu.SemaphoreType.DMA((slots_n,)),
            pltpu.SemaphoreType.DMA((2,)),
            pltpu.SMEM((2 * n_col,), jnp.int32),
            pltpu.SMEM((2 * n_col * local_cols,), jnp.int32),
        ],
        flops=slots_n * edge * edge * width,
        mib=20,
        after=after,
    )


def backward_body(local_cols, cap, *refs):
    count_ref, slot_ref, tiles_ref, ranged, out = refs[:5]
    held, source, total, sems, source_sem, number_ref, list_ref = refs[5:]
    sort_tiles(count_ref, slot_ref, number_ref, list_ref, local_cols, local_cols, cap, False)
    mask = lax.axis_index("row") * 2
    copy = pltpu.make_async_copy(ranged, source, source_sem)
    copy.start()

    def start(i, _):
        start_group(i ^ mask, tiles_ref, held, sems, number_ref, list_ref, cap)
        return 0

    lax.fori_loop(0, local_cols, start, 0)
    copy.wait()

    def product(pieces):
        lhs = [source[u] for _, u in pieces]
        rhs = [held[s] for s, _ in pieces]
        return jnp.dot(
            jnp.concatenate(lhs, 1), jnp.concatenate(rhs, 0), preferred_element_type=F32
        )

    def block(i, _):
        sum_group(
            i ^ mask, tiles_ref, held, sems, number_ref, list_ref, cap, total, product
        )
        out[i] = total[...].astype(BF16)
        return 0

    lax.fori_loop(0, local_cols, block, 0)


def backward(count, slots, tiles, ranged, n_row):
    slots_n, edge, _ = tiles.shape
    block_rows, width, _ = ranged.shape
    local_cols = 2 * n_row
    return run(
        functools.partial(backward_body, local_cols, block_rows),
        (count, slots, tiles, ranged),
        [SMEM, SMEM, ANY, ANY],
        [shape((local_cols, width, edge))],
        [
            pltpu.VMEM(tiles.shape, BF16),
            pltpu.VMEM(ranged.shape, BF16),
            pltpu.VMEM((width, edge), F32),
            pltpu.SemaphoreType.DMA((slots_n,)),
            pltpu.SemaphoreType.DMA,
            pltpu.SMEM((local_cols,), jnp.int32),
            pltpu.SMEM((block_rows * local_cols,), jnp.int32),
        ],
        flops=2 * slots_n * edge * edge * width,
        mib=20,
    )[0]


def pair_sum_body(n, keep, come, *outs):
    for j in range(n):
        outs[j][...] = (keep[j].astype(F32) + come[j].astype(F32)).astype(BF16)


def pair_sum(keep, come):
    n = keep.shape[0]
    return run(
        functools.partial(pair_sum_body, n),
        (keep, come),
        [VMEM] * 2,
        [shape(keep.shape[1:])] * n,
        flops=keep.size,
    )


def tree(items):
    while len(items) > 1:
        items = [a + b for a, b in zip(items[::2], items[1::2])]
    return items[0]


def scaled_body(cot, scale, out):
    row = lax.axis_index("row")
    edge = out.shape[2]
    for e in range(out.shape[0]):
        value = cot[e * edge : (e + 1) * edge, :].astype(F32) * scale[row * 2 + e]
        out[e] = value.T.astype(BF16)


def scaled_transposed(cotangent, scale):
    _, edge, _ = scale.shape
    rows, width = cotangent.shape
    return run(
        scaled_body,
        (cotangent, scale),
        [VMEM] * 2,
        [shape((rows // edge, width, edge))],
        flops=cotangent.size,
    )[0]


def agg_body(n, half, *refs):
    scale, out = refs[n], refs[n + 1]
    summed = tree([x[...].astype(F32) for x in refs[:n]])
    out[...] = (summed * scale[lax.axis_index("row") * 2 + half]).astype(BF16)


def aggregate(parts, scale, half, after):
    return run(
        functools.partial(agg_body, len(parts), half),
        (*parts, scale),
        [VMEM] * (len(parts) + 1),
        [shape(parts[0].shape)],
        flops=parts[0].size * len(parts),
        after=after,
    )[0]


def first_body(n, half, *refs):
    scale, weight, agg, out = refs[n:]
    row = lax.axis_index("row")
    for j in range(n):
        value = jnp.dot(refs[j][...], weight[...], preferred_element_type=F32)
        out[j] = (jax.nn.gelu(value) * scale[(row ^ j) * 2 + half]).astype(BF16)
        agg[j] = refs[j][...]


def first_layer(aggs, scale, weight, half, after):
    n = len(aggs)
    dims = (n, *aggs[0].shape)
    return run(
        functools.partial(first_body, n, half),
        (*aggs, scale, weight),
        [VMEM] * (n + 2),
        [shape(dims)] * 2,
        flops=2 * n * dims[1] * weight.size,
        trans=n * aggs[0].size,
        mib=12,
        after=after,
    )


def second_body(n, half, *refs):
    scale, weight, out = refs[n:]
    summed = tree([x[...].astype(F32) for x in refs[:n]])
    agg = (summed * scale[lax.axis_index("row") * 2 + half]).astype(BF16)
    out[...] = jnp.dot(agg, weight[...], preferred_element_type=F32).astype(BF16)


def second_layer(parts, scale, weight, half):
    dims = parts[0].shape
    return run(
        functools.partial(second_body, len(parts), half),
        (*parts, scale, weight),
        [VMEM] * (len(parts) + 2),
        [shape(dims)],
        flops=2 * dims[0] * weight.size,
    )[0]


def grad_body(hidden_ref, *refs):
    aggs, outs = refs[:2], refs[2:4]
    scale, w_first, w_second, give, keep, first, second = refs[4:]
    row = lax.axis_index("row")
    core = lax.rem(lax.axis_index("col"), 2)
    first[...] = jnp.zeros_like(first)
    second[...] = jnp.zeros_like(second)
    for e in range(2):

        def block(j, _):
            hidden, agg = hidden_ref[2 * j + e], aggs[e][j]
            pre = jnp.dot(agg, w_first[...], preferred_element_type=F32)
            grad_hidden = lax.dot_general(
                hidden, w_second[...], (((0,), (1,)), ((), ())), preferred_element_type=F32
            )
            _, pullback = jax.vjp(jax.nn.gelu, pre)
            grad_pre = pullback(grad_hidden * scale[(row ^ j) * 2 + e])[0].astype(BF16)
            first[...] += lax.dot_general(
                agg, grad_pre, (((0,), (0,)), ((), ())), preferred_element_type=F32
            )
            second[...] += lax.dot_general(
                outs[e][j], hidden, (((0,), (1,)), ((), ())), preferred_element_type=F32
            )
            return 0

        lax.fori_loop(0, aggs[e].shape[0], block, 0)
    keep[...] = jnp.where(core == 0, first[...], second[...]).astype(BF16)
    give[...] = jnp.where(core == 0, second[...], first[...]).astype(BF16)


def weight_grads(hidden, aggs, outs, scale, w_first, w_second, after):
    return run(
        grad_body,
        (hidden, *aggs, *outs, scale, w_first, w_second),
        [VMEM] * 8,
        [shape(w_first.shape)] * 2,
        [pltpu.VMEM(w_first.shape, F32)] * 2,
        flops=8 * hidden.size * w_first.shape[0],
        trans=hidden.size,
        mib=28,
        after=after,
    )


def split_body(n, keep, come, *outs):
    row = lax.axis_index("row")
    rows = keep.shape[0] // n
    for j in range(n):
        part = pl.ds(pl.multiple_of((row ^ j) * rows, rows), rows)
        outs[j][...] = (keep[part, :].astype(F32) + come[part, :].astype(F32)).astype(BF16)


def split_sum(keep, come, n, after):
    rows, width = keep.shape
    return run(
        functools.partial(split_body, n),
        (keep, come),
        [VMEM] * 2,
        [shape((rows // n, width))] * n,
        flops=keep.size,
        after=after,
    )


def sum_body(n, *refs):
    refs[n][...] = tree([x[...].astype(F32) for x in refs[:n]]).astype(BF16)


def sum_parts(parts, after=()):
    return run(
        functools.partial(sum_body, len(parts)),
        tuple(parts),
        [VMEM] * len(parts),
        [shape(parts[0].shape)],
        flops=parts[0].size * len(parts),
        after=after,
    )[0]


def join_body(n, *refs):
    row = lax.axis_index("row")
    rows = refs[0].shape[0]
    for j in range(n):
        refs[n][pl.ds(pl.multiple_of((row ^ j) * rows, rows), rows), :] = refs[j][...]


def join(parts):
    rows, width = parts[0].shape
    return run(
        functools.partial(join_body, len(parts)),
        tuple(parts),
        [VMEM] * len(parts),
        [shape((rows * len(parts), width))],
    )[0]


def per_device(features, degree, tile_vals, tile_slot, tile_count, w_first, w_second, cotangent):
    n_row, n_col = lax.axis_size("row"), lax.axis_size("col")
    line = n_col // 2
    piece, width = cotangent.shape
    tiles = tile_vals[0, 0]
    edge = tiles.shape[-1]
    local_cols = n_row * 2
    slots, count = tile_slot[0, 0], tile_count[0]

    def col_send(value, pairs):
        return lax.ppermute(
            value, "col", [(2 * a + k, 2 * b + k) for a, b in pairs for k in range(2)]
        )

    def line_flip(value, j):
        return col_send(value, [(a, a ^ j) for a in range(line)])

    def core_flip(value):
        return lax.ppermute(value, "col", [(a, a ^ 1) for a in range(n_col)])

    def row_flip(value, j):
        return lax.ppermute(value, "row", [(a, a ^ j) for a in range(n_row)])

    def scatter_line(own):
        if line != 4:
            return [own[0]] + [line_flip(own[j], j) for j in range(1, line)], own[0]
        inward = col_send(own[3], [(0, 1), (3, 2)])
        middle = col_send(own[3], [(1, 2), (2, 1)])
        near = line_flip(own[1], 1)
        joined = sum_parts([own[2], inward])
        return [own[0], near, middle, line_flip(joined, 2)], joined

    values = features[:, 0].reshape(local_cols, edge, width)
    scale = (1.0 / jnp.sqrt(degree.astype(F32))).reshape(local_cols, edge, 1)
    halves = piece // edge

    ranged = lax.all_gather(scaled_transposed(cotangent, scale), "col", axis=0, tiled=True)

    aggs, outs = [], []
    partials, after = [], ()
    for half in range(halves):
        give, keep = forward(
            count, slots, tiles, (values, scale), True, half, local_cols, n_col, after
        )
        own = pair_sum(keep, core_flip(give))
        after = (own[-1],)
        partials.append(own)
    hidden = backward(count, slots, tiles, ranged, n_row)
    for half in range(halves):
        after = (agg,) if half else ()
        agg = aggregate(scatter_line(partials[half])[0], scale, half, after)
        spread = [agg] + [row_flip(agg, j) for j in range(1, n_row)]
        stacked, out = first_layer(spread, scale, w_first, half, (hidden,) if half else ())
        aggs.append(stacked)
        outs.append(out)

    partials, after = [], ()
    for half in range(halves):
        give, keep = forward(count, slots, tiles, outs, False, half, local_cols, n_col, after)
        own = pair_sum(keep, core_flip(give))
        after = (own[-1],)
        partials.append(own)

    give, keep = weight_grads(hidden, aggs, outs, scale, w_first, w_second, after)
    arrived, marks = zip(*[scatter_line(own) for own in partials])
    parts = split_sum(keep, core_flip(give), n_row, marks[:1])
    part = sum_parts([parts[0]] + [row_flip(parts[j], j) for j in range(1, n_row)], marks[1:])
    part = sum_parts([part] + [line_flip(part, j) for j in range(1, line)])
    mine = join([part] + [row_flip(part, j) for j in range(1, n_row)])
    other = core_flip(mine)
    core = lax.rem(lax.axis_index("col"), 2)
    grad_first = jnp.where(core == 0, mine, other).astype(F32)
    grad_second = jnp.where(core == 0, other, mine).astype(F32)

    logits = [second_layer(arrived[half], scale, w_second, half) for half in range(halves)]
    return jnp.concatenate(logits, 0), grad_first, grad_second


def solution(mesh):
    return jax.shard_map(
        per_device,
        mesh=mesh,
        in_specs=(
            P(None, "col", None, None),
            P(None, "col", None),
            P("row", "col", None, None, None),
            P("row", "col", None),
            P("row", "col"),
            P(),
            P(),
            P(("row", "col"), None),
        ),
        out_specs=(P(("row", "col"), None), P(), P()),
        check_vma=False,
    )
```

```python
import functools

import jax
import jax.numpy as jnp
from jax import lax
from jax.experimental import pallas as pl
from jax.experimental.pallas import tpu as pltpu
from jax.sharding import PartitionSpec as P

F32 = jnp.float32
BF16 = jnp.bfloat16
MIB = 1024 * 1024
VMEM = pl.BlockSpec(memory_space=pltpu.VMEM)
SMEM = pl.BlockSpec(memory_space=pltpu.SMEM)
ANY = pl.BlockSpec(memory_space=pl.ANY)


def nbytes(items):
    return sum(x.size * x.dtype.itemsize for x in items)


def run(body, args, specs, outs, scratch=(), flops=0, trans=0, mib=8, after=(), out_specs=None):
    n, extra = len(args), len(after)

    def whole(*refs):
        body(*refs[:n], *refs[n + extra :])

    return pl.pallas_call(
        whole,
        out_shape=outs,
        in_specs=specs + [ANY] * extra,
        out_specs=out_specs or [VMEM] * len(outs),
        scratch_shapes=list(scratch),
        compiler_params=pltpu.CompilerParams(vmem_limit_bytes=mib * MIB),
        cost_estimate=pl.CostEstimate(
            flops=flops, bytes_accessed=nbytes(args) + nbytes(outs), transcendentals=trans
        ),
    )(*args, *after)


def shape(dims, dtype=BF16):
    return jax.ShapeDtypeStruct(dims, dtype)


def list_tiles(count, slot_ref, number_ref, list_ref, local_cols, by_row):
    groups, cap = number_ref.shape[0], list_ref.shape[0] // number_ref.shape[0]
    blank = slot_ref.shape[0] * 1024
    bits = local_cols.bit_length() - 1

    def clear(g, _):
        number_ref[g] = 0
        for j in range(cap):
            list_ref[g * cap + j] = blank
        return 0

    lax.fori_loop(0, groups, clear, 0)

    def place(s, _):
        p = slot_ref[s]
        u, v = lax.shift_right_logical(p, bits), p & (local_cols - 1)
        g, other = (u, v) if by_row else (v, u)
        n = number_ref[g]
        list_ref[g * cap + n] = s * 1024 + other
        number_ref[g] = n + 1
        return 0

    lax.fori_loop(0, count, place, 0)


def repeat_lanes(scale, width):
    return jnp.concatenate([scale] * (width // scale.shape[-1]), 1)


def scale_body(degree, cot, scale, out):
    edge, lanes = scale.shape[1:]
    width = cot.shape[1]
    for i in range(scale.shape[0]):
        part = degree[i // 2 : i // 2 + 1, i % 2 * edge : (i % 2 + 1) * edge]
        line = 1.0 / jnp.sqrt(part.astype(F32))
        scale[i] = jnp.broadcast_to(line, (lanes, edge)).T
    row = lax.axis_index("row")
    for e in range(2):
        value = cot[e * edge : (e + 1) * edge, :].astype(F32)
        out[e] = (value * repeat_lanes(scale[row * 2 + e], width)).T.astype(BF16)


def scale_kernel(degree, cotangent, edge):
    return run(
        scale_body,
        (degree, cotangent),
        [VMEM] * 2,
        [shape((2 * degree.shape[0], edge, 128), F32), shape((2, cotangent.shape[1], edge))],
        flops=cotangent.size,
    )


def prepare_body(local_cols, count_ref, slot_ref, values, scale, out, *lists):
    list_tiles(count_ref[0], slot_ref, lists[0], lists[1], local_cols, True)
    list_tiles(count_ref[0], slot_ref, lists[2], lists[3], local_cols, False)

    def fill(i, _):
        wide = repeat_lanes(scale[i], values.shape[-1])
        out[i] = (values[i].astype(F32) * wide).astype(BF16)
        return 0

    lax.fori_loop(0, local_cols, fill, 0)


def prepare(count, slots, values, scale, block_rows):
    local_cols = values.shape[0]
    sizes = (block_rows, block_rows * local_cols, local_cols, block_rows * local_cols)
    return run(
        functools.partial(prepare_body, local_cols),
        (count, slots, values, scale),
        [SMEM] * 2 + [VMEM] * 2,
        [shape(values.shape)] + [shape((n,), jnp.int32) for n in sizes],
        flops=values.size,
        out_specs=[VMEM] + [SMEM] * 4,
        mib=12,
    )


def tile_copy(tiles_ref, held, sems, s):
    return pltpu.make_async_copy(tiles_ref.at[s], held.at[s], sems.at[s])


def each_tile(g, number_ref, list_ref, action):
    cap = list_ref.shape[0] // number_ref.shape[0]

    def one(j, _):
        action(lax.shift_right_logical(list_ref[g * cap + j], 10))
        return 0

    lax.fori_loop(0, number_ref[g], one, 0)


def sum_group(g, number_ref, list_ref, total, product, store):
    cap = list_ref.shape[0] // number_ref.shape[0]
    n = number_ref[g]

    def take(start, width):
        entries = [list_ref[g * cap + start + j] for j in range(width)]
        return product([(lax.shift_right_logical(x, 10), x & 1023) for x in entries])

    @pl.when(n == 0)
    def _():
        store(jnp.zeros_like(total))

    @pl.when(jnp.logical_and(n >= 1, n <= 2))
    def _():
        store(take(0, 2))

    @pl.when(jnp.logical_and(n >= 3, n <= 4))
    def _():
        store(take(0, 4))

    @pl.when(n > 4)
    def _():
        total[...] = jnp.zeros_like(total)

        def more(m, _):
            total[...] += take(4 * m, 4)
            return 0

        lax.fori_loop(0, lax.shift_right_logical(n + 3, 2), more, 0)
        store(total[...])


def joined_dot(lhs, rhs):
    return jnp.dot(
        jnp.concatenate(lhs, 1), jnp.concatenate(rhs, 0), preferred_element_type=F32
    )


def forward_body(first, half, n_in, *refs):
    number_ref, list_ref, tiles_ref = refs[:3]
    inputs = refs[3 : 3 + n_in]
    give, keep, held, source, total, sems, source_sems = refs[3 + n_in :]
    col, row = lax.axis_index("col"), lax.axis_index("row")
    parts = give.shape[0]
    per = source.shape[0] // n_in
    copies = [
        pltpu.make_async_copy(x, source.at[pl.ds(i * per, per)], source_sems.at[i])
        for i, x in enumerate(inputs)
    ]
    for copy in copies:
        copy.start()

    def block_row(i):
        flip = jnp.where(i < parts, 1, 0)
        return (col ^ (2 * lax.rem(i, parts) + flip)) * 2 + half

    def start(i, _):
        each_tile(
            block_row(i),
            number_ref,
            list_ref,
            lambda s: tile_copy(tiles_ref, held, sems, s).start(),
        )
        return 0

    lax.fori_loop(0, 2 * parts, start, 0)
    held[held.shape[0] - 1] = jnp.zeros(held.shape[1:], BF16)
    for copy in copies:
        copy.wait()

    def product(pieces):
        def locate(v):
            return v if first else (v & 1) * per + (lax.shift_right_logical(v, 1) ^ row)

        return joined_dot([held[s] for s, _ in pieces], [source[locate(v)] for _, v in pieces])

    for base, out in ((0, give), (parts, keep)):

        def block(i, _):
            def store(value):
                out[i] = value.astype(BF16)

            g = block_row(base + i)
            each_tile(
                g, number_ref, list_ref, lambda s: tile_copy(tiles_ref, held, sems, s).wait()
            )
            sum_group(g, number_ref, list_ref, total, product, store)
            return 0

        lax.fori_loop(0, parts, block, 0)


def forward(number, entries, tiles, sources, first, half, after):
    slots_n, edge, _ = tiles.shape
    width = sources[0].shape[-1]
    blocks = sum(x.shape[0] for x in sources)
    return run(
        functools.partial(forward_body, first, half, len(sources)),
        (number, entries, tiles, *sources),
        [SMEM, SMEM, ANY] + [ANY] * len(sources),
        [shape((number.shape[0] // 4, edge, width))] * 2,
        [
            pltpu.VMEM((slots_n + 1, edge, edge), BF16),
            pltpu.VMEM((blocks, edge, width), BF16),
            pltpu.VMEM((edge, width), F32),
            pltpu.SemaphoreType.DMA((slots_n,)),
            pltpu.SemaphoreType.DMA((len(sources),)),
        ],
        flops=slots_n * edge * edge * width,
        mib=20,
        after=after,
    )


def backward_body(number_ref, list_ref, tiles_ref, ranged, out, *refs):
    held, source, total, sems, source_sem = refs
    mask = lax.axis_index("row") * 2
    copy = pltpu.make_async_copy(ranged, source, source_sem)
    copy.start()

    def start(i, _):
        each_tile(
            i ^ mask,
            number_ref,
            list_ref,
            lambda s: tile_copy(tiles_ref, held, sems, s).start(),
        )
        return 0

    lax.fori_loop(0, out.shape[0], start, 0)
    held[held.shape[0] - 1] = jnp.zeros(held.shape[1:], BF16)
    copy.wait()

    def product(pieces):
        return joined_dot([source[u] for _, u in pieces], [held[s] for s, _ in pieces])

    def block(i, _):
        def store(value):
            out[i] = value.astype(BF16)

        each_tile(
            i ^ mask, number_ref, list_ref, lambda s: tile_copy(tiles_ref, held, sems, s).wait()
        )
        sum_group(i ^ mask, number_ref, list_ref, total, product, store)
        return 0

    lax.fori_loop(0, out.shape[0], block, 0)


def backward(number, entries, tiles, ranged):
    slots_n, edge, _ = tiles.shape
    width = ranged.shape[1]
    return run(
        backward_body,
        (number, entries, tiles, ranged),
        [SMEM, SMEM, ANY, ANY],
        [shape((number.shape[0], width, edge))],
        [
            pltpu.VMEM((slots_n + 1, edge, edge), BF16),
            pltpu.VMEM(ranged.shape, BF16),
            pltpu.VMEM((width, edge), F32),
            pltpu.SemaphoreType.DMA((slots_n,)),
            pltpu.SemaphoreType.DMA,
        ],
        flops=2 * slots_n * edge * edge * width,
        mib=20,
    )[0]


def pair_sum_body(n, keep, come, *outs):
    for j in range(n):
        outs[j][...] = (keep[j].astype(F32) + come[j].astype(F32)).astype(BF16)


def pair_sum(keep, come):
    n = keep.shape[0]
    return run(
        functools.partial(pair_sum_body, n),
        (keep, come),
        [VMEM] * 2,
        [shape(keep.shape[1:])] * n,
        flops=keep.size,
    )


def tree(items):
    while len(items) > 1:
        items = [a + b for a, b in zip(items[::2], items[1::2])]
    return items[0]


def agg_body(n, half, *refs):
    scale, out = refs[n], refs[n + 1]
    summed = tree([x[...].astype(F32) for x in refs[:n]])
    out[...] = (summed * repeat_lanes(scale[lax.axis_index("row") * 2 + half], summed.shape[1])).astype(
        BF16
    )


def aggregate(parts, scale, half, after):
    return run(
        functools.partial(agg_body, len(parts), half),
        (*parts, scale),
        [VMEM] * (len(parts) + 1),
        [shape(parts[0].shape)],
        flops=parts[0].size * len(parts),
        after=after,
    )[0]


def first_body(n, half, *refs):
    scale, weight, agg, out = refs[n:]
    row = lax.axis_index("row")
    for j in range(n):
        value = jnp.dot(refs[j][...], weight[...], preferred_element_type=F32)
        wide = repeat_lanes(scale[(row ^ j) * 2 + half], value.shape[1])
        out[j] = (jax.nn.gelu(value) * wide).astype(BF16)
        agg[j] = refs[j][...]


def first_layer(aggs, scale, weight, half, after):
    n = len(aggs)
    dims = (n, *aggs[0].shape)
    return run(
        functools.partial(first_body, n, half),
        (*aggs, scale, weight),
        [VMEM] * (n + 2),
        [shape(dims)] * 2,
        flops=2 * n * dims[1] * weight.size,
        trans=n * aggs[0].size,
        mib=12,
        after=after,
    )


def second_body(n, half, *refs):
    scale, weight, out = refs[n:]
    summed = tree([x[...].astype(F32) for x in refs[:n]])
    agg = (summed * repeat_lanes(scale[lax.axis_index("row") * 2 + half], summed.shape[1])).astype(
        BF16
    )
    out[...] = jnp.dot(agg, weight[...], preferred_element_type=F32).astype(BF16)


def second_layer(parts, scale, weight, half):
    dims = parts[0].shape
    return run(
        functools.partial(second_body, len(parts), half),
        (*parts, scale, weight),
        [VMEM] * (len(parts) + 2),
        [shape(dims)],
        flops=2 * dims[0] * weight.size,
    )[0]


def grad_body(hidden_ref, *refs):
    aggs, outs = refs[:2], refs[2:4]
    scale, w_first, w_second, give, keep, first, second = refs[4:]
    row = lax.axis_index("row")
    core = lax.rem(lax.axis_index("col"), 2)
    first[...] = jnp.zeros_like(first)
    second[...] = jnp.zeros_like(second)
    for e in range(2):

        def block(j, _):
            hidden, agg = hidden_ref[2 * j + e], aggs[e][j]
            pre = jnp.dot(agg, w_first[...], preferred_element_type=F32)
            grad_hidden = lax.dot_general(
                hidden, w_second[...], (((0,), (1,)), ((), ())), preferred_element_type=F32
            )
            _, pullback = jax.vjp(jax.nn.gelu, pre)
            wide = repeat_lanes(scale[(row ^ j) * 2 + e], pre.shape[1])
            grad_pre = pullback(grad_hidden * wide)[0].astype(BF16)
            first[...] += lax.dot_general(
                agg, grad_pre, (((0,), (0,)), ((), ())), preferred_element_type=F32
            )
            second[...] += lax.dot_general(
                outs[e][j], hidden, (((0,), (1,)), ((), ())), preferred_element_type=F32
            )
            return 0

        lax.fori_loop(0, aggs[e].shape[0], block, 0)
    keep[...] = jnp.where(core == 0, first[...], second[...]).astype(BF16)
    give[...] = jnp.where(core == 0, second[...], first[...]).astype(BF16)


def weight_grads(hidden, aggs, outs, scale, w_first, w_second, after):
    return run(
        grad_body,
        (hidden, *aggs, *outs, scale, w_first, w_second),
        [VMEM] * 8,
        [shape(w_first.shape)] * 2,
        [pltpu.VMEM(w_first.shape, F32)] * 2,
        flops=8 * hidden.size * w_first.shape[0],
        trans=hidden.size,
        mib=28,
        after=after,
    )


def split_body(n, keep, come, *outs):
    row = lax.axis_index("row")
    rows = keep.shape[0] // n
    for j in range(n):
        part = pl.ds(pl.multiple_of((row ^ j) * rows, rows), rows)
        outs[j][...] = (keep[part, :].astype(F32) + come[part, :].astype(F32)).astype(BF16)


def split_sum(keep, come, n, after):
    rows, width = keep.shape
    return run(
        functools.partial(split_body, n),
        (keep, come),
        [VMEM] * 2,
        [shape((rows // n, width))] * n,
        flops=keep.size,
        after=after,
    )


def sum_body(n, *refs):
    refs[n][...] = tree([x[...].astype(F32) for x in refs[:n]]).astype(BF16)


def sum_parts(parts, after=()):
    return run(
        functools.partial(sum_body, len(parts)),
        tuple(parts),
        [VMEM] * len(parts),
        [shape(parts[0].shape)],
        flops=parts[0].size * len(parts),
        after=after,
    )[0]


def join_body(n, *refs):
    row = lax.axis_index("row")
    rows = refs[0].shape[0]
    for j in range(n):
        refs[n][pl.ds(pl.multiple_of((row ^ j) * rows, rows), rows), :] = refs[j][...]


def join(parts):
    rows, width = parts[0].shape
    return run(
        functools.partial(join_body, len(parts)),
        tuple(parts),
        [VMEM] * len(parts),
        [shape((rows * len(parts), width))],
    )[0]


def select_body(mine, other, first, second):
    core = lax.rem(lax.axis_index("col"), 2)
    first[...] = jnp.where(core == 0, mine[...].astype(F32), other[...].astype(F32))
    second[...] = jnp.where(core == 0, other[...].astype(F32), mine[...].astype(F32))


def select(mine, other):
    return run(select_body, (mine, other), [VMEM] * 2, [shape(mine.shape, F32)] * 2)


def per_device(features, degree, tile_vals, tile_slot, tile_count, w_first, w_second, cotangent):
    n_row, n_col = lax.axis_size("row"), lax.axis_size("col")
    line = n_col // 2
    piece, width = cotangent.shape
    tiles = tile_vals[0, 0]
    edge = tiles.shape[-1]
    local_cols = n_row * 2
    slots, count = tile_slot[0, 0], tile_count[0]

    def col_send(value, pairs):
        return lax.ppermute(
            value, "col", [(2 * a + k, 2 * b + k) for a, b in pairs for k in range(2)]
        )

    def line_flip(value, j):
        return col_send(value, [(a, a ^ j) for a in range(line)])

    def core_flip(value):
        return lax.ppermute(value, "col", [(a, a ^ 1) for a in range(n_col)])

    def row_flip(value, j):
        return lax.ppermute(value, "row", [(a, a ^ j) for a in range(n_row)])

    def scatter_line(own):
        if line != 4:
            return [own[0]] + [line_flip(own[j], j) for j in range(1, line)], own[0]
        inward = col_send(own[3], [(0, 1), (3, 2)])
        middle = col_send(own[3], [(1, 2), (2, 1)])
        near = line_flip(own[1], 1)
        joined = sum_parts([own[2], inward])
        return [own[0], near, middle, line_flip(joined, 2)], joined

    halves = piece // edge
    scale, scaled = scale_kernel(degree[:, 0], cotangent, edge)
    ranged = lax.all_gather(scaled, "col", axis=0, tiled=True)
    values = features[:, 0].reshape(local_cols, edge, width)
    first_in, number, entries, t_number, t_entries = prepare(
        count, slots, values, scale, 2 * n_col
    )

    aggs, outs = [], []
    partials, after = [], ()
    for half in range(halves):
        give, keep = forward(number, entries, tiles, (first_in,), True, half, after)
        own = pair_sum(keep, core_flip(give))
        after = (own[-1],)
        partials.append(own)
    hidden = backward(t_number, t_entries, tiles, ranged)
    for half in range(halves):
        after = (agg,) if half else ()
        agg = aggregate(scatter_line(partials[half])[0], scale, half, after)
        spread = [agg] + [row_flip(agg, j) for j in range(1, n_row)]
        stacked, out = first_layer(spread, scale, w_first, half, (hidden,) if half else ())
        aggs.append(stacked)
        outs.append(out)

    partials, after = [], ()
    for half in range(halves):
        give, keep = forward(number, entries, tiles, outs, False, half, after)
        own = pair_sum(keep, core_flip(give))
        after = (own[-1],)
        partials.append(own)

    give, keep = weight_grads(hidden, aggs, outs, scale, w_first, w_second, after)
    arrived, marks = zip(*[scatter_line(own) for own in partials])
    parts = split_sum(keep, core_flip(give), n_row, marks[:1])
    part = sum_parts([parts[0]] + [row_flip(parts[j], j) for j in range(1, n_row)], marks[1:])
    part = sum_parts([part] + [line_flip(part, j) for j in range(1, line)], arrived[0][1:])
    mine = join([part] + [row_flip(part, j) for j in range(1, n_row)])
    grad_first, grad_second = select(mine, core_flip(mine))

    logits = [second_layer(arrived[half], scale, w_second, half) for half in range(halves)]
    return jnp.concatenate(logits, 0), grad_first, grad_second


def solution(mesh):
    return jax.shard_map(
        per_device,
        mesh=mesh,
        in_specs=(
            P(None, "col", None, None),
            P(None, "col", None),
            P("row", "col", None, None, None),
            P("row", "col", None),
            P("row", "col"),
            P(),
            P(),
            P(("row", "col"), None),
        ),
        out_specs=(P(("row", "col"), None), P(), P()),
        check_vma=False,
    )
```

```python
import functools

import jax
import jax.numpy as jnp
from jax import lax
from jax.experimental import pallas as pl
from jax.experimental.pallas import tpu as pltpu
from jax.sharding import PartitionSpec as P

F32 = jnp.float32
BF16 = jnp.bfloat16
MIB = 1024 * 1024
VMEM = pl.BlockSpec(memory_space=pltpu.VMEM)
SMEM = pl.BlockSpec(memory_space=pltpu.SMEM)
ANY = pl.BlockSpec(memory_space=pl.ANY)


def nbytes(items):
    return sum(x.size * x.dtype.itemsize for x in items)


def run(body, args, specs, outs, scratch=(), flops=0, trans=0, mib=8, after=(), out_specs=None):
    n, extra = len(args), len(after)

    def whole(*refs):
        body(*refs[:n], *refs[n + extra :])

    return pl.pallas_call(
        whole,
        out_shape=outs,
        in_specs=specs + [ANY] * extra,
        out_specs=out_specs or [VMEM] * len(outs),
        scratch_shapes=list(scratch),
        compiler_params=pltpu.CompilerParams(vmem_limit_bytes=mib * MIB),
        cost_estimate=pl.CostEstimate(
            flops=flops, bytes_accessed=nbytes(args) + nbytes(outs), transcendentals=trans
        ),
    )(*args, *after)


def shape(dims, dtype=BF16):
    return jax.ShapeDtypeStruct(dims, dtype)


def list_tiles(count, slot_ref, number_ref, list_ref, local_cols, by_row):
    groups, cap = number_ref.shape[0], list_ref.shape[0] // number_ref.shape[0]
    blank = slot_ref.shape[0] * 1024
    bits = local_cols.bit_length() - 1

    def clear(g, _):
        number_ref[g] = 0
        for j in range(cap):
            list_ref[g * cap + j] = blank
        return 0

    lax.fori_loop(0, groups, clear, 0)

    def place(s, _):
        p = slot_ref[s]
        u, v = lax.shift_right_logical(p, bits), p & (local_cols - 1)
        g, other = (u, v) if by_row else (v, u)
        n = number_ref[g]
        list_ref[g * cap + n] = s * 1024 + other
        number_ref[g] = n + 1
        return 0

    lax.fori_loop(0, count, place, 0)


def repeat_lanes(scale, width):
    return jnp.concatenate([scale] * (width // scale.shape[-1]), 1)


def scale_body(degree, cot, scale, out):
    edge, lanes = scale.shape[1:]
    width = cot.shape[1]
    for i in range(scale.shape[0]):
        part = degree[i // 2 : i // 2 + 1, i % 2 * edge : (i % 2 + 1) * edge]
        line = 1.0 / jnp.sqrt(part.astype(F32))
        scale[i] = jnp.broadcast_to(line, (lanes, edge)).T
    row = lax.axis_index("row")
    for e in range(2):
        value = cot[e * edge : (e + 1) * edge, :].astype(F32)
        out[e] = (value * repeat_lanes(scale[row * 2 + e], width)).T.astype(BF16)


def scale_kernel(degree, cotangent, edge):
    return run(
        scale_body,
        (degree, cotangent),
        [VMEM] * 2,
        [shape((2 * degree.shape[0], edge, 128), F32), shape((2, cotangent.shape[1], edge))],
        flops=cotangent.size,
    )


def prepare_body(local_cols, count_ref, slot_ref, values, scale, out, *lists):
    list_tiles(count_ref[0], slot_ref, lists[0], lists[1], local_cols, True)
    list_tiles(count_ref[0], slot_ref, lists[2], lists[3], local_cols, False)

    def fill(i, _):
        wide = repeat_lanes(scale[i], values.shape[-1])
        out[i] = (values[i].astype(F32) * wide).astype(BF16)
        return 0

    lax.fori_loop(0, local_cols, fill, 0)


def prepare(count, slots, values, scale, block_rows):
    local_cols = values.shape[0]
    sizes = (block_rows, block_rows * local_cols, local_cols, block_rows * local_cols)
    return run(
        functools.partial(prepare_body, local_cols),
        (count, slots, values, scale),
        [SMEM] * 2 + [VMEM] * 2,
        [shape(values.shape)] + [shape((n,), jnp.int32) for n in sizes],
        flops=values.size,
        out_specs=[VMEM] + [SMEM] * 4,
        mib=12,
    )


def sum_group(g, number_ref, list_ref, total, product, store):
    cap = list_ref.shape[0] // number_ref.shape[0]
    n = number_ref[g]

    def take(start, width):
        entries = [list_ref[g * cap + start + j] for j in range(width)]
        return product([(lax.shift_right_logical(x, 10), x & 1023) for x in entries])

    def exact(width):
        @pl.when(n == width)
        def _():
            store(take(0, width))

    @pl.when(n == 0)
    def _():
        store(jnp.zeros_like(total))

    for width in range(1, 5):
        exact(width)

    @pl.when(n > 4)
    def _():
        total[...] = jnp.zeros_like(total)
        fours = lax.shift_right_logical(n, 2)

        def four(m, _):
            total[...] += take(4 * m, 4)
            return 0

        def one(m, _):
            total[...] += take(m, 1)
            return 0

        lax.fori_loop(0, fours, four, 0)
        lax.fori_loop(4 * fours, n, one, 0)
        store(total[...])


def joined_dot(lhs, rhs):
    return jnp.dot(
        jnp.concatenate(lhs, 1), jnp.concatenate(rhs, 0), preferred_element_type=F32
    )


def forward_body(first, half, number_ref, list_ref, tiles, source, give, keep, total):
    col, row = lax.axis_index("col"), lax.axis_index("row")
    per = source.shape[0] // 2

    def product(pieces):
        def locate(v):
            return v if first else (v & 1) * per + (lax.shift_right_logical(v, 1) ^ row)

        return joined_dot([tiles[s] for s, _ in pieces], [source[locate(v)] for _, v in pieces])

    for flip, out in ((1, give), (0, keep)):

        def block(i, _):
            def store(value):
                out[i] = value.astype(BF16)

            g = (col ^ (2 * i + flip)) * 2 + half
            sum_group(g, number_ref, list_ref, total, product, store)
            return 0

        lax.fori_loop(0, out.shape[0], block, 0)


def forward(number, entries, tiles, source, first, half, after):
    slots_n, edge, _ = tiles.shape
    width = source.shape[-1]
    return run(
        functools.partial(forward_body, first, half),
        (number, entries, tiles, source),
        [SMEM, SMEM, VMEM, VMEM],
        [shape((number.shape[0] // 4, edge, width))] * 2,
        [pltpu.VMEM((edge, width), F32)],
        flops=slots_n * edge * edge * width,
        mib=16,
        after=after,
    )


def backward_body(number_ref, list_ref, tiles, ranged, out, total):
    mask = lax.axis_index("row") * 2

    def product(pieces):
        return joined_dot([ranged[u] for _, u in pieces], [tiles[s] for s, _ in pieces])

    def block(i, _):
        def store(value):
            out[i] = value.astype(BF16)

        sum_group(i ^ mask, number_ref, list_ref, total, product, store)
        return 0

    lax.fori_loop(0, out.shape[0], block, 0)


def backward(number, entries, tiles, ranged):
    slots_n, edge, _ = tiles.shape
    width = ranged.shape[1]
    return run(
        backward_body,
        (number, entries, tiles, ranged),
        [SMEM, SMEM, VMEM, VMEM],
        [shape((number.shape[0], width, edge))],
        [pltpu.VMEM((width, edge), F32)],
        flops=2 * slots_n * edge * edge * width,
        mib=18,
    )[0]


def pair_sum_body(n, keep, come, *outs):
    for j in range(n):
        outs[j][...] = (keep[j].astype(F32) + come[j].astype(F32)).astype(BF16)


def pair_sum(keep, come):
    n = keep.shape[0]
    return run(
        functools.partial(pair_sum_body, n),
        (keep, come),
        [VMEM] * 2,
        [shape(keep.shape[1:])] * n,
        flops=keep.size,
    )


def tree(items):
    while len(items) > 1:
        items = [a + b for a, b in zip(items[::2], items[1::2])]
    return items[0]


def agg_body(n, half, *refs):
    scale, out = refs[n], refs[n + 1]
    summed = tree([x[...].astype(F32) for x in refs[:n]])
    out[...] = (summed * repeat_lanes(scale[lax.axis_index("row") * 2 + half], summed.shape[1])).astype(
        BF16
    )


def aggregate(parts, scale, half, after):
    return run(
        functools.partial(agg_body, len(parts), half),
        (*parts, scale),
        [VMEM] * (len(parts) + 1),
        [shape(parts[0].shape)],
        flops=parts[0].size * len(parts),
        after=after,
    )[0]


def first_body(n, half, *refs):
    scale, weight, agg, out = refs[n], refs[n + 1], refs[-2], refs[-1]
    row = lax.axis_index("row")
    if half:
        agg[: half * n] = refs[n + 2][...]
        out[: half * n] = refs[n + 3][...]
    for j in range(n):
        value = jnp.dot(refs[j][...], weight[...], preferred_element_type=F32)
        wide = repeat_lanes(scale[(row ^ j) * 2 + half], value.shape[1])
        out[half * n + j] = (jax.nn.gelu(value) * wide).astype(BF16)
        agg[half * n + j] = refs[j][...]


def first_layer(aggs, scale, weight, half, before, after):
    n = len(aggs)
    dims = ((half + 1) * n, *aggs[0].shape)
    return run(
        functools.partial(first_body, n, half),
        (*aggs, scale, weight, *before),
        [VMEM] * (n + 2 + len(before)),
        [shape(dims)] * 2,
        flops=2 * n * dims[1] * weight.size,
        trans=n * aggs[0].size,
        mib=14,
        after=after,
    )


def second_body(n, half, *refs):
    scale, weight, out = refs[n:]
    summed = tree([x[...].astype(F32) for x in refs[:n]])
    agg = (summed * repeat_lanes(scale[lax.axis_index("row") * 2 + half], summed.shape[1])).astype(
        BF16
    )
    out[...] = jnp.dot(agg, weight[...], preferred_element_type=F32).astype(BF16)


def second_layer(parts, scale, weight, half):
    dims = parts[0].shape
    return run(
        functools.partial(second_body, len(parts), half),
        (*parts, scale, weight),
        [VMEM] * (len(parts) + 2),
        [shape(dims)],
        flops=2 * dims[0] * weight.size,
    )[0]


def grad_body(hidden_ref, aggs, outs, scale, w_first, w_second, give, keep, first, second):
    row = lax.axis_index("row")
    core = lax.rem(lax.axis_index("col"), 2)
    n = aggs.shape[0] // 2
    first[...] = jnp.zeros_like(first)
    second[...] = jnp.zeros_like(second)
    for e in range(2):

        def block(j, _):
            hidden, agg = hidden_ref[2 * j + e], aggs[e * n + j]
            pre = jnp.dot(agg, w_first[...], preferred_element_type=F32)
            grad_hidden = lax.dot_general(
                hidden, w_second[...], (((0,), (1,)), ((), ())), preferred_element_type=F32
            )
            _, pullback = jax.vjp(jax.nn.gelu, pre)
            wide = repeat_lanes(scale[(row ^ j) * 2 + e], pre.shape[1])
            grad_pre = pullback(grad_hidden * wide)[0].astype(BF16)
            first[...] += lax.dot_general(
                agg, grad_pre, (((0,), (0,)), ((), ())), preferred_element_type=F32
            )
            second[...] += lax.dot_general(
                outs[e * n + j], hidden, (((0,), (1,)), ((), ())), preferred_element_type=F32
            )
            return 0

        lax.fori_loop(0, n, block, 0)
    keep[...] = jnp.where(core == 0, first[...], second[...]).astype(BF16)
    give[...] = jnp.where(core == 0, second[...], first[...]).astype(BF16)


def weight_grads(hidden, aggs, outs, scale, w_first, w_second, after):
    return run(
        grad_body,
        (hidden, aggs, outs, scale, w_first, w_second),
        [VMEM] * 6,
        [shape(w_first.shape)] * 2,
        [pltpu.VMEM(w_first.shape, F32)] * 2,
        flops=8 * hidden.size * w_first.shape[0],
        trans=hidden.size,
        mib=24,
        after=after,
    )


def split_body(n, keep, come, *outs):
    row = lax.axis_index("row")
    rows = keep.shape[0] // n
    for j in range(n):
        part = pl.ds(pl.multiple_of((row ^ j) * rows, rows), rows)
        outs[j][...] = (keep[part, :].astype(F32) + come[part, :].astype(F32)).astype(BF16)


def split_sum(keep, come, n, after):
    rows, width = keep.shape
    return run(
        functools.partial(split_body, n),
        (keep, come),
        [VMEM] * 2,
        [shape((rows // n, width))] * n,
        flops=keep.size,
        after=after,
    )


def sum_body(n, *refs):
    refs[n][...] = tree([x[...].astype(F32) for x in refs[:n]]).astype(BF16)


def sum_parts(parts, after=()):
    return run(
        functools.partial(sum_body, len(parts)),
        tuple(parts),
        [VMEM] * len(parts),
        [shape(parts[0].shape)],
        flops=parts[0].size * len(parts),
        after=after,
    )[0]


def join_body(n, *refs):
    row = lax.axis_index("row")
    rows = refs[0].shape[0]
    for j in range(n):
        refs[n][pl.ds(pl.multiple_of((row ^ j) * rows, rows), rows), :] = refs[j][...]


def join(parts):
    rows, width = parts[0].shape
    return run(
        functools.partial(join_body, len(parts)),
        tuple(parts),
        [VMEM] * len(parts),
        [shape((rows * len(parts), width))],
    )[0]


def select_body(mine, other, first, second):
    core = lax.rem(lax.axis_index("col"), 2)
    first[...] = jnp.where(core == 0, mine[...].astype(F32), other[...].astype(F32))
    second[...] = jnp.where(core == 0, other[...].astype(F32), mine[...].astype(F32))


def select(mine, other):
    return run(select_body, (mine, other), [VMEM] * 2, [shape(mine.shape, F32)] * 2)


def per_device(features, degree, tile_vals, tile_slot, tile_count, w_first, w_second, cotangent):
    n_row, n_col = lax.axis_size("row"), lax.axis_size("col")
    line = n_col // 2
    piece, width = cotangent.shape
    tiles = tile_vals[0, 0]
    edge = tiles.shape[-1]
    local_cols = n_row * 2
    slots, count = tile_slot[0, 0], tile_count[0]

    def col_send(value, pairs):
        return lax.ppermute(
            value, "col", [(2 * a + k, 2 * b + k) for a, b in pairs for k in range(2)]
        )

    def line_flip(value, j):
        return col_send(value, [(a, a ^ j) for a in range(line)])

    def core_flip(value):
        return lax.ppermute(value, "col", [(a, a ^ 1) for a in range(n_col)])

    def row_flip(value, j):
        return lax.ppermute(value, "row", [(a, a ^ j) for a in range(n_row)])

    def scatter_line(own):
        if line != 4:
            return [own[0]] + [line_flip(own[j], j) for j in range(1, line)], own[0]
        inward = col_send(own[3], [(0, 1), (3, 2)])
        middle = col_send(own[3], [(1, 2), (2, 1)])
        near = line_flip(own[1], 1)
        joined = sum_parts([own[2], inward])
        return [own[0], near, middle, line_flip(joined, 2)], joined

    halves = piece // edge
    scale, scaled = scale_kernel(degree[:, 0], cotangent, edge)
    ranged = lax.all_gather(scaled, "col", axis=0, tiled=True)
    values = features[:, 0].reshape(local_cols, edge, width)
    first_in, number, entries, t_number, t_entries = prepare(
        count, slots, values, scale, 2 * n_col
    )

    partials, after, stacked = [], (), ()
    for half in range(halves):
        give, keep = forward(number, entries, tiles, first_in, True, half, after)
        own = pair_sum(keep, core_flip(give))
        after = (own[-1],)
        partials.append(own)
    hidden = backward(t_number, t_entries, tiles, ranged)
    for half in range(halves):
        after = (agg,) if half else ()
        agg = aggregate(scatter_line(partials[half])[0], scale, half, after)
        spread = [agg] + [row_flip(agg, j) for j in range(1, n_row)]
        stacked = first_layer(
            spread, scale, w_first, half, stacked, (hidden,) if half else ()
        )
    aggs, outs = stacked

    partials, after = [], ()
    for half in range(halves):
        give, keep = forward(number, entries, tiles, outs, False, half, after)
        own = pair_sum(keep, core_flip(give))
        after = (own[-1],)
        partials.append(own)

    give, keep = weight_grads(hidden, aggs, outs, scale, w_first, w_second, after)
    arrived, marks = zip(*[scatter_line(own) for own in partials])
    parts = split_sum(keep, core_flip(give), n_row, marks[:1])
    part = sum_parts([parts[0]] + [row_flip(parts[j], j) for j in range(1, n_row)], marks[1:])
    part = sum_parts([part] + [line_flip(part, j) for j in range(1, line)], arrived[0][1:])
    mine = join([part] + [row_flip(part, j) for j in range(1, n_row)])
    grad_first, grad_second = select(mine, core_flip(mine))

    logits = [second_layer(arrived[half], scale, w_second, half) for half in range(halves)]
    return jnp.concatenate(logits, 0), grad_first, grad_second


def solution(mesh):
    return jax.shard_map(
        per_device,
        mesh=mesh,
        in_specs=(
            P(None, "col", None, None),
            P(None, "col", None),
            P("row", "col", None, None, None),
            P("row", "col", None),
            P("row", "col"),
            P(),
            P(),
            P(("row", "col"), None),
        ),
        out_specs=(P(("row", "col"), None), P(), P()),
        check_vma=False,
    )
```

```python
import functools

import jax
import jax.numpy as jnp
from jax import lax
from jax.experimental import pallas as pl
from jax.experimental.pallas import tpu as pltpu
from jax.sharding import PartitionSpec as P

F32 = jnp.float32
BF16 = jnp.bfloat16
MIB = 1024 * 1024
VMEM = pl.BlockSpec(memory_space=pltpu.VMEM)
SMEM = pl.BlockSpec(memory_space=pltpu.SMEM)
ANY = pl.BlockSpec(memory_space=pl.ANY)


def run(body, args, specs, outs, scratch=(), mib=8, after=(), out_specs=None):
    n, extra = len(args), len(after)

    def whole(*refs):
        body(*refs[:n], *refs[n + extra :])

    return pl.pallas_call(
        whole,
        out_shape=outs,
        in_specs=specs + [ANY] * extra,
        out_specs=out_specs or [VMEM] * len(outs),
        scratch_shapes=list(scratch),
        compiler_params=pltpu.CompilerParams(vmem_limit_bytes=mib * MIB),
        cost_estimate=pl.CostEstimate(
            flops=int(COST.get(getattr(body, "func", body), 0) * 1e9),
            bytes_accessed=0,
            transcendentals=0,
        ),
    )(*args, *after)


def shape(dims, dtype=BF16):
    return jax.ShapeDtypeStruct(dims, dtype)


def list_tiles(count, slot_ref, number_ref, list_ref, local_cols, by_row):
    groups, cap = number_ref.shape[0], list_ref.shape[0] // number_ref.shape[0]
    blank = slot_ref.shape[0] * 1024
    bits = local_cols.bit_length() - 1

    def clear(g, _):
        number_ref[g] = 0
        for j in range(cap):
            list_ref[g * cap + j] = blank
        return 0

    lax.fori_loop(0, groups, clear, 0)

    def place(s, _):
        p = slot_ref[s]
        u, v = lax.shift_right_logical(p, bits), p & (local_cols - 1)
        g, other = (u, v) if by_row else (v, u)
        n = number_ref[g]
        list_ref[g * cap + n] = s * 1024 + other
        number_ref[g] = n + 1
        return 0

    lax.fori_loop(0, count, place, 0)


def repeat_lanes(scale, width):
    return jnp.concatenate([scale] * (width // scale.shape[-1]), 1)


def scale_body(degree, cot, scale, out):
    edge, lanes = scale.shape[1:]
    width = cot.shape[1]
    for i in range(scale.shape[0]):
        part = degree[i // 2 : i // 2 + 1, i % 2 * edge : (i % 2 + 1) * edge]
        line = 1.0 / jnp.sqrt(part.astype(F32))
        scale[i] = jnp.broadcast_to(line, (lanes, edge)).T
    row = lax.axis_index("row")
    for e in range(2):
        value = cot[e * edge : (e + 1) * edge, :].astype(F32)
        out[e] = (value * repeat_lanes(scale[row * 2 + e], width)).T.astype(BF16)


def scale_kernel(degree, cotangent, edge):
    return run(
        scale_body,
        (degree, cotangent),
        [VMEM] * 2,
        [shape((2 * degree.shape[0], edge, 128), F32), shape((2, cotangent.shape[1], edge))],
    )


def prepare_body(local_cols, count_ref, slot_ref, values, scale, out, *lists):
    list_tiles(count_ref[0], slot_ref, lists[0], lists[1], local_cols, True)
    list_tiles(count_ref[0], slot_ref, lists[2], lists[3], local_cols, False)

    def fill(i, _):
        wide = repeat_lanes(scale[i], values.shape[-1])
        out[i] = (values[i].astype(F32) * wide).astype(BF16)
        return 0

    lax.fori_loop(0, local_cols, fill, 0)


def prepare(count, slots, values, scale, block_rows):
    local_cols = values.shape[0]
    sizes = (block_rows, block_rows * local_cols, local_cols, block_rows * local_cols)
    return run(
        functools.partial(prepare_body, local_cols),
        (count, slots, values, scale),
        [SMEM] * 2 + [VMEM] * 2,
        [shape(values.shape)] + [shape((n,), jnp.int32) for n in sizes],
        out_specs=[VMEM] + [SMEM] * 4,
        mib=12,
    )


def sum_group(g, number_ref, list_ref, total, product, store):
    cap = list_ref.shape[0] // number_ref.shape[0]
    n = number_ref[g]

    def take(start, width):
        entries = [list_ref[g * cap + start + j] for j in range(width)]
        return product([(lax.shift_right_logical(x, 10), x & 1023) for x in entries])

    def exact(width):
        @pl.when(n == width)
        def _():
            store(take(0, width))

    @pl.when(n == 0)
    def _():
        store(jnp.zeros_like(total))

    for width in range(1, 5):
        exact(width)

    @pl.when(n > 4)
    def _():
        total[...] = jnp.zeros_like(total)
        fours = lax.shift_right_logical(n, 2)

        def four(m, _):
            total[...] += take(4 * m, 4)
            return 0

        def one(m, _):
            total[...] += take(m, 1)
            return 0

        lax.fori_loop(0, fours, four, 0)
        lax.fori_loop(4 * fours, n, one, 0)
        store(total[...])


def joined_dot(lhs, rhs):
    return jnp.dot(
        jnp.concatenate(lhs, 1), jnp.concatenate(rhs, 0), preferred_element_type=F32
    )


def forward_body(first, flip, number_ref, list_ref, tiles, source, out, total):
    col, row = lax.axis_index("col"), lax.axis_index("row")
    line = out.shape[0] // 2

    def product(pieces):
        def locate(v):
            return v if first else v ^ (2 * row)

        return joined_dot([tiles[s] for s, _ in pieces], [source[locate(v)] for _, v in pieces])

    for half in range(2):

        def block(i, _):
            def store(value):
                out[half * line + i] = value.astype(BF16)

            g = (col ^ (2 * i + flip)) * 2 + half
            sum_group(g, number_ref, list_ref, total, product, store)
            return 0

        lax.fori_loop(0, line, block, 0)


def forward(number, entries, tiles, source, first, flip, after=()):
    slots_n, edge, _ = tiles.shape
    width = source.shape[-1]
    return run(
        functools.partial(forward_body, first, flip),
        (number, entries, tiles, source),
        [SMEM, SMEM, VMEM, VMEM],
        [shape((number.shape[0] // 2, edge, width))],
        [pltpu.VMEM((edge, width), F32)],
        mib=16,
        after=after,
    )[0]


def backward_body(n, number_ref, list_ref, tiles, *refs):
    pieces_in, (out, ranged, total) = refs[:n], refs[n:]
    mask, flips = lax.axis_index("row") * 2, lax.axis_index("col") * 2
    for i, piece in enumerate(pieces_in):
        ranged[2 * i : 2 * i + 2] = piece[...]

    def product(pieces):
        return joined_dot([ranged[u ^ flips] for _, u in pieces], [tiles[s] for s, _ in pieces])

    def block(i, _):
        def store(value):
            out[i] = value.astype(BF16)

        sum_group(i ^ mask, number_ref, list_ref, total, product, store)
        return 0

    lax.fori_loop(0, out.shape[0], block, 0)


def backward(number, entries, tiles, pieces, after=()):
    slots_n, edge, _ = tiles.shape
    _, width, _ = pieces[0].shape
    n = len(pieces)
    return run(
        functools.partial(backward_body, n),
        (number, entries, tiles, *pieces),
        [SMEM, SMEM] + [VMEM] * (n + 1),
        [shape((number.shape[0], width, edge))],
        [pltpu.VMEM((2 * n, width, edge), BF16), pltpu.VMEM((width, edge), F32)],
        mib=20,
        after=after,
    )[0]


def pair_sum_body(n, keep, come, *outs):
    for j in range(n):
        for half in range(2):
            i = half * n + j
            outs[j][half] = (keep[i].astype(F32) + come[i].astype(F32)).astype(BF16)


def pair_sum(keep, come):
    n = keep.shape[0] // 2
    return run(
        functools.partial(pair_sum_body, n),
        (keep, come),
        [VMEM] * 2,
        [shape((2, *keep.shape[1:]))] * n,
        mib=12,
    )


def tree(items):
    while len(items) > 1:
        items = [a + b for a, b in zip(items[::2], items[1::2])]
    return items[0]


def onward_body(own, far, near, middle, inward, part, message):
    part[...] = own[...].astype(F32) + near[...].astype(F32) + middle[...].astype(F32)
    message[...] = (far[...].astype(F32) + inward[...].astype(F32)).astype(BF16)


def onward(own, far, near, middle, inward, after):
    return run(
        onward_body,
        (own, far, near, middle, inward),
        [VMEM] * 5,
        [shape(own.shape, F32), shape(own.shape)],
        mib=12,
        after=after,
    )


def relay_body(n, *refs):
    for source, out in zip(refs[:n], refs[n:]):
        out[...] = source[...]


def relay(items, after):
    return run(
        functools.partial(relay_body, len(items)),
        tuple(items),
        [VMEM] * len(items),
        [shape(x.shape) for x in items],
        after=after,
    )


def choose_body(at_ends, across, middle, out_two, out_three, two, three):
    position = lax.shift_right_logical(lax.axis_index("col"), 1)
    ends = jnp.logical_or(position == 0, position == at_ends)
    two[...] = jnp.where(ends, out_two[...], across[...])
    three[...] = jnp.where(ends, out_three[...], middle[...])


def choose(last, across, middle, out_two, out_three):
    return run(
        functools.partial(choose_body, last),
        (across, middle, out_two, out_three),
        [VMEM] * 4,
        [shape(across.shape)] * 2,
    )


def agg_body(part, *refs):
    scale, out = refs[-2:]
    for half in range(2):
        summed = part[half]
        for x in refs[:-2]:
            summed = summed + x[half].astype(F32)
        wide = repeat_lanes(scale[lax.axis_index("row") * 2 + half], summed.shape[1])
        out[half] = (summed * wide).astype(BF16)


def aggregate(part, far, scale):
    return run(
        agg_body,
        (part, *far, scale),
        [VMEM] * (2 + len(far)),
        [shape(part.shape)],
    )[0]


def first_body(start, n, *refs):
    scale, weight, agg, out = refs[n], refs[n + 1], refs[-2], refs[-1]
    row = lax.axis_index("row")
    if start:
        agg[: 2 * start] = refs[n + 2][...]
        out[: 2 * start] = refs[n + 3][...]
    for i in range(n):
        j = start + i
        for half in range(2):
            value = jnp.dot(refs[i][half], weight[...], preferred_element_type=F32)
            wide = repeat_lanes(scale[(row ^ j) * 2 + half], value.shape[1])
            out[2 * j + half] = (jax.nn.gelu(value) * wide).astype(BF16)
            agg[2 * j + half] = refs[i][half]


def first_layer(aggs, scale, weight, before=(), after=()):
    n = len(aggs)
    start = before[0].shape[0] // 2 if before else 0
    return run(
        functools.partial(first_body, start, n),
        (*aggs, scale, weight, *before),
        [VMEM] * (n + 2 + len(before)),
        [shape((2 * (start + n), *aggs[0].shape[1:]))] * 2,
        mib=14,
        after=after,
    )


def second_body(part, *refs):
    scale, weight, out = refs[-3:]
    edge = part.shape[1]
    for half in range(2):
        summed = part[half]
        for x in refs[:-3]:
            summed = summed + x[half].astype(F32)
        wide = repeat_lanes(scale[lax.axis_index("row") * 2 + half], summed.shape[1])
        agg = (summed * wide).astype(BF16)
        value = jnp.dot(agg, weight[...], preferred_element_type=F32)
        out[half * edge : (half + 1) * edge, :] = value.astype(BF16)


def second_layer(part, far, scale, weight):
    halves, edge, width = part.shape
    return run(
        second_body,
        (part, *far, scale, weight),
        [VMEM] * (3 + len(far)),
        [shape((halves * edge, width))],
    )[0]


def grad_body(start, last, hidden_ref, aggs, outs, scale, w_first, w_second, *refs):
    row = lax.axis_index("row")
    core = lax.rem(lax.axis_index("col"), 2)
    first, second = refs[-2:]
    if start:
        first[...] = refs[0][...]
        second[...] = refs[1][...]
    else:
        first[...] = jnp.zeros_like(first)
        second[...] = jnp.zeros_like(second)

    def block(i, _):
        hidden, agg = hidden_ref[i], aggs[i]
        pre = jnp.dot(agg, w_first[...], preferred_element_type=F32)
        grad_hidden = lax.dot_general(
            hidden, w_second[...], (((0,), (1,)), ((), ())), preferred_element_type=F32
        )
        _, pullback = jax.vjp(jax.nn.gelu, pre)
        wide = repeat_lanes(scale[i ^ (2 * row)], pre.shape[1])
        grad_pre = pullback(grad_hidden * wide)[0].astype(BF16)
        first[...] += lax.dot_general(
            agg, grad_pre, (((0,), (0,)), ((), ())), preferred_element_type=F32
        )
        second[...] += lax.dot_general(
            outs[i], hidden, (((0,), (1,)), ((), ())), preferred_element_type=F32
        )
        return 0

    lax.fori_loop(start, aggs.shape[0], block, 0)
    if last:
        give, keep = refs[2:4]
        keep[...] = jnp.where(core == 0, first[...], second[...]).astype(BF16)
        give[...] = jnp.where(core == 0, second[...], first[...]).astype(BF16)


def weight_grads(start, hidden, aggs, outs, scale, w_first, w_second, before=(), after=()):
    dims = w_first.shape
    last = aggs.shape[0] == hidden.shape[0]
    return run(
        functools.partial(grad_body, start, last),
        (hidden, aggs, outs, scale, w_first, w_second, *before),
        [VMEM] * (6 + len(before)),
        [shape(dims)] * 2 if last else [shape(dims, F32)] * 2,
        [pltpu.VMEM(dims, F32)] * 2 if last else [],
        mib=26,
        after=after,
    )


def split_body(n, keep, come, *outs):
    row = lax.axis_index("row")
    rows = keep.shape[0] // n
    for j in range(n):
        part = pl.ds(pl.multiple_of((row ^ j) * rows, rows), rows)
        outs[j][...] = (keep[part, :].astype(F32) + come[part, :].astype(F32)).astype(BF16)


def split_sum(keep, come, n, after):
    rows, width = keep.shape
    return run(
        functools.partial(split_body, n),
        (keep, come),
        [VMEM] * 2,
        [shape((rows // n, width))] * n,
        after=after,
    )


def sum_body(n, *refs):
    refs[n][...] = tree([x[...].astype(F32) for x in refs[:n]]).astype(BF16)


def sum_parts(parts, after=()):
    return run(
        functools.partial(sum_body, len(parts)),
        tuple(parts),
        [VMEM] * len(parts),
        [shape(parts[0].shape)],
        after=after,
    )[0]


def join_body(n, *refs):
    row = lax.axis_index("row")
    rows = refs[0].shape[0]
    for j in range(n):
        refs[n][pl.ds(pl.multiple_of((row ^ j) * rows, rows), rows), :] = refs[j][...]


def join(parts):
    rows, width = parts[0].shape
    return run(
        functools.partial(join_body, len(parts)),
        tuple(parts),
        [VMEM] * len(parts),
        [shape((rows * len(parts), width))],
    )[0]


def select_body(mine, other, first, second):
    core = lax.rem(lax.axis_index("col"), 2)
    first[...] = jnp.where(core == 0, mine[...].astype(F32), other[...].astype(F32))
    second[...] = jnp.where(core == 0, other[...].astype(F32), mine[...].astype(F32))


def select(mine, other):
    return run(select_body, (mine, other), [VMEM] * 2, [shape(mine.shape, F32)] * 2)


COST = {
    prepare_body: 36,
    forward_body: 36,
    backward_body: 36,
    grad_body: 36,
}


def per_device(features, degree, tile_vals, tile_slot, tile_count, w_first, w_second, cotangent):
    n_row, n_col = lax.axis_size("row"), lax.axis_size("col")
    line = n_col // 2
    piece, width = cotangent.shape
    tiles = tile_vals[0, 0]
    edge = tiles.shape[-1]
    local_cols = n_row * 2
    slots, count = tile_slot[0, 0], tile_count[0]

    def col_send(value, pairs):
        return lax.ppermute(
            value, "col", [(2 * a + k, 2 * b + k) for a, b in pairs for k in range(2)]
        )

    def line_flip(value, j):
        return col_send(value, [(a, a ^ j) for a in range(line)])

    def core_flip(value):
        return lax.ppermute(value, "col", [(a, a ^ 1) for a in range(n_col)])

    def row_flip(value, j):
        return lax.ppermute(value, "row", [(a, a ^ j) for a in range(n_row)])

    def scatter_line(own, after=()):
        if line != 4:
            parts = [own[0]] + [line_flip(own[j], j) for j in range(1, line)]
            return tree([x.astype(F32) for x in parts]), []
        inward = col_send(own[3], [(0, 1), (3, 2)])
        middle = col_send(own[3], [(1, 2), (2, 1)])
        near = line_flip(own[1], 1)
        part, message = onward(own[0], own[2], near, middle, inward, after)
        return part, [line_flip(message, 2)]

    def gather_near(own):
        if line != 4:
            return []
        return [line_flip(own, 1), col_send(own, [(1, 2), (2, 1)])]

    def gather_far(own, near, middle, after):
        (across,) = relay([col_send(near, [(1, 2), (2, 1)])], after)
        out_two = col_send(middle, [(1, 0), (2, 3)])
        out_three = col_send(across, [(1, 0), (2, 3)])
        return [own, near, *choose(line - 1, across, middle, out_two, out_three)]

    halves = piece // edge
    scale, scaled = scale_kernel(degree[:, 0], cotangent, edge)
    early = gather_near(scaled)
    values = features[:, 0].reshape(local_cols, edge, width)
    first_in, number, entries, t_number, t_entries = prepare(
        count, slots, values, scale, 2 * n_col
    )

    give = forward(number, entries, tiles, first_in, True, 1)
    keep = forward(number, entries, tiles, first_in, True, 0)
    if early:
        early = relay(early, (keep,))
    own = pair_sum(keep, core_flip(give))
    part, far = scatter_line(own)
    if early:
        gathered = gather_far(scaled, *early, (own[0],))
    else:
        gathered = [scaled] + [line_flip(scaled, j) for j in range(1, line)]
    ranged = [x for g in gathered for x in (g, core_flip(g))]
    hidden = backward(t_number, t_entries, tiles, ranged)
    agg = aggregate(part, far, scale)
    spread = [agg] + [row_flip(agg, j) for j in range(1, n_row)]
    stacked = first_layer(spread[:-1], scale, w_first)
    sums = weight_grads(0, hidden, *stacked, scale, w_first, w_second)
    aggs, outs = first_layer(spread[-1:], scale, w_first, stacked, sums[:1])

    give = forward(number, entries, tiles, outs, False, 1)
    keep = forward(number, entries, tiles, outs, False, 0)
    own = pair_sum(keep, core_flip(give))

    give, keep = weight_grads(
        2 * n_row - 2, hidden, aggs, outs, scale, w_first, w_second, sums, (own[0],)
    )
    part, far = scatter_line(own, (keep,))
    parts = split_sum(keep, core_flip(give), n_row, (part,))
    moment = sum_parts([parts[0]] + [row_flip(parts[j], j) for j in range(1, n_row)])
    moment = sum_parts([moment] + [line_flip(moment, j) for j in range(1, line)], far)
    mine = join([moment] + [row_flip(moment, j) for j in range(1, n_row)])
    grad_first, grad_second = select(mine, core_flip(mine))
    return second_layer(part, far, scale, w_second), grad_first, grad_second


def solution(mesh):
    return jax.shard_map(
        per_device,
        mesh=mesh,
        in_specs=(
            P(None, "col", None, None),
            P(None, "col", None),
            P("row", "col", None, None, None),
            P("row", "col", None),
            P("row", "col"),
            P(),
            P(),
            P(("row", "col"), None),
        ),
        out_specs=(P(("row", "col"), None), P(), P()),
        check_vma=False,
    )
```

```python
import functools

import jax
import jax.numpy as jnp
from jax import lax
from jax.experimental import pallas as pl
from jax.experimental.pallas import tpu as pltpu
from jax.sharding import PartitionSpec as P

F32 = jnp.float32
BF16 = jnp.bfloat16
MIB = 1024 * 1024
VMEM = pl.BlockSpec(memory_space=pltpu.VMEM)
SMEM = pl.BlockSpec(memory_space=pltpu.SMEM)
ANY = pl.BlockSpec(memory_space=pl.ANY)


def run(body, args, specs, outs, scratch=(), mib=8, after=(), out_specs=None):
    n, extra = len(args), len(after)

    def whole(*refs):
        body(*refs[:n], *refs[n + extra :])

    return pl.pallas_call(
        whole,
        out_shape=outs,
        in_specs=specs + [ANY] * extra,
        out_specs=out_specs or [VMEM] * len(outs),
        scratch_shapes=list(scratch),
        compiler_params=pltpu.CompilerParams(vmem_limit_bytes=mib * MIB),
        cost_estimate=pl.CostEstimate(
            flops=int(COST.get(getattr(body, "func", body), 0) * 1e9),
            bytes_accessed=0,
            transcendentals=0,
        ),
    )(*args, *after)


def shape(dims, dtype=BF16):
    return jax.ShapeDtypeStruct(dims, dtype)


def list_tiles(count, slot_ref, number_ref, list_ref, local_cols, by_row):
    groups, cap = number_ref.shape[0], list_ref.shape[0] // number_ref.shape[0]
    blank = slot_ref.shape[0] * 1024
    bits = local_cols.bit_length() - 1

    def clear(g, _):
        number_ref[g] = 0
        for j in range(cap):
            list_ref[g * cap + j] = blank
        return 0

    lax.fori_loop(0, groups, clear, 0)

    def place(s, _):
        p = slot_ref[s]
        u, v = lax.shift_right_logical(p, bits), p & (local_cols - 1)
        g, other = (u, v) if by_row else (v, u)
        n = number_ref[g]
        list_ref[g * cap + n] = s * 1024 + other
        number_ref[g] = n + 1
        return 0

    lax.fori_loop(0, count, place, 0)


def repeat_lanes(scale, width):
    return jnp.concatenate([scale] * (width // scale.shape[-1]), 1)


def scale_body(degree, cot, scale, out):
    edge, lanes = scale.shape[1:]
    width = cot.shape[1]
    for i in range(scale.shape[0]):
        part = degree[i // 2 : i // 2 + 1, i % 2 * edge : (i % 2 + 1) * edge]
        line = 1.0 / jnp.sqrt(part.astype(F32))
        scale[i] = jnp.broadcast_to(line, (lanes, edge)).T
    row = lax.axis_index("row")
    for e in range(2):
        value = cot[e * edge : (e + 1) * edge, :].astype(F32)
        out[e] = (value * repeat_lanes(scale[row * 2 + e], width)).T.astype(BF16)


def scale_kernel(degree, cotangent, edge):
    return run(
        scale_body,
        (degree, cotangent),
        [VMEM] * 2,
        [shape((2 * degree.shape[0], edge, 128), F32), shape((2, cotangent.shape[1], edge))],
    )


def prepare_body(local_cols, count_ref, slot_ref, values, scale, out, *lists):
    list_tiles(count_ref[0], slot_ref, lists[0], lists[1], local_cols, True)
    list_tiles(count_ref[0], slot_ref, lists[2], lists[3], local_cols, False)

    def fill(i, _):
        wide = repeat_lanes(scale[i], values.shape[-1])
        out[i] = (values[i].astype(F32) * wide).astype(BF16)
        return 0

    lax.fori_loop(0, local_cols, fill, 0)


def prepare(count, slots, values, scale, block_rows):
    local_cols = values.shape[0]
    sizes = (block_rows, block_rows * local_cols, local_cols, block_rows * local_cols)
    return run(
        functools.partial(prepare_body, local_cols),
        (count, slots, values, scale),
        [SMEM] * 2 + [VMEM] * 2,
        [shape(values.shape)] + [shape((n,), jnp.int32) for n in sizes],
        out_specs=[VMEM] + [SMEM] * 4,
        mib=12,
    )


def sum_group(g, number_ref, list_ref, total, product, store):
    cap = list_ref.shape[0] // number_ref.shape[0]
    n = number_ref[g]

    def take(start, width):
        entries = [list_ref[g * cap + start + j] for j in range(width)]
        return product([(lax.shift_right_logical(x, 10), x & 1023) for x in entries])

    def exact(width):
        @pl.when(n == width)
        def _():
            store(take(0, width))

    @pl.when(n == 0)
    def _():
        store(jnp.zeros_like(total))

    for width in range(1, 5):
        exact(width)

    @pl.when(n > 4)
    def _():
        total[...] = jnp.zeros_like(total)
        fours = lax.shift_right_logical(n, 2)

        def four(m, _):
            total[...] += take(4 * m, 4)
            return 0

        def one(m, _):
            total[...] += take(m, 1)
            return 0

        lax.fori_loop(0, fours, four, 0)
        lax.fori_loop(4 * fours, n, one, 0)
        store(total[...])


def joined_dot(lhs, rhs):
    return jnp.dot(
        jnp.concatenate(lhs, 1), jnp.concatenate(rhs, 0), preferred_element_type=F32
    )


def forward_body(first, flip, number_ref, list_ref, tiles, source, out, total):
    col, row = lax.axis_index("col"), lax.axis_index("row")
    line = out.shape[0] // 2

    def product(pieces):
        def locate(v):
            return v if first else v ^ (2 * row)

        return joined_dot([tiles[s] for s, _ in pieces], [source[locate(v)] for _, v in pieces])

    for half in range(2):

        def block(i, _):
            def store(value):
                out[half * line + i] = value.astype(BF16)

            g = (col ^ (2 * i + flip)) * 2 + half
            sum_group(g, number_ref, list_ref, total, product, store)
            return 0

        lax.fori_loop(0, line, block, 0)


def forward(number, entries, tiles, source, first, flip, after=()):
    slots_n, edge, _ = tiles.shape
    width = source.shape[-1]
    return run(
        functools.partial(forward_body, first, flip),
        (number, entries, tiles, source),
        [SMEM, SMEM, VMEM, VMEM],
        [shape((number.shape[0] // 2, edge, width))],
        [pltpu.VMEM((edge, width), F32)],
        mib=16,
        after=after,
    )[0]


def backward_body(n, number_ref, list_ref, tiles, *refs):
    pieces_in, (out, ranged, total) = refs[:n], refs[n:]
    mask, flips = lax.axis_index("row") * 2, lax.axis_index("col") * 2
    for i, piece in enumerate(pieces_in):
        ranged[2 * i : 2 * i + 2] = piece[...]

    def product(pieces):
        return joined_dot([ranged[u ^ flips] for _, u in pieces], [tiles[s] for s, _ in pieces])

    def block(i, _):
        def store(value):
            out[i] = value.astype(BF16)

        sum_group(i ^ mask, number_ref, list_ref, total, product, store)
        return 0

    lax.fori_loop(0, out.shape[0], block, 0)


def backward(number, entries, tiles, pieces, after=()):
    slots_n, edge, _ = tiles.shape
    _, width, _ = pieces[0].shape
    n = len(pieces)
    return run(
        functools.partial(backward_body, n),
        (number, entries, tiles, *pieces),
        [SMEM, SMEM] + [VMEM] * (n + 1),
        [shape((number.shape[0], width, edge))],
        [pltpu.VMEM((2 * n, width, edge), BF16), pltpu.VMEM((width, edge), F32)],
        mib=20,
        after=after,
    )[0]


def pair_sum_body(n, keep, come, *outs):
    for j in range(n):
        for half in range(2):
            i = half * n + j
            outs[j][half] = (keep[i].astype(F32) + come[i].astype(F32)).astype(BF16)


def pair_sum(keep, come):
    n = keep.shape[0] // 2
    return run(
        functools.partial(pair_sum_body, n),
        (keep, come),
        [VMEM] * 2,
        [shape((2, *keep.shape[1:]))] * n,
        mib=12,
    )


def tree(items):
    while len(items) > 1:
        rest = items[len(items) // 2 * 2 :]
        items = [a + b for a, b in zip(items[::2], items[1::2])] + rest
    return items[0]


def relay_body(n, *refs):
    for source, out in zip(refs[:n], refs[n:]):
        out[...] = source[...]


def relay(items, after):
    return run(
        functools.partial(relay_body, len(items)),
        tuple(items),
        [VMEM] * len(items),
        [shape(x.shape) for x in items],
        after=after,
    )


def choose_body(at_ends, across, middle, out_two, out_three, two, three):
    position = lax.shift_right_logical(lax.axis_index("col"), 1)
    ends = jnp.logical_or(position == 0, position == at_ends)
    two[...] = jnp.where(ends, out_two[...], across[...])
    three[...] = jnp.where(ends, out_three[...], middle[...])


def choose(last, across, middle, out_two, out_three):
    return run(
        functools.partial(choose_body, last),
        (across, middle, out_two, out_three),
        [VMEM] * 4,
        [shape(across.shape)] * 2,
    )


def agg_body(n, *refs):
    scale, outs = refs[n], refs[n + 1 :]
    for half, out in enumerate(outs):
        summed = tree([x[half].astype(F32) for x in refs[:n]])
        wide = repeat_lanes(scale[lax.axis_index("row") * 2 + half], summed.shape[1])
        out[...] = (summed * wide).astype(BF16)


def aggregate(parts, scale):
    return run(
        functools.partial(agg_body, len(parts)),
        (*parts, scale),
        [VMEM] * (len(parts) + 1),
        [shape(parts[0].shape[1:])] * 2,
    )


def first_body(start, n, *refs):
    scale, weight, agg, out = refs[2 * n], refs[2 * n + 1], refs[-2], refs[-1]
    row = lax.axis_index("row")
    if start:
        agg[: 2 * start] = refs[2 * n + 2][...]
        out[: 2 * start] = refs[2 * n + 3][...]
    for i in range(2 * n):
        block = 2 * start + i
        value = jnp.dot(refs[i][...], weight[...], preferred_element_type=F32)
        wide = repeat_lanes(scale[block ^ (2 * row)], value.shape[1])
        out[block] = (jax.nn.gelu(value) * wide).astype(BF16)
        agg[block] = refs[i][...]


def first_layer(aggs, scale, weight, before=(), after=()):
    n = len(aggs)
    start = before[0].shape[0] // 2 if before else 0
    return run(
        functools.partial(first_body, start, n),
        (*[x for pair in aggs for x in pair], scale, weight, *before),
        [VMEM] * (2 * n + 2 + len(before)),
        [shape((2 * (start + n), *aggs[0][0].shape))] * 2,
        mib=14,
        after=after,
    )


def second_body(*refs):
    scale, weight, out = refs[-3:]
    edge = refs[0].shape[1]
    for half in range(2):
        summed = tree([x[half].astype(F32) for x in refs[:-3]])
        wide = repeat_lanes(scale[lax.axis_index("row") * 2 + half], summed.shape[1])
        agg = (summed * wide).astype(BF16)
        value = jnp.dot(agg, weight[...], preferred_element_type=F32)
        out[half * edge : (half + 1) * edge, :] = value.astype(BF16)


def second_layer(parts, scale, weight):
    halves, edge, width = parts[0].shape
    return run(
        second_body,
        (*parts, scale, weight),
        [VMEM] * (2 + len(parts)),
        [shape((halves * edge, width))],
    )[0]


def grad_body(start, last, hidden_ref, aggs, outs, scale, w_first, w_second, *refs):
    row = lax.axis_index("row")
    core = lax.rem(lax.axis_index("col"), 2)
    first, second = refs[-2:]
    if start:
        first[...] = refs[0][...]
        second[...] = refs[1][...]
    else:
        first[...] = jnp.zeros_like(first)
        second[...] = jnp.zeros_like(second)

    def block(i, _):
        hidden, agg = hidden_ref[i], aggs[i]
        pre = jnp.dot(agg, w_first[...], preferred_element_type=F32)
        grad_hidden = lax.dot_general(
            hidden, w_second[...], (((0,), (1,)), ((), ())), preferred_element_type=F32
        )
        _, pullback = jax.vjp(jax.nn.gelu, pre)
        wide = repeat_lanes(scale[i ^ (2 * row)], pre.shape[1])
        grad_pre = pullback(grad_hidden * wide)[0].astype(BF16)
        first[...] += lax.dot_general(
            agg, grad_pre, (((0,), (0,)), ((), ())), preferred_element_type=F32
        )
        second[...] += lax.dot_general(
            outs[i], hidden, (((0,), (1,)), ((), ())), preferred_element_type=F32
        )
        return 0

    lax.fori_loop(start, aggs.shape[0], block, 0)
    if last:
        give, keep = refs[2:4]
        keep[...] = jnp.where(core == 0, first[...], second[...]).astype(BF16)
        give[...] = jnp.where(core == 0, second[...], first[...]).astype(BF16)


def weight_grads(start, hidden, aggs, outs, scale, w_first, w_second, before=(), after=()):
    dims = w_first.shape
    last = aggs.shape[0] == hidden.shape[0]
    return run(
        functools.partial(grad_body, start, last),
        (hidden, aggs, outs, scale, w_first, w_second, *before),
        [VMEM] * (6 + len(before)),
        [shape(dims)] * 2 if last else [shape(dims, F32)] * 2,
        [pltpu.VMEM(dims, F32)] * 2 if last else [],
        mib=26,
        after=after,
    )


def position(axis):
    if axis == "row":
        return lax.axis_index("row")
    return lax.shift_right_logical(lax.axis_index("col"), 1)


def split_body(n, axis, *refs):
    ins, outs = refs[:-n], refs[-n:]
    rows = ins[0].shape[0] // n
    for j in range(n):
        part = pl.ds(pl.multiple_of((position(axis) ^ j) * rows, rows), rows)
        outs[j][...] = tree([x[part, :].astype(F32) for x in ins]).astype(BF16)


def split_sum(items, n, axis, after=()):
    rows, width = items[0].shape
    return run(
        functools.partial(split_body, n, axis),
        tuple(items),
        [VMEM] * len(items),
        [shape((rows // n, width))] * n,
        after=after,
    )


def sum_body(n, *refs):
    refs[n][...] = tree([x[...].astype(F32) for x in refs[:n]]).astype(BF16)


def sum_parts(parts, after=()):
    return run(
        functools.partial(sum_body, len(parts)),
        tuple(parts),
        [VMEM] * len(parts),
        [shape(parts[0].shape)],
        after=after,
    )[0]


def join_body(n, axis, *refs):
    rows = refs[0].shape[0]
    for j in range(n):
        part = pl.ds(pl.multiple_of((position(axis) ^ j) * rows, rows), rows)
        refs[n][part, :] = refs[j][...]


def join(parts, axis, after=()):
    rows, width = parts[0].shape
    return run(
        functools.partial(join_body, len(parts), axis),
        tuple(parts),
        [VMEM] * len(parts),
        [shape((rows * len(parts), width))],
        after=after,
    )[0]


def select_body(mine, other, first, second):
    core = lax.rem(lax.axis_index("col"), 2)
    first[...] = jnp.where(core == 0, mine[...].astype(F32), other[...].astype(F32))
    second[...] = jnp.where(core == 0, other[...].astype(F32), mine[...].astype(F32))


def select(mine, other):
    return run(select_body, (mine, other), [VMEM] * 2, [shape(mine.shape, F32)] * 2)


COST = {
    prepare_body: 36,
    forward_body: 36,
    backward_body: 36,
    grad_body: 36,
}


def per_device(features, degree, tile_vals, tile_slot, tile_count, w_first, w_second, cotangent):
    n_row, n_col = lax.axis_size("row"), lax.axis_size("col")
    line = n_col // 2
    piece, width = cotangent.shape
    tiles = tile_vals[0, 0]
    edge = tiles.shape[-1]
    local_cols = n_row * 2
    slots, count = tile_slot[0, 0], tile_count[0]

    def col_send(value, pairs):
        return lax.ppermute(
            value, "col", [(2 * a + k, 2 * b + k) for a, b in pairs for k in range(2)]
        )

    def line_flip(value, j):
        return col_send(value, [(a, a ^ j) for a in range(line)])

    def core_flip(value):
        return lax.ppermute(value, "col", [(a, a ^ 1) for a in range(n_col)])

    def row_flip(value, j):
        return lax.ppermute(value, "row", [(a, a ^ j) for a in range(n_row)])

    def scatter_line(own, after=()):
        if line != 4:
            return [own[0]] + [line_flip(own[j], j) for j in range(1, line)]
        inward = col_send(own[3], [(0, 1), (3, 2)])
        middle = col_send(own[3], [(1, 2), (2, 1)])
        onward = col_send(sum_parts([own[2], inward], after), [(1, 3), (2, 0)])
        near = line_flip(own[1], 1)
        far = col_send(own[2], [(0, 2), (3, 1)])
        return [own[0], near, middle, onward, far]

    def gather_row(pair):
        if n_row != 4:
            return [pair] + [[row_flip(x, j) for x in pair] for j in range(1, n_row)]
        x_first, y_second = row_flip(pair[0], 1), row_flip(pair[1], 2)
        x_second, y_first = row_flip(pair[1], 1), row_flip(pair[0], 2)
        diagonal = [row_flip(x_first, 2), row_flip(y_second, 1)]
        return [pair, [x_first, x_second], [y_first, y_second], diagonal]

    def gather_near(own):
        if line != 4:
            return []
        return [line_flip(own, 1), col_send(own, [(1, 2), (2, 1)])]

    def gather_far(own, near, middle, after):
        (across,) = relay([col_send(near, [(1, 2), (2, 1)])], after)
        out_two = col_send(middle, [(1, 0), (2, 3)])
        out_three = col_send(across, [(1, 0), (2, 3)])
        return [own, near, *choose(line - 1, across, middle, out_two, out_three)]

    halves = piece // edge
    scale, scaled = scale_kernel(degree[:, 0], cotangent, edge)
    early = gather_near(scaled)
    values = features[:, 0].reshape(local_cols, edge, width)
    first_in, number, entries, t_number, t_entries = prepare(
        count, slots, values, scale, 2 * n_col
    )

    give = forward(number, entries, tiles, first_in, True, 1)
    keep = forward(number, entries, tiles, first_in, True, 0)
    if early:
        early = relay(early, (give,))
    own = pair_sum(keep, core_flip(give))
    parts = scatter_line(own)
    if early:
        gathered = gather_far(scaled, *early, (own[0],))
    else:
        gathered = [scaled] + [line_flip(scaled, j) for j in range(1, line)]
    ranged = [x for g in gathered for x in (g, core_flip(g))]
    spread = gather_row(aggregate(parts, scale))
    arrived = [spread[1][0], spread[2][1]]
    hidden = backward(t_number, t_entries, tiles, ranged, arrived)
    stacked = first_layer(spread[:1], scale, w_first)
    sums = weight_grads(0, hidden, *stacked, scale, w_first, w_second)
    stacked = first_layer(spread[1:-1], scale, w_first, stacked, sums[:1])
    aggs, outs = first_layer(spread[-1:], scale, w_first, stacked)

    give = forward(number, entries, tiles, outs, False, 1)
    keep = forward(number, entries, tiles, outs, False, 0)
    own = pair_sum(keep, core_flip(give))

    give, keep = weight_grads(2, hidden, aggs, outs, scale, w_first, w_second, sums, (own[0],))
    parts = scatter_line(own, (keep,))
    split = split_sum([keep, core_flip(give)], n_row, "row")
    moment = [split[0]] + [row_flip(split[j], j) for j in range(1, n_row)]
    if moment[0].shape[0] % (16 * line) == 0:
        split = split_sum(moment, line, "line", parts[1:3])
        moment = sum_parts([split[0]] + [line_flip(split[j], j) for j in range(1, line)])
        moment = [moment] + [line_flip(moment, j) for j in range(1, line)]
        moment = join(moment, "line", parts[3:])
    else:
        moment = sum_parts(moment)
        moment = sum_parts([moment] + [line_flip(moment, j) for j in range(1, line)])
    mine = join([moment] + [row_flip(moment, j) for j in range(1, n_row)], "row")
    grad_first, grad_second = select(mine, core_flip(mine))
    return second_layer(parts, scale, w_second), grad_first, grad_second


def solution(mesh):
    return jax.shard_map(
        per_device,
        mesh=mesh,
        in_specs=(
            P(None, "col", None, None),
            P(None, "col", None),
            P("row", "col", None, None, None),
            P("row", "col", None),
            P("row", "col"),
            P(),
            P(),
            P(("row", "col"), None),
        ),
        out_specs=(P(("row", "col"), None), P(), P()),
        check_vma=False,
    )
```

```python
import functools

import jax
import jax.numpy as jnp
from jax import lax
from jax.experimental import pallas as pl
from jax.experimental.pallas import tpu as pltpu
from jax.sharding import PartitionSpec as P

F32 = jnp.float32
BF16 = jnp.bfloat16
MIB = 1024 * 1024
VMEM = pl.BlockSpec(memory_space=pltpu.VMEM)
SMEM = pl.BlockSpec(memory_space=pltpu.SMEM)
ANY = pl.BlockSpec(memory_space=pl.ANY)


def run(body, args, specs, outs, scratch=(), mib=8, after=(), out_specs=None):
    n, extra = len(args), len(after)

    def whole(*refs):
        body(*refs[:n], *refs[n + extra :])

    return pl.pallas_call(
        whole,
        out_shape=outs,
        in_specs=specs + [ANY] * extra,
        out_specs=out_specs or [VMEM] * len(outs),
        scratch_shapes=list(scratch),
        compiler_params=pltpu.CompilerParams(vmem_limit_bytes=mib * MIB),
        cost_estimate=pl.CostEstimate(
            flops=int(COST.get(getattr(body, "func", body), 0) * 1e9),
            bytes_accessed=0,
            transcendentals=0,
        ),
    )(*args, *after)


def shape(dims, dtype=BF16):
    return jax.ShapeDtypeStruct(dims, dtype)


def list_tiles(count, slot_ref, number_ref, list_ref, local_cols, by_row):
    groups, cap = number_ref.shape[0], list_ref.shape[0] // number_ref.shape[0]
    blank = slot_ref.shape[0] * 1024
    bits = local_cols.bit_length() - 1

    def clear(g, _):
        number_ref[g] = 0
        for j in range(cap):
            list_ref[g * cap + j] = blank
        return 0

    lax.fori_loop(0, groups, clear, 0)

    def place(s, _):
        p = slot_ref[s]
        u, v = lax.shift_right_logical(p, bits), p & (local_cols - 1)
        g, other = (u, v) if by_row else (v, u)
        n = number_ref[g]
        list_ref[g * cap + n] = s * 1024 + other
        number_ref[g] = n + 1
        return 0

    lax.fori_loop(0, count, place, 0)


def repeat_lanes(scale, width):
    return jnp.concatenate([scale] * (width // scale.shape[-1]), 1)


def scale_body(degree, cot, scale, out):
    edge, lanes = scale.shape[1:]
    width = cot.shape[1]
    for i in range(scale.shape[0]):
        part = degree[i // 2 : i // 2 + 1, i % 2 * edge : (i % 2 + 1) * edge]
        line = 1.0 / jnp.sqrt(part.astype(F32))
        scale[i] = jnp.broadcast_to(line, (lanes, edge)).T
    row = lax.axis_index("row")
    for e in range(2):
        value = cot[e * edge : (e + 1) * edge, :].astype(F32)
        out[e] = (value * repeat_lanes(scale[row * 2 + e], width)).T.astype(BF16)


def scale_kernel(degree, cotangent, edge):
    return run(
        scale_body,
        (degree, cotangent),
        [VMEM] * 2,
        [shape((2 * degree.shape[0], edge, 128), F32), shape((2, cotangent.shape[1], edge))],
    )


def prepare_body(count_ref, slot_ref, values, scale, out, *lists):
    local_cols = values.shape[0]
    list_tiles(count_ref[0], slot_ref, lists[0], lists[1], local_cols, True)
    list_tiles(count_ref[0], slot_ref, lists[2], lists[3], local_cols, False)

    def fill(i, _):
        wide = repeat_lanes(scale[i], values.shape[-1])
        out[i] = (values[i].astype(F32) * wide).astype(BF16)
        return 0

    lax.fori_loop(0, local_cols, fill, 0)


def prepare(count, slots, values, scale, block_rows):
    local_cols = values.shape[0]
    sizes = (block_rows, block_rows * local_cols, local_cols, block_rows * local_cols)
    return run(
        prepare_body,
        (count, slots, values, scale),
        [SMEM] * 2 + [VMEM] * 2,
        [shape(values.shape)] + [shape((n,), jnp.int32) for n in sizes],
        out_specs=[VMEM] + [SMEM] * 4,
        mib=12,
    )


def sum_group(g, number_ref, list_ref, total, product, store):
    cap = list_ref.shape[0] // number_ref.shape[0]
    n = number_ref[g]

    def take(start, width):
        entries = [list_ref[g * cap + start + j] for j in range(width)]
        return product([(lax.shift_right_logical(x, 10), x & 1023) for x in entries])

    def exact(width):
        @pl.when(n == width)
        def _():
            store(take(0, width))

    @pl.when(n == 0)
    def _():
        store(jnp.zeros_like(total))

    for width in range(1, 5):
        exact(width)

    @pl.when(n > 4)
    def _():
        total[...] = jnp.zeros_like(total)
        fours = lax.shift_right_logical(n, 2)

        def four(m, _):
            total[...] += take(4 * m, 4)
            return 0

        def one(m, _):
            total[...] += take(m, 1)
            return 0

        lax.fori_loop(0, fours, four, 0)
        lax.fori_loop(4 * fours, n, one, 0)
        store(total[...])


def joined_dot(lhs, rhs):
    return jnp.dot(
        jnp.concatenate(lhs, 1), jnp.concatenate(rhs, 0), preferred_element_type=F32
    )


def forward_body(first, flip, number_ref, list_ref, tiles, source, out, total):
    col, row = lax.axis_index("col"), lax.axis_index("row")
    line = out.shape[0] // 2

    def product(pieces):
        def locate(v):
            return v if first else v ^ (2 * row)

        return joined_dot([tiles[s] for s, _ in pieces], [source[locate(v)] for _, v in pieces])

    for half in range(2):

        def block(i, _):
            def store(value):
                out[half * line + i] = value.astype(BF16)

            g = (col ^ (2 * i + flip)) * 2 + half
            sum_group(g, number_ref, list_ref, total, product, store)
            return 0

        lax.fori_loop(0, line, block, 0)


def forward(number, entries, tiles, source, first, flip, after=()):
    slots_n, edge, _ = tiles.shape
    width = source.shape[-1]
    return run(
        functools.partial(forward_body, first, flip),
        (number, entries, tiles, source),
        [SMEM, SMEM, VMEM, VMEM],
        [shape((number.shape[0] // 2, edge, width))],
        [pltpu.VMEM((edge, width), F32)],
        mib=16,
        after=after,
    )[0]


def backward_body(n, number_ref, list_ref, tiles, *refs):
    pieces_in, (out, ranged, total) = refs[:n], refs[n:]
    mask, flips = lax.axis_index("row") * 2, lax.axis_index("col") * 2
    for i, piece in enumerate(pieces_in):
        ranged[2 * i : 2 * i + 2] = piece[...]

    def product(pieces):
        return joined_dot([ranged[u ^ flips] for _, u in pieces], [tiles[s] for s, _ in pieces])

    def block(i, _):
        def store(value):
            out[i] = value.astype(BF16)

        sum_group(i ^ mask, number_ref, list_ref, total, product, store)
        return 0

    lax.fori_loop(0, out.shape[0], block, 0)


def backward(number, entries, tiles, pieces, after=()):
    slots_n, edge, _ = tiles.shape
    _, width, _ = pieces[0].shape
    n = len(pieces)
    return run(
        functools.partial(backward_body, n),
        (number, entries, tiles, *pieces),
        [SMEM, SMEM] + [VMEM] * (n + 1),
        [shape((number.shape[0], width, edge))],
        [pltpu.VMEM((2 * n, width, edge), BF16), pltpu.VMEM((width, edge), F32)],
        mib=20,
        after=after,
    )[0]


def pair_sum_body(n, keep, come, *outs):
    for j in range(n):
        for half in range(2):
            i = half * n + j
            outs[j][half] = (keep[i].astype(F32) + come[i].astype(F32)).astype(BF16)


def pair_sum(keep, come):
    n = keep.shape[0] // 2
    return run(
        functools.partial(pair_sum_body, n),
        (keep, come),
        [VMEM] * 2,
        [shape((2, *keep.shape[1:]))] * n,
        mib=12,
    )


def tree(items):
    while len(items) > 1:
        rest = items[len(items) // 2 * 2 :]
        items = [a + b for a, b in zip(items[::2], items[1::2])] + rest
    return items[0]


def relay_body(n, *refs):
    for source, out in zip(refs[:n], refs[n:]):
        out[...] = source[...]


def relay(items, after):
    return run(
        functools.partial(relay_body, len(items)),
        tuple(items),
        [VMEM] * len(items),
        [shape(x.shape) for x in items],
        after=after,
    )


def choose_body(at_ends, across, middle, out_two, out_three, two, three):
    position = lax.shift_right_logical(lax.axis_index("col"), 1)
    ends = jnp.logical_or(position == 0, position == at_ends)
    two[...] = jnp.where(ends, out_two[...], across[...])
    three[...] = jnp.where(ends, out_three[...], middle[...])


def choose(last, across, middle, out_two, out_three, after):
    return run(
        functools.partial(choose_body, last),
        (across, middle, out_two, out_three),
        [VMEM] * 4,
        [shape(across.shape)] * 2,
        after=after,
    )


def agg_body(n, *refs):
    scale, outs = refs[n], refs[n + 1 :]
    for half, out in enumerate(outs):
        summed = tree([x[half].astype(F32) for x in refs[:n]])
        wide = repeat_lanes(scale[lax.axis_index("row") * 2 + half], summed.shape[1])
        out[...] = (summed * wide).astype(BF16)


def aggregate(parts, scale, after):
    return run(
        functools.partial(agg_body, len(parts)),
        (*parts, scale),
        [VMEM] * (len(parts) + 1),
        [shape(parts[0].shape[1:])] * 2,
        after=after,
    )


def first_body(start, n, *refs):
    scale, weight, agg, out = refs[2 * n], refs[2 * n + 1], refs[-2], refs[-1]
    row = lax.axis_index("row")
    if start:
        agg[: 2 * start] = refs[2 * n + 2][...]
        out[: 2 * start] = refs[2 * n + 3][...]
    for i in range(2 * n):
        block = 2 * start + i
        value = jnp.dot(refs[i][...], weight[...], preferred_element_type=F32)
        wide = repeat_lanes(scale[block ^ (2 * row)], value.shape[1])
        out[block] = (jax.nn.gelu(value) * wide).astype(BF16)
        agg[block] = refs[i][...]


def first_layer(aggs, scale, weight, before=(), after=()):
    n = len(aggs)
    start = before[0].shape[0] // 2 if before else 0
    return run(
        functools.partial(first_body, start, n),
        (*[x for pair in aggs for x in pair], scale, weight, *before),
        [VMEM] * (2 * n + 2 + len(before)),
        [shape((2 * (start + n), *aggs[0][0].shape))] * 2,
        mib=14,
        after=after,
    )


def second_body(*refs):
    scale, weight, out = refs[-3:]
    edge = refs[0].shape[1]
    for half in range(2):
        summed = tree([x[half].astype(F32) for x in refs[:-3]])
        wide = repeat_lanes(scale[lax.axis_index("row") * 2 + half], summed.shape[1])
        agg = (summed * wide).astype(BF16)
        value = jnp.dot(agg, weight[...], preferred_element_type=F32)
        out[half * edge : (half + 1) * edge, :] = value.astype(BF16)


def second_layer(parts, scale, weight):
    halves, edge, width = parts[0].shape
    return run(
        second_body,
        (*parts, scale, weight),
        [VMEM] * (2 + len(parts)),
        [shape((halves * edge, width))],
    )[0]


def grad_body(start, last, hidden_ref, aggs, outs, scale, w_first, w_second, *refs):
    row = lax.axis_index("row")
    core = lax.rem(lax.axis_index("col"), 2)
    first, second = refs[-2:]
    if start:
        first[...] = refs[0][...]
        second[...] = refs[1][...]
    else:
        first[...] = jnp.zeros_like(first)
        second[...] = jnp.zeros_like(second)

    def block(i, _):
        hidden, agg = hidden_ref[i], aggs[i]
        pre = jnp.dot(agg, w_first[...], preferred_element_type=F32)
        grad_hidden = lax.dot_general(
            hidden, w_second[...], (((0,), (1,)), ((), ())), preferred_element_type=F32
        )
        _, pullback = jax.vjp(jax.nn.gelu, pre)
        wide = repeat_lanes(scale[i ^ (2 * row)], pre.shape[1])
        grad_pre = pullback(grad_hidden * wide)[0].astype(BF16)
        first[...] += lax.dot_general(
            agg, grad_pre, (((0,), (0,)), ((), ())), preferred_element_type=F32
        )
        second[...] += lax.dot_general(
            outs[i], hidden, (((0,), (1,)), ((), ())), preferred_element_type=F32
        )
        return 0

    lax.fori_loop(start, aggs.shape[0], block, 0)
    if last:
        give, keep = refs[2:4]
        keep[...] = jnp.where(core == 0, first[...], second[...]).astype(BF16)
        give[...] = jnp.where(core == 0, second[...], first[...]).astype(BF16)


def weight_grads(start, hidden, aggs, outs, scale, w_first, w_second, before=(), after=()):
    dims = w_first.shape
    last = aggs.shape[0] == hidden.shape[0]
    return run(
        functools.partial(grad_body, start, last),
        (hidden, aggs, outs, scale, w_first, w_second, *before),
        [VMEM] * (6 + len(before)),
        [shape(dims)] * 2 if last else [shape(dims, F32)] * 2,
        [pltpu.VMEM(dims, F32)] * 2 if last else [],
        mib=26,
        after=after,
    )


def position(axis):
    if axis == "row":
        return lax.axis_index("row")
    return lax.shift_right_logical(lax.axis_index("col"), 1)


def split_body(n, axis, *refs):
    ins, outs = refs[:-n], refs[-n:]
    rows = ins[0].shape[0] // n
    for j in range(n):
        part = pl.ds(pl.multiple_of((position(axis) ^ j) * rows, rows), rows)
        outs[j][...] = tree([x[part, :].astype(F32) for x in ins]).astype(BF16)


def split_sum(items, n, axis, after=()):
    rows, width = items[0].shape
    return run(
        functools.partial(split_body, n, axis),
        tuple(items),
        [VMEM] * len(items),
        [shape((rows // n, width))] * n,
        after=after,
    )


def sum_body(n, *refs):
    refs[n][...] = tree([x[...].astype(F32) for x in refs[:n]]).astype(BF16)


def sum_parts(parts, after=()):
    return run(
        functools.partial(sum_body, len(parts)),
        tuple(parts),
        [VMEM] * len(parts),
        [shape(parts[0].shape)],
        after=after,
    )[0]


def join_body(n, axis, *refs):
    rows = refs[0].shape[0]
    for j in range(n):
        part = pl.ds(pl.multiple_of((position(axis) ^ j) * rows, rows), rows)
        refs[n][part, :] = refs[j][...]


def join(parts, axis, after=()):
    rows, width = parts[0].shape
    return run(
        functools.partial(join_body, len(parts), axis),
        tuple(parts),
        [VMEM] * len(parts),
        [shape((rows * len(parts), width))],
        after=after,
    )[0]


def select_body(mine, other, first, second):
    core = lax.rem(lax.axis_index("col"), 2)
    first[...] = jnp.where(core == 0, mine[...].astype(F32), other[...].astype(F32))
    second[...] = jnp.where(core == 0, other[...].astype(F32), mine[...].astype(F32))


def select(mine, other):
    return run(select_body, (mine, other), [VMEM] * 2, [shape(mine.shape, F32)] * 2)


COST = {
    forward_body: 36,
    grad_body: 36,
}


def per_device(features, degree, tile_vals, tile_slot, tile_count, w_first, w_second, cotangent):
    n_row, n_col = lax.axis_size("row"), lax.axis_size("col")
    line = n_col // 2
    piece, width = cotangent.shape
    tiles = tile_vals[0, 0]
    edge = tiles.shape[-1]
    local_cols = n_row * 2
    slots, count = tile_slot[0, 0], tile_count[0]

    def col_send(value, pairs):
        return lax.ppermute(
            value, "col", [(2 * a + k, 2 * b + k) for a, b in pairs for k in range(2)]
        )

    def line_flip(value, j):
        return col_send(value, [(a, a ^ j) for a in range(line)])

    def core_flip(value):
        return lax.ppermute(value, "col", [(a, a ^ 1) for a in range(n_col)])

    def row_flip(value, j):
        return lax.ppermute(value, "row", [(a, a ^ j) for a in range(n_row)])

    def scatter_begin(own, after=()):
        if line != 4:
            return own[2], None
        to_three = col_send(own[3], [(0, 1), (3, 2)])
        to_two = col_send(own[2], [(0, 1), (3, 2)])
        return sum_parts([own[2], to_three], after), to_two

    def scatter_next(own, begun, after):
        if line != 4:
            return own[3], []
        crossing = sum_parts([own[3], begun[1]], after)
        onward = col_send(begun[0], [(1, 3), (2, 0)])
        return crossing, [col_send(crossing, [(1, 2), (2, 1)]), onward]

    def scatter_end(own, arrived, near):
        if line != 4:
            return [own[0]] + [line_flip(own[j], j) for j in range(1, line)]
        return [own[0], line_flip(near, 1), *arrived]

    def gather_row(pair):
        if n_row != 4:
            return [pair] + [[row_flip(x, j) for x in pair] for j in range(1, n_row)]
        x_first, y_second = row_flip(pair[0], 1), row_flip(pair[1], 2)
        x_second, y_first = row_flip(pair[1], 1), row_flip(pair[0], 2)
        diagonal = [row_flip(x_first, 2), row_flip(y_second, 1)]
        return [pair, [x_first, x_second], [y_first, y_second], diagonal]

    def gather_near(own):
        if line != 4:
            return []
        return [line_flip(own, 1), col_send(own, [(1, 2), (2, 1)])]

    def gather_far(own, near, middle, after, late):
        (across,) = relay([col_send(near, [(1, 2), (2, 1)])], after)
        out_two = col_send(middle, [(1, 0), (2, 3)])
        out_three = col_send(across, [(1, 0), (2, 3)])
        return [own, near, *choose(line - 1, across, middle, out_two, out_three, late)]

    halves = piece // edge
    scale, scaled = scale_kernel(degree[:, 0], cotangent, edge)
    early = gather_near(scaled)
    values = features[:, 0].reshape(local_cols, edge, width)
    first_in, number, entries, t_number, t_entries = prepare(
        count, slots, values, scale, 2 * n_col
    )

    give = forward(number, entries, tiles, first_in, True, 1)
    keep = forward(number, entries, tiles, first_in, True, 0)
    if early:
        early = relay(early, (give,))
    own = pair_sum(keep, core_flip(give))
    begun = scatter_begin(own)
    crossing, arrived = scatter_next(own, begun, begun[:1])
    parts = scatter_end(own, arrived, own[1])
    if early:
        late = (crossing, arrived[1])
        gathered = gather_far(scaled, *early, begun[:1], late)
    else:
        gathered = [scaled] + [line_flip(scaled, j) for j in range(1, line)]
    ranged = [x for g in gathered for x in (g, core_flip(g))]
    hidden = backward(t_number, t_entries, tiles, ranged)
    spread = gather_row(aggregate(parts, scale, (hidden,)))
    stacked = first_layer(spread[:1], scale, w_first)
    sums = weight_grads(0, hidden, *stacked, scale, w_first, w_second)
    stacked = first_layer(spread[1:-1], scale, w_first, stacked, sums[:1])
    aggs, outs = first_layer(spread[-1:], scale, w_first, stacked)

    give = forward(number, entries, tiles, outs, False, 1)
    keep = forward(number, entries, tiles, outs, False, 0)
    own = pair_sum(keep, core_flip(give))

    give, keep = weight_grads(2, hidden, aggs, outs, scale, w_first, w_second, sums, (own[0],))
    begun = scatter_begin(own, (keep,))
    split = split_sum([keep, core_flip(give)], n_row, "row", begun[:1])
    moment = [split[0]] + [row_flip(split[j], j) for j in range(1, n_row)]
    crossing, arrived = scatter_next(own, begun, moment[1:])
    if moment[0].shape[0] % (16 * line) == 0:
        split = split_sum(moment, line, "line", (crossing,))
        moment = sum_parts(
            [split[0]] + [line_flip(split[j], j) for j in range(1, line)], arrived[1:]
        )
        moment = join([moment] + [line_flip(moment, j) for j in range(1, line)], "line")
    else:
        moment = sum_parts(moment)
        moment = sum_parts([moment] + [line_flip(moment, j) for j in range(1, line)])
    (near,) = relay(own[1:2], (moment,))
    moment = [moment] + [row_flip(moment, j) for j in range(1, n_row)]
    mine = join(moment, "row", arrived[:1])
    grad_first, grad_second = select(mine, core_flip(mine))
    parts = scatter_end(own, arrived, near)
    return second_layer(parts, scale, w_second), grad_first, grad_second


def solution(mesh):
    return jax.shard_map(
        per_device,
        mesh=mesh,
        in_specs=(
            P(None, "col", None, None),
            P(None, "col", None),
            P("row", "col", None, None, None),
            P("row", "col", None),
            P("row", "col"),
            P(),
            P(),
            P(("row", "col"), None),
        ),
        out_specs=(P(("row", "col"), None), P(), P()),
        check_vma=False,
    )
```

```python
import functools

import jax
import jax.numpy as jnp
from jax import lax
from jax.experimental import pallas as pl
from jax.experimental.pallas import tpu as pltpu
from jax.sharding import PartitionSpec as P

F32 = jnp.float32
BF16 = jnp.bfloat16
MIB = 1024 * 1024
VMEM = pl.BlockSpec(memory_space=pltpu.VMEM)
SMEM = pl.BlockSpec(memory_space=pltpu.SMEM)
ANY = pl.BlockSpec(memory_space=pl.ANY)


def run(body, args, specs, outs, scratch=(), mib=8, after=(), out_specs=None):
    n, extra = len(args), len(after)

    def whole(*refs):
        body(*refs[:n], *refs[n + extra :])

    return pl.pallas_call(
        whole,
        out_shape=outs,
        in_specs=specs + [ANY] * extra,
        out_specs=out_specs or [VMEM] * len(outs),
        scratch_shapes=list(scratch),
        compiler_params=pltpu.CompilerParams(vmem_limit_bytes=mib * MIB),
        cost_estimate=pl.CostEstimate(
            flops=int(COST.get(getattr(body, "func", body), 0) * 1e9),
            bytes_accessed=0,
            transcendentals=0,
        ),
    )(*args, *after)


def shape(dims, dtype=BF16):
    return jax.ShapeDtypeStruct(dims, dtype)


def list_tiles(count, slot_ref, number_ref, list_ref, local_cols, by_row):
    groups, cap = number_ref.shape[0], list_ref.shape[0] // number_ref.shape[0]
    blank = slot_ref.shape[0] * 1024
    bits = local_cols.bit_length() - 1

    def clear(g, _):
        number_ref[g] = 0
        for j in range(cap):
            list_ref[g * cap + j] = blank
        return 0

    lax.fori_loop(0, groups, clear, 0)

    def place(s, _):
        p = slot_ref[s]
        u, v = lax.shift_right_logical(p, bits), p & (local_cols - 1)
        g, other = (u, v) if by_row else (v, u)
        n = number_ref[g]
        list_ref[g * cap + n] = s * 1024 + other
        number_ref[g] = n + 1
        return 0

    lax.fori_loop(0, count, place, 0)


def repeat_lanes(scale, width):
    return jnp.concatenate([scale] * (width // scale.shape[-1]), 1)


def scale_body(degree, cot, scale, out):
    edge, lanes = scale.shape[1:]
    width = cot.shape[1]
    for i in range(scale.shape[0]):
        part = degree[i // 2 : i // 2 + 1, i % 2 * edge : (i % 2 + 1) * edge]
        line = 1.0 / jnp.sqrt(part.astype(F32))
        scale[i] = jnp.broadcast_to(line, (lanes, edge)).T
    row = lax.axis_index("row")
    for e in range(2):
        value = cot[e * edge : (e + 1) * edge, :].astype(F32)
        out[e] = (value * repeat_lanes(scale[row * 2 + e], width)).T.astype(BF16)


def scale_kernel(degree, cotangent, edge):
    return run(
        scale_body,
        (degree, cotangent),
        [VMEM] * 2,
        [shape((2 * degree.shape[0], edge, 128), F32), shape((2, cotangent.shape[1], edge))],
    )


def prepare_body(count_ref, slot_ref, values, scale, out, *lists):
    local_cols = values.shape[0]
    list_tiles(count_ref[0], slot_ref, lists[0], lists[1], local_cols, True)
    list_tiles(count_ref[0], slot_ref, lists[2], lists[3], local_cols, False)

    def fill(i, _):
        wide = repeat_lanes(scale[i], values.shape[-1])
        out[i] = (values[i].astype(F32) * wide).astype(BF16)
        return 0

    lax.fori_loop(0, local_cols, fill, 0)


def prepare(count, slots, values, scale, block_rows):
    local_cols = values.shape[0]
    sizes = (block_rows, block_rows * local_cols, local_cols, block_rows * local_cols)
    return run(
        prepare_body,
        (count, slots, values, scale),
        [SMEM] * 2 + [VMEM] * 2,
        [shape(values.shape)] + [shape((n,), jnp.int32) for n in sizes],
        out_specs=[VMEM] + [SMEM] * 4,
        mib=12,
    )


def sum_group(g, number_ref, list_ref, total, product, store):
    cap = list_ref.shape[0] // number_ref.shape[0]
    n = number_ref[g]

    def take(start, width):
        entries = [list_ref[g * cap + start + j] for j in range(width)]
        return product([(lax.shift_right_logical(x, 10), x & 1023) for x in entries])

    def exact(width):
        @pl.when(n == width)
        def _():
            store(take(0, width))

    @pl.when(n == 0)
    def _():
        store(jnp.zeros_like(total))

    for width in range(1, 5):
        exact(width)

    @pl.when(n > 4)
    def _():
        total[...] = jnp.zeros_like(total)
        fours = lax.shift_right_logical(n, 2)

        def four(m, _):
            total[...] += take(4 * m, 4)
            return 0

        def one(m, _):
            total[...] += take(m, 1)
            return 0

        lax.fori_loop(0, fours, four, 0)
        lax.fori_loop(4 * fours, n, one, 0)
        store(total[...])


def joined_dot(lhs, rhs):
    return jnp.dot(
        jnp.concatenate(lhs, 1), jnp.concatenate(rhs, 0), preferred_element_type=F32
    )


def forward_body(first, flip, number_ref, list_ref, tiles, source, out, total):
    col, row = lax.axis_index("col"), lax.axis_index("row")
    line = out.shape[0] // 2

    def product(pieces):
        def locate(v):
            return v if first else v ^ (2 * row)

        return joined_dot([tiles[s] for s, _ in pieces], [source[locate(v)] for _, v in pieces])

    for half in range(2):

        def block(i, _):
            def store(value):
                out[half * line + i] = value.astype(BF16)

            g = (col ^ (2 * i + flip)) * 2 + half
            sum_group(g, number_ref, list_ref, total, product, store)
            return 0

        lax.fori_loop(0, line, block, 0)


def forward(number, entries, tiles, source, first, flip, after=()):
    slots_n, edge, _ = tiles.shape
    width = source.shape[-1]
    return run(
        functools.partial(forward_body, first, flip),
        (number, entries, tiles, source),
        [SMEM, SMEM, VMEM, VMEM],
        [shape((number.shape[0] // 2, edge, width))],
        [pltpu.VMEM((edge, width), F32)],
        mib=16,
        after=after,
    )[0]


def backward_body(n, number_ref, list_ref, tiles, *refs):
    pieces_in, (out, ranged, total) = refs[:n], refs[n:]
    mask, flips = lax.axis_index("row") * 2, lax.axis_index("col") * 2
    for i, piece in enumerate(pieces_in):
        ranged[2 * i : 2 * i + 2] = piece[...]

    def product(pieces):
        return joined_dot([ranged[u ^ flips] for _, u in pieces], [tiles[s] for s, _ in pieces])

    def block(i, _):
        def store(value):
            out[i] = value.astype(BF16)

        sum_group(i ^ mask, number_ref, list_ref, total, product, store)
        return 0

    lax.fori_loop(0, out.shape[0], block, 0)


def backward(number, entries, tiles, pieces, after=()):
    slots_n, edge, _ = tiles.shape
    _, width, _ = pieces[0].shape
    n = len(pieces)
    return run(
        functools.partial(backward_body, n),
        (number, entries, tiles, *pieces),
        [SMEM, SMEM] + [VMEM] * (n + 1),
        [shape((number.shape[0], width, edge))],
        [pltpu.VMEM((2 * n, width, edge), BF16), pltpu.VMEM((width, edge), F32)],
        mib=20,
        after=after,
    )[0]


def pair_sum_body(n, keep, come, *outs):
    for j in range(n):
        for half in range(2):
            i = half * n + j
            outs[j][half] = (keep[i].astype(F32) + come[i].astype(F32)).astype(BF16)


def pair_sum(keep, come, after=()):
    n = keep.shape[0] // 2
    return run(
        functools.partial(pair_sum_body, n),
        (keep, come),
        [VMEM] * 2,
        [shape((2, *keep.shape[1:]))] * n,
        mib=12,
        after=after,
    )


def tree(items):
    while len(items) > 1:
        rest = items[len(items) // 2 * 2 :]
        items = [a + b for a, b in zip(items[::2], items[1::2])] + rest
    return items[0]


def relay_body(n, *refs):
    for source, out in zip(refs[:n], refs[n:]):
        out[...] = source[...]


def relay(items, after):
    return run(
        functools.partial(relay_body, len(items)),
        tuple(items),
        [VMEM] * len(items),
        [shape(x.shape) for x in items],
        after=after,
    )


def choose_body(at_ends, across, middle, out_two, out_three, two, three):
    position = lax.shift_right_logical(lax.axis_index("col"), 1)
    ends = jnp.logical_or(position == 0, position == at_ends)
    two[...] = jnp.where(ends, out_two[...], across[...])
    three[...] = jnp.where(ends, out_three[...], middle[...])


def choose(last, across, middle, out_two, out_three, after):
    return run(
        functools.partial(choose_body, last),
        (across, middle, out_two, out_three),
        [VMEM] * 4,
        [shape(across.shape)] * 2,
        after=after,
    )


def agg_body(n, *refs):
    scale, outs = refs[n], refs[n + 1 :]
    for half, out in enumerate(outs):
        summed = tree([x[half].astype(F32) for x in refs[:n]])
        wide = repeat_lanes(scale[lax.axis_index("row") * 2 + half], summed.shape[1])
        out[...] = (summed * wide).astype(BF16)


def aggregate(parts, scale, after):
    return run(
        functools.partial(agg_body, len(parts)),
        (*parts, scale),
        [VMEM] * (len(parts) + 1),
        [shape(parts[0].shape[1:])] * 2,
        after=after,
    )


def first_body(start, n, *refs):
    scale, weight, agg, out = refs[2 * n], refs[2 * n + 1], refs[-2], refs[-1]
    row = lax.axis_index("row")
    if start:
        agg[: 2 * start] = refs[2 * n + 2][...]
        out[: 2 * start] = refs[2 * n + 3][...]
    for i in range(2 * n):
        block = 2 * start + i
        value = jnp.dot(refs[i][...], weight[...], preferred_element_type=F32)
        wide = repeat_lanes(scale[block ^ (2 * row)], value.shape[1])
        out[block] = (jax.nn.gelu(value) * wide).astype(BF16)
        agg[block] = refs[i][...]


def first_layer(aggs, scale, weight, before=(), after=()):
    n = len(aggs)
    start = before[0].shape[0] // 2 if before else 0
    return run(
        functools.partial(first_body, start, n),
        (*[x for pair in aggs for x in pair], scale, weight, *before),
        [VMEM] * (2 * n + 2 + len(before)),
        [shape((2 * (start + n), *aggs[0][0].shape))] * 2,
        mib=14,
        after=after,
    )


def second_body(*refs):
    scale, weight, out = refs[-3:]
    edge = refs[0].shape[1]
    for half in range(2):
        summed = tree([x[half].astype(F32) for x in refs[:-3]])
        wide = repeat_lanes(scale[lax.axis_index("row") * 2 + half], summed.shape[1])
        agg = (summed * wide).astype(BF16)
        value = jnp.dot(agg, weight[...], preferred_element_type=F32)
        out[half * edge : (half + 1) * edge, :] = value.astype(BF16)


def second_layer(parts, scale, weight):
    halves, edge, width = parts[0].shape
    return run(
        second_body,
        (*parts, scale, weight),
        [VMEM] * (2 + len(parts)),
        [shape((halves * edge, width))],
    )[0]


def grad_body(start, last, hidden_ref, aggs, outs, scale, w_first, w_second, *refs):
    row = lax.axis_index("row")
    core = lax.rem(lax.axis_index("col"), 2)
    first, second = refs[-2:]
    if start:
        first[...] = refs[0][...]
        second[...] = refs[1][...]
    else:
        first[...] = jnp.zeros_like(first)
        second[...] = jnp.zeros_like(second)

    def block(i, _):
        hidden, agg = hidden_ref[i], aggs[i]
        pre = jnp.dot(agg, w_first[...], preferred_element_type=F32)
        grad_hidden = lax.dot_general(
            hidden, w_second[...], (((0,), (1,)), ((), ())), preferred_element_type=F32
        )
        _, pullback = jax.vjp(jax.nn.gelu, pre)
        wide = repeat_lanes(scale[i ^ (2 * row)], pre.shape[1])
        grad_pre = pullback(grad_hidden * wide)[0].astype(BF16)
        first[...] += lax.dot_general(
            agg, grad_pre, (((0,), (0,)), ((), ())), preferred_element_type=F32
        )
        second[...] += lax.dot_general(
            outs[i], hidden, (((0,), (1,)), ((), ())), preferred_element_type=F32
        )
        return 0

    lax.fori_loop(start, aggs.shape[0], block, 0)
    if last:
        give, keep = refs[2:4]
        keep[...] = jnp.where(core == 0, first[...], second[...]).astype(BF16)
        give[...] = jnp.where(core == 0, second[...], first[...]).astype(BF16)


def weight_grads(start, hidden, aggs, outs, scale, w_first, w_second, before=(), after=()):
    dims = w_first.shape
    last = aggs.shape[0] == hidden.shape[0]
    return run(
        functools.partial(grad_body, start, last),
        (hidden, aggs, outs, scale, w_first, w_second, *before),
        [VMEM] * (6 + len(before)),
        [shape(dims)] * 2 if last else [shape(dims, F32)] * 2,
        [pltpu.VMEM(dims, F32)] * 2 if last else [],
        mib=26,
        after=after,
    )


def position(axis):
    if axis == "row":
        return lax.axis_index("row")
    return lax.shift_right_logical(lax.axis_index("col"), 1)


def split_body(n, axis, *refs):
    ins, outs = refs[:-n], refs[-n:]
    rows = ins[0].shape[0] // n
    for j in range(n):
        part = pl.ds(pl.multiple_of((position(axis) ^ j) * rows, rows), rows)
        outs[j][...] = tree([x[part, :].astype(F32) for x in ins]).astype(BF16)


def split_sum(items, n, axis, after=()):
    rows, width = items[0].shape
    return run(
        functools.partial(split_body, n, axis),
        tuple(items),
        [VMEM] * len(items),
        [shape((rows // n, width))] * n,
        after=after,
    )


def sum_body(n, *refs):
    refs[n][...] = tree([x[...].astype(F32) for x in refs[:n]]).astype(BF16)


def sum_parts(parts, after=()):
    return run(
        functools.partial(sum_body, len(parts)),
        tuple(parts),
        [VMEM] * len(parts),
        [shape(parts[0].shape)],
        after=after,
    )[0]


def join_body(n, axis, *refs):
    rows = refs[0].shape[0]
    for j in range(n):
        part = pl.ds(pl.multiple_of((position(axis) ^ j) * rows, rows), rows)
        refs[n][part, :] = refs[j][...]


def join(parts, axis):
    rows, width = parts[0].shape
    return run(
        functools.partial(join_body, len(parts), axis),
        tuple(parts),
        [VMEM] * len(parts),
        [shape((rows * len(parts), width))],
    )[0]


def select_body(mine, other, first, second):
    core = lax.rem(lax.axis_index("col"), 2)
    first[...] = jnp.where(core == 0, mine[...].astype(F32), other[...].astype(F32))
    second[...] = jnp.where(core == 0, other[...].astype(F32), mine[...].astype(F32))


def select(mine, other, after):
    return run(
        select_body, (mine, other), [VMEM] * 2, [shape(mine.shape, F32)] * 2, after=after
    )


COST = {
    scale_body: 36,
    prepare_body: 36,
    forward_body: 36,
    grad_body: 36,
    second_body: 36,
}


def per_device(features, degree, tile_vals, tile_slot, tile_count, w_first, w_second, cotangent):
    n_row, n_col = lax.axis_size("row"), lax.axis_size("col")
    line = n_col // 2
    piece, width = cotangent.shape
    tiles = tile_vals[0, 0]
    edge = tiles.shape[-1]
    local_cols = n_row * 2
    slots, count = tile_slot[0, 0], tile_count[0]

    def col_send(value, pairs):
        return lax.ppermute(
            value, "col", [(2 * a + k, 2 * b + k) for a, b in pairs for k in range(2)]
        )

    def line_flip(value, j):
        return col_send(value, [(a, a ^ j) for a in range(line)])

    def core_flip(value):
        return lax.ppermute(value, "col", [(a, a ^ 1) for a in range(n_col)])

    def row_flip(value, j):
        return lax.ppermute(value, "row", [(a, a ^ j) for a in range(n_row)])

    def scatter_line(own, after=()):
        if line != 4:
            return [own[0]] + [line_flip(own[j], j) for j in range(1, line)], own[:2]
        to_three = col_send(own[3], [(0, 1), (3, 2)])
        to_two = col_send(own[2], [(0, 1), (3, 2)])
        crossing = sum_parts([own[2], to_three])
        meeting = sum_parts([own[3], to_two], (crossing, *after))
        crossed = col_send(crossing, [(1, 2), (2, 1)])
        met = col_send(meeting, [(1, 2), (2, 1)])
        outward = sum_parts([own[1], crossed])
        return [own[0], line_flip(outward, 1), met], (meeting, outward)

    def gather_row(pair):
        if n_row != 4:
            return [pair] + [[row_flip(x, j) for x in pair] for j in range(1, n_row)]
        x_first, y_second = row_flip(pair[0], 1), row_flip(pair[1], 2)
        x_second, y_first = row_flip(pair[1], 1), row_flip(pair[0], 2)
        diagonal = [row_flip(x_first, 2), row_flip(y_second, 1)]
        return [pair, [x_first, x_second], [y_first, y_second], diagonal]

    def gather_near(own):
        if line != 4:
            return []
        return [line_flip(own, 1), col_send(own, [(1, 2), (2, 1)])]

    def gather_far(own, near, middle, after, late):
        (across,) = relay([col_send(near, [(1, 2), (2, 1)])], after)
        out_two = col_send(middle, [(1, 0), (2, 3)])
        out_three = col_send(across, [(1, 0), (2, 3)])
        return [own, near, *choose(line - 1, across, middle, out_two, out_three, late)]

    halves = piece // edge
    scale, scaled = scale_kernel(degree[:, 0], cotangent, edge)
    early = gather_near(scaled)
    values = features[:, 0].reshape(local_cols, edge, width)
    first_in, number, entries, t_number, t_entries = prepare(
        count, slots, values, scale, 2 * n_col
    )

    give = forward(number, entries, tiles, first_in, True, 1)
    keep = forward(number, entries, tiles, first_in, True, 0)
    if early:
        early = relay(early, (give,))
    own = pair_sum(keep, core_flip(give))
    parts, late = scatter_line(own)
    if early:
        gathered = gather_far(scaled, *early, (own[0],), late)
    else:
        gathered = [scaled] + [line_flip(scaled, j) for j in range(1, line)]
    ranged = [x for g in gathered for x in (g, core_flip(g))]
    hidden = backward(t_number, t_entries, tiles, ranged)
    spread = gather_row(aggregate(parts, scale, (hidden,)))
    sums, stacked = (), ()
    for group in (spread[:1], spread[1:-1], spread[-1:]):
        start = stacked[0].shape[0] if stacked else 0
        stacked = first_layer(group, scale, w_first, stacked, sums[:1])
        sums = weight_grads(start, hidden, *stacked, scale, w_first, w_second, sums)

    give, keep = sums
    split = split_sum([keep, core_flip(give)], n_row, "row")
    moment = [split[0]] + [row_flip(split[j], j) for j in range(1, n_row)]
    give = forward(number, entries, tiles, stacked[1], False, 1, (keep,))
    keep = forward(number, entries, tiles, stacked[1], False, 0, (split[0],))
    if split[0].shape[0] % (16 * line) == 0:
        split = split_sum(moment, line, "line")
        moment = sum_parts([split[0]] + [line_flip(split[j], j) for j in range(1, line)])
        moment = join([moment] + [line_flip(moment, j) for j in range(1, line)], "line")
    else:
        split = [sum_parts(moment)]
        moment = sum_parts(split + [line_flip(split[0], j) for j in range(1, line)])
    own = pair_sum(keep, core_flip(give), split[:1])
    parts, _ = scatter_line(own, (moment,))
    moment = [moment] + [row_flip(moment, j) for j in range(1, n_row)]
    mine = join(moment, "row")
    logits = second_layer(parts, scale, w_second)
    return logits, *select(mine, core_flip(mine), (logits,))


def solution(mesh):
    return jax.shard_map(
        per_device,
        mesh=mesh,
        in_specs=(
            P(None, "col", None, None),
            P(None, "col", None),
            P("row", "col", None, None, None),
            P("row", "col", None),
            P("row", "col"),
            P(),
            P(),
            P(("row", "col"), None),
        ),
        out_specs=(P(("row", "col"), None), P(), P()),
        check_vma=False,
    )
```

```python
import functools

import jax
import jax.numpy as jnp
from jax import lax
from jax.experimental import pallas as pl
from jax.experimental.pallas import tpu as pltpu
from jax.sharding import PartitionSpec as P

F32 = jnp.float32
BF16 = jnp.bfloat16
MIB = 1024 * 1024
VMEM = pl.BlockSpec(memory_space=pltpu.VMEM)
SMEM = pl.BlockSpec(memory_space=pltpu.SMEM)
ANY = pl.BlockSpec(memory_space=pl.ANY)


def run(body, args, specs, outs, scratch=(), mib=8, after=(), out_specs=None):
    n, extra = len(args), len(after)

    def whole(*refs):
        body(*refs[:n], *refs[n + extra :])

    return pl.pallas_call(
        whole,
        out_shape=outs,
        in_specs=specs + [ANY] * extra,
        out_specs=out_specs or [VMEM] * len(outs),
        scratch_shapes=list(scratch),
        compiler_params=pltpu.CompilerParams(vmem_limit_bytes=mib * MIB),
        cost_estimate=pl.CostEstimate(
            flops=int(COST.get(getattr(body, "func", body), 0) * 1e9),
            bytes_accessed=0,
            transcendentals=0,
        ),
    )(*args, *after)


def shape(dims, dtype=BF16):
    return jax.ShapeDtypeStruct(dims, dtype)


def list_tiles(count, slot_ref, number_ref, list_ref, local_cols, by_row):
    groups, cap = number_ref.shape[0], list_ref.shape[0] // number_ref.shape[0]
    blank = slot_ref.shape[0] * 1024
    bits = local_cols.bit_length() - 1

    def clear(g, _):
        number_ref[g] = 0
        for j in range(cap):
            list_ref[g * cap + j] = blank
        return 0

    lax.fori_loop(0, groups, clear, 0)

    def place(s, _):
        p = slot_ref[s]
        u, v = lax.shift_right_logical(p, bits), p & (local_cols - 1)
        g, other = (u, v) if by_row else (v, u)
        n = number_ref[g]
        list_ref[g * cap + n] = s * 1024 + other
        number_ref[g] = n + 1
        return 0

    lax.fori_loop(0, count, place, 0)


def repeat_lanes(scale, width):
    return jnp.concatenate([scale] * (width // scale.shape[-1]), 1)


def scale_body(degree, cot, scale, out):
    edge, lanes = scale.shape[1:]
    width = cot.shape[1]
    for i in range(scale.shape[0]):
        part = degree[i // 2 : i // 2 + 1, i % 2 * edge : (i % 2 + 1) * edge]
        line = 1.0 / jnp.sqrt(part.astype(F32))
        scale[i] = jnp.broadcast_to(line, (lanes, edge)).T
    row = lax.axis_index("row")
    for e in range(2):
        value = cot[e * edge : (e + 1) * edge, :].astype(F32)
        out[e] = (value * repeat_lanes(scale[row * 2 + e], width)).T.astype(BF16)


def scale_kernel(degree, cotangent, edge):
    return run(
        scale_body,
        (degree, cotangent),
        [VMEM] * 2,
        [shape((2 * degree.shape[0], edge, 128), F32), shape((2, cotangent.shape[1], edge))],
    )


def prepare_body(count_ref, slot_ref, values, scale, out, *lists):
    local_cols = values.shape[0]
    list_tiles(count_ref[0], slot_ref, lists[0], lists[1], local_cols, True)
    list_tiles(count_ref[0], slot_ref, lists[2], lists[3], local_cols, False)

    def fill(i, _):
        wide = repeat_lanes(scale[i], values.shape[-1])
        out[i] = (values[i].astype(F32) * wide).astype(BF16)
        return 0

    lax.fori_loop(0, local_cols, fill, 0)


def prepare(count, slots, values, scale, block_rows):
    local_cols = values.shape[0]
    sizes = (block_rows, block_rows * local_cols, local_cols, block_rows * local_cols)
    return run(
        prepare_body,
        (count, slots, values, scale),
        [SMEM] * 2 + [VMEM] * 2,
        [shape(values.shape)] + [shape((n,), jnp.int32) for n in sizes],
        out_specs=[VMEM] + [SMEM] * 4,
        mib=12,
    )


def sum_group(g, number_ref, list_ref, total, product, store):
    cap = list_ref.shape[0] // number_ref.shape[0]
    n = number_ref[g]

    def take(start, width):
        entries = [list_ref[g * cap + start + j] for j in range(width)]
        return product([(lax.shift_right_logical(x, 10), x & 1023) for x in entries])

    def exact(width):
        @pl.when(n == width)
        def _():
            store(take(0, width))

    @pl.when(n == 0)
    def _():
        store(jnp.zeros_like(total))

    for width in range(1, 5):
        exact(width)

    @pl.when(n > 4)
    def _():
        total[...] = jnp.zeros_like(total)
        fours = lax.shift_right_logical(n, 2)

        def four(m, _):
            total[...] += take(4 * m, 4)
            return 0

        def one(m, _):
            total[...] += take(m, 1)
            return 0

        lax.fori_loop(0, fours, four, 0)
        lax.fori_loop(4 * fours, n, one, 0)
        store(total[...])


def joined_dot(lhs, rhs):
    return jnp.dot(
        jnp.concatenate(lhs, 1), jnp.concatenate(rhs, 0), preferred_element_type=F32
    )


def forward_body(first, flip, number_ref, list_ref, tiles, source, out, total):
    col, row = lax.axis_index("col"), lax.axis_index("row")
    line = out.shape[0] // 2

    def product(pieces):
        def locate(v):
            return v if first else v ^ (2 * row)

        return joined_dot([tiles[s] for s, _ in pieces], [source[locate(v)] for _, v in pieces])

    for half in range(2):

        def block(i, _):
            def store(value):
                out[half * line + i] = value.astype(BF16)

            g = (col ^ (2 * i + flip)) * 2 + half
            sum_group(g, number_ref, list_ref, total, product, store)
            return 0

        lax.fori_loop(0, line, block, 0)


def forward(number, entries, tiles, source, first, flip, after=()):
    slots_n, edge, _ = tiles.shape
    width = source.shape[-1]
    return run(
        functools.partial(forward_body, first, flip),
        (number, entries, tiles, source),
        [SMEM, SMEM, VMEM, VMEM],
        [shape((number.shape[0] // 2, edge, width))],
        [pltpu.VMEM((edge, width), F32)],
        mib=16,
        after=after,
    )[0]


def backward_body(n, number_ref, list_ref, tiles, *refs):
    pieces_in, (out, ranged, total) = refs[:n], refs[n:]
    mask, flips = lax.axis_index("row") * 2, lax.axis_index("col") * 2
    blocks, start = ranged.shape[0], 0
    for piece in pieces_in:
        ranged[start : start + piece.shape[0]] = piece[...]
        start += piece.shape[0]

    def product(pieces):
        def locate(u):
            x = u ^ flips
            return (x & 2) * (blocks // 4) + lax.shift_right_logical(x, 2) * 2 + (x & 1)

        return joined_dot([ranged[locate(u)] for _, u in pieces], [tiles[s] for s, _ in pieces])

    def block(i, _):
        def store(value):
            out[i] = value.astype(BF16)

        sum_group(i ^ mask, number_ref, list_ref, total, product, store)
        return 0

    lax.fori_loop(0, out.shape[0], block, 0)


def backward(number, entries, tiles, pieces, after=()):
    slots_n, edge, _ = tiles.shape
    _, width, _ = pieces[0].shape
    n, blocks = len(pieces), sum(x.shape[0] for x in pieces)
    return run(
        functools.partial(backward_body, n),
        (number, entries, tiles, *pieces),
        [SMEM, SMEM] + [VMEM] * (n + 1),
        [shape((number.shape[0], width, edge))],
        [pltpu.VMEM((blocks, width, edge), BF16), pltpu.VMEM((width, edge), F32)],
        mib=20,
        after=after,
    )[0]


def pair_sum_body(n, keep, come, *outs):
    for j in range(n):
        for half in range(2):
            i = half * n + j
            outs[j][half] = (keep[i].astype(F32) + come[i].astype(F32)).astype(BF16)


def pair_sum(keep, come, after=()):
    n = keep.shape[0] // 2
    return run(
        functools.partial(pair_sum_body, n),
        (keep, come),
        [VMEM] * 2,
        [shape((2, *keep.shape[1:]))] * n,
        mib=12,
        after=after,
    )


def tree(items):
    while len(items) > 1:
        rest = items[len(items) // 2 * 2 :]
        items = [a + b for a, b in zip(items[::2], items[1::2])] + rest
    return items[0]


def relay_body(n, *refs):
    for source, out in zip(refs[:n], refs[n:]):
        out[...] = source[...]


def relay(items, after):
    return run(
        functools.partial(relay_body, len(items)),
        tuple(items),
        [VMEM] * len(items),
        [shape(x.shape) for x in items],
        after=after,
    )


def choose_body(last, across, middle, out_two, out_three, *outs):
    ends = jnp.logical_or(position("col") == 0, position("col") == last)
    for half in range(2):
        outs[half][0] = jnp.where(ends, out_two[half], across[half])
        outs[2 + half][0] = jnp.where(ends, out_three[half], middle[half])


def choose(last, across, middle, out_two, out_three, after):
    return run(
        functools.partial(choose_body, last),
        (across, middle, out_two, out_three),
        [VMEM] * 4,
        [shape((1, *across.shape[1:]))] * 4,
        after=after,
    )


def agg_body(n, *refs):
    scale, outs = refs[n], refs[n + 1 :]
    for half, out in enumerate(outs):
        summed = tree([x[half].astype(F32) for x in refs[:n]])
        wide = repeat_lanes(scale[lax.axis_index("row") * 2 + half], summed.shape[1])
        out[...] = (summed * wide).astype(BF16)


def aggregate(parts, scale, after):
    return run(
        functools.partial(agg_body, len(parts)),
        (*parts, scale),
        [VMEM] * (len(parts) + 1),
        [shape(parts[0].shape[1:])] * 2,
        after=after,
    )


def first_body(start, n, *refs):
    scale, weight, agg, out = refs[2 * n], refs[2 * n + 1], refs[-2], refs[-1]
    row = lax.axis_index("row")
    if start:
        agg[: 2 * start] = refs[2 * n + 2][...]
        out[: 2 * start] = refs[2 * n + 3][...]
    for i in range(2 * n):
        block = 2 * start + i
        value = jnp.dot(refs[i][...], weight[...], preferred_element_type=F32)
        wide = repeat_lanes(scale[block ^ (2 * row)], value.shape[1])
        out[block] = (jax.nn.gelu(value) * wide).astype(BF16)
        agg[block] = refs[i][...]


def first_layer(aggs, scale, weight, before=(), after=()):
    n = len(aggs)
    start = before[0].shape[0] // 2 if before else 0
    return run(
        functools.partial(first_body, start, n),
        (*[x for pair in aggs for x in pair], scale, weight, *before),
        [VMEM] * (2 * n + 2 + len(before)),
        [shape((2 * (start + n), *aggs[0][0].shape))] * 2,
        mib=14,
        after=after,
    )


def second_body(*refs):
    scale, weight, out = refs[-3:]
    edge = refs[0].shape[1]
    for half in range(2):
        summed = tree([x[half].astype(F32) for x in refs[:-3]])
        wide = repeat_lanes(scale[lax.axis_index("row") * 2 + half], summed.shape[1])
        agg = (summed * wide).astype(BF16)
        value = jnp.dot(agg, weight[...], preferred_element_type=F32)
        out[half * edge : (half + 1) * edge, :] = value.astype(BF16)


def second_layer(parts, scale, weight):
    halves, edge, width = parts[0].shape
    return run(
        second_body,
        (*parts, scale, weight),
        [VMEM] * (2 + len(parts)),
        [shape((halves * edge, width))],
    )[0]


def grad_body(start, last, hidden_ref, aggs, outs, scale, w_first, w_second, *refs):
    row = lax.axis_index("row")
    core = lax.rem(lax.axis_index("col"), 2)
    first, second = refs[-2:]
    if start:
        first[...] = refs[0][...]
        second[...] = refs[1][...]
    else:
        first[...] = jnp.zeros_like(first)
        second[...] = jnp.zeros_like(second)

    def block(i, _):
        hidden, agg = hidden_ref[i], aggs[i]
        pre = jnp.dot(agg, w_first[...], preferred_element_type=F32)
        grad_hidden = lax.dot_general(
            hidden, w_second[...], (((0,), (1,)), ((), ())), preferred_element_type=F32
        )
        _, pullback = jax.vjp(jax.nn.gelu, pre)
        wide = repeat_lanes(scale[i ^ (2 * row)], pre.shape[1])
        grad_pre = pullback(grad_hidden * wide)[0].astype(BF16)
        first[...] += lax.dot_general(
            agg, grad_pre, (((0,), (0,)), ((), ())), preferred_element_type=F32
        )
        second[...] += lax.dot_general(
            outs[i], hidden, (((0,), (1,)), ((), ())), preferred_element_type=F32
        )
        return 0

    lax.fori_loop(start, aggs.shape[0], block, 0)
    if last:
        give, keep = refs[2:4]
        keep[...] = jnp.where(core == 0, first[...], second[...]).astype(BF16)
        give[...] = jnp.where(core == 0, second[...], first[...]).astype(BF16)


def weight_grads(start, hidden, aggs, outs, scale, w_first, w_second, before=(), after=()):
    dims = w_first.shape
    last = aggs.shape[0] == hidden.shape[0]
    return run(
        functools.partial(grad_body, start, last),
        (hidden, aggs, outs, scale, w_first, w_second, *before),
        [VMEM] * (6 + len(before)),
        [shape(dims)] * 2 if last else [shape(dims, F32)] * 2,
        [pltpu.VMEM(dims, F32)] * 2 if last else [],
        mib=26,
        after=after,
    )


def position(axis):
    if axis == "row":
        return lax.axis_index("row")
    return lax.shift_right_logical(lax.axis_index("col"), 1)


def split_body(n, axis, *refs):
    ins, outs = refs[:-n], refs[-n:]
    rows = ins[0].shape[0] // n
    for j in range(n):
        part = pl.ds(pl.multiple_of((position(axis) ^ j) * rows, rows), rows)
        outs[j][...] = tree([x[part, :].astype(F32) for x in ins]).astype(BF16)


def split_sum(items, n, axis, after=()):
    rows, width = items[0].shape
    return run(
        functools.partial(split_body, n, axis),
        tuple(items),
        [VMEM] * len(items),
        [shape((rows // n, width))] * n,
        after=after,
    )


def sum_body(n, *refs):
    refs[n][...] = tree([x[...].astype(F32) for x in refs[:n]]).astype(BF16)


def sum_parts(parts, after=()):
    return run(
        functools.partial(sum_body, len(parts)),
        tuple(parts),
        [VMEM] * len(parts),
        [shape(parts[0].shape)],
        after=after,
    )[0]


def join_body(n, axis, *refs):
    rows = refs[0].shape[0]
    for j in range(n):
        part = pl.ds(pl.multiple_of((position(axis) ^ j) * rows, rows), rows)
        refs[n][part, :] = refs[j][...]


def join(parts, axis):
    rows, width = parts[0].shape
    return run(
        functools.partial(join_body, len(parts), axis),
        tuple(parts),
        [VMEM] * len(parts),
        [shape((rows * len(parts), width))],
    )[0]


def select_body(mine, other, first, second):
    core = lax.rem(lax.axis_index("col"), 2)
    first[...] = jnp.where(core == 0, mine[...].astype(F32), other[...].astype(F32))
    second[...] = jnp.where(core == 0, other[...].astype(F32), mine[...].astype(F32))


def select(mine, other, after):
    return run(
        select_body, (mine, other), [VMEM] * 2, [shape(mine.shape, F32)] * 2, after=after
    )


COST = {
    scale_body: 36,
    prepare_body: 36,
    forward_body: 36,
    grad_body: 36,
    second_body: 36,
}


def per_device(features, degree, tile_vals, tile_slot, tile_count, w_first, w_second, cotangent):
    n_row, n_col = lax.axis_size("row"), lax.axis_size("col")
    line = n_col // 2
    piece, width = cotangent.shape
    tiles = tile_vals[0, 0]
    edge = tiles.shape[-1]
    local_cols = n_row * 2
    slots, count = tile_slot[0, 0], tile_count[0]

    def col_send(value, pairs):
        return lax.ppermute(
            value, "col", [(2 * a + k, 2 * b + k) for a, b in pairs for k in range(2)]
        )

    def line_flip(value, j):
        return col_send(value, [(a, a ^ j) for a in range(line)])

    def core_flip(value):
        return lax.ppermute(value, "col", [(a, a ^ 1) for a in range(n_col)])

    def row_flip(value, j):
        return lax.ppermute(value, "row", [(a, a ^ j) for a in range(n_row)])

    def scatter_line(own, behind):
        if line != 4:
            return [own[0]] + [line_flip(own[j], j) for j in range(1, line)], own[:2]
        to_three = col_send(own[3], [(0, 1), (3, 2)])
        to_two = col_send(behind, [(0, 1), (3, 2)])
        crossing = sum_parts([behind, to_three])
        meeting = sum_parts([own[3], to_two], (crossing,))
        crossed = col_send(crossing, [(1, 2), (2, 1)])
        met = col_send(meeting, [(1, 2), (2, 1)])
        outward = sum_parts([own[1], crossed])
        return [own[0], line_flip(outward, 1), met], (meeting, outward)

    def gather_row(pair, behind):
        if n_row != 4:
            return [pair] + [[row_flip(x, j) for x in pair] for j in range(1, n_row)]
        x_first, y_second = row_flip(pair[0], 1), row_flip(pair[1], 2)
        x_second, y_first = row_flip(behind[1], 1), row_flip(behind[0], 2)
        diagonal = [row_flip(x_first, 2), row_flip(y_second, 1)]
        return [pair, [x_first, x_second], [y_first, y_second], diagonal]

    def gather_near(own):
        if line != 4:
            return []
        return [line_flip(own, 1), col_send(own, [(1, 2), (2, 1)])]

    def gather_far(own, near, middle, after, late):
        (across,) = relay([col_send(near, [(1, 2), (2, 1)])], after)
        out_two = col_send(middle, [(1, 0), (2, 3)])
        out_three = col_send(across, [(1, 0), (2, 3)])
        return [own, near, *choose(line - 1, across, middle, out_two, out_three, late)]

    halves = piece // edge
    scale, scaled = scale_kernel(degree[:, 0], cotangent, edge)
    early = gather_near(scaled)
    values = features[:, 0].reshape(local_cols, edge, width)
    first_in, number, entries, t_number, t_entries = prepare(
        count, slots, values, scale, 2 * n_col
    )

    give = forward(number, entries, tiles, first_in, True, 1)
    keep = forward(number, entries, tiles, first_in, True, 0)
    if early:
        early = relay(early, (give,))
    own = pair_sum(keep, core_flip(give))
    parts, late = scatter_line(own, own[2])
    if early:
        gathered = gather_far(scaled, *early, (own[0],), late)
    else:
        gathered = [scaled] + [line_flip(scaled, j) for j in range(1, line)]
    ranged = gathered + [core_flip(g) for g in gathered]
    hidden = backward(t_number, t_entries, tiles, ranged)
    pair = aggregate(parts, scale, (hidden,))
    stacked = first_layer([pair], scale, w_first)
    spread = gather_row(pair, relay(pair, stacked[:1]))
    sums = weight_grads(0, hidden, *stacked, scale, w_first, w_second)
    for group in (spread[1:-1], spread[-1:]):
        start = stacked[0].shape[0]
        stacked = first_layer(group, scale, w_first, stacked, sums[:1])
        sums = weight_grads(start, hidden, *stacked, scale, w_first, w_second, sums)

    grad_give, grad_keep = sums
    give = forward(number, entries, tiles, stacked[1], False, 1, (grad_keep,))
    keep = forward(number, entries, tiles, stacked[1], False, 0)
    own = pair_sum(keep, core_flip(give))
    split = split_sum([grad_keep, core_flip(grad_give)], n_row, "row", own[:1])
    moment = [split[0]] + [row_flip(split[j], j) for j in range(1, n_row)]
    if split[0].shape[0] % (16 * line) == 0:
        split = split_sum(moment, line, "line")
        moment = sum_parts([split[0]] + [line_flip(split[j], j) for j in range(1, line)])
        moment = join([moment] + [line_flip(moment, j) for j in range(1, line)], "line")
    else:
        moment = sum_parts(moment)
        moment = sum_parts([moment] + [line_flip(moment, j) for j in range(1, line)])
    (behind,) = relay(own[2:3], (moment,))
    moment = [moment] + [row_flip(moment, j) for j in range(1, n_row)]
    mine = join(moment, "row")
    parts, _ = scatter_line(own, behind)
    logits = second_layer(parts, scale, w_second)
    return logits, *select(mine, core_flip(mine), (logits,))


def solution(mesh):
    return jax.shard_map(
        per_device,
        mesh=mesh,
        in_specs=(
            P(None, "col", None, None),
            P(None, "col", None),
            P("row", "col", None, None, None),
            P("row", "col", None),
            P("row", "col"),
            P(),
            P(),
            P(("row", "col"), None),
        ),
        out_specs=(P(("row", "col"), None), P(), P()),
        check_vma=False,
    )
```

```python
import functools

import jax
import jax.numpy as jnp
from jax import lax
from jax.experimental import pallas as pl
from jax.experimental.pallas import tpu as pltpu
from jax.sharding import PartitionSpec as P

F32 = jnp.float32
BF16 = jnp.bfloat16
MIB = 1024 * 1024
VMEM = pl.BlockSpec(memory_space=pltpu.VMEM)
SMEM = pl.BlockSpec(memory_space=pltpu.SMEM)
ANY = pl.BlockSpec(memory_space=pl.ANY)


def run(body, args, specs, outs, scratch=(), mib=8, after=(), out_specs=None, cost=None):
    n, extra = len(args), len(after)
    cost = COST.get(getattr(body, "func", body), 0) if cost is None else cost

    def whole(*refs):
        body(*refs[:n], *refs[n + extra :])

    return pl.pallas_call(
        whole,
        out_shape=outs,
        in_specs=specs + [ANY] * extra,
        out_specs=out_specs or [VMEM] * len(outs),
        scratch_shapes=list(scratch),
        compiler_params=pltpu.CompilerParams(vmem_limit_bytes=mib * MIB),
        cost_estimate=pl.CostEstimate(
            flops=int(cost * 1e9),
            bytes_accessed=0,
            transcendentals=0,
        ),
    )(*args, *after)


def shape(dims, dtype=BF16):
    return jax.ShapeDtypeStruct(dims, dtype)


def list_tiles(count, slot_ref, number_ref, list_ref, local_cols, by_row):
    groups, cap = number_ref.shape[0], list_ref.shape[0] // number_ref.shape[0]
    blank = slot_ref.shape[0] * 1024
    bits = local_cols.bit_length() - 1

    def clear(g, _):
        number_ref[g] = 0
        for j in range(cap):
            list_ref[g * cap + j] = blank
        return 0

    lax.fori_loop(0, groups, clear, 0)

    def place(s, _):
        p = slot_ref[s]
        u, v = lax.shift_right_logical(p, bits), p & (local_cols - 1)
        g, other = (u, v) if by_row else (v, u)
        n = number_ref[g]
        list_ref[g * cap + n] = s * 1024 + other
        number_ref[g] = n + 1
        return 0

    lax.fori_loop(0, count, place, 0)


def repeat_lanes(scale, width):
    return jnp.concatenate([scale] * (width // scale.shape[-1]), 1)


def scale_body(degree, cot, scale, out):
    edge, lanes = scale.shape[1:]
    width = cot.shape[1]
    for i in range(scale.shape[0]):
        part = degree[i // 2 : i // 2 + 1, i % 2 * edge : (i % 2 + 1) * edge]
        line = 1.0 / jnp.sqrt(part.astype(F32))
        scale[i] = jnp.broadcast_to(line, (lanes, edge)).T
    row = lax.axis_index("row")
    for e in range(2):
        value = cot[e * edge : (e + 1) * edge, :].astype(F32)
        out[e] = (value * repeat_lanes(scale[row * 2 + e], width)).T.astype(BF16)


def scale_kernel(degree, cotangent, edge):
    return run(
        scale_body,
        (degree, cotangent),
        [VMEM] * 2,
        [shape((2 * degree.shape[0], edge, 128), F32), shape((2, cotangent.shape[1], edge))],
    )


def prepare_body(count_ref, slot_ref, values, scale, out, *lists):
    local_cols = values.shape[0]
    list_tiles(count_ref[0], slot_ref, lists[0], lists[1], local_cols, True)
    list_tiles(count_ref[0], slot_ref, lists[2], lists[3], local_cols, False)

    def fill(i, _):
        wide = repeat_lanes(scale[i], values.shape[-1])
        out[i] = (values[i].astype(F32) * wide).astype(BF16)
        return 0

    lax.fori_loop(0, local_cols, fill, 0)


def prepare(count, slots, values, scale, block_rows):
    local_cols = values.shape[0]
    sizes = (block_rows, block_rows * local_cols, local_cols, block_rows * local_cols)
    return run(
        prepare_body,
        (count, slots, values, scale),
        [SMEM] * 2 + [VMEM] * 2,
        [shape(values.shape)] + [shape((n,), jnp.int32) for n in sizes],
        out_specs=[VMEM] + [SMEM] * 4,
        mib=12,
    )


def sum_group(g, number_ref, list_ref, total, product, store):
    cap = list_ref.shape[0] // number_ref.shape[0]
    n = number_ref[g]

    def take(start, width):
        entries = [list_ref[g * cap + start + j] for j in range(width)]
        return product([(lax.shift_right_logical(x, 10), x & 1023) for x in entries])

    def exact(width):
        @pl.when(n == width)
        def _():
            store(take(0, width))

    @pl.when(n == 0)
    def _():
        store(jnp.zeros_like(total))

    for width in range(1, 5):
        exact(width)

    @pl.when(n > 4)
    def _():
        total[...] = jnp.zeros_like(total)
        fours = lax.shift_right_logical(n, 2)

        def four(m, _):
            total[...] += take(4 * m, 4)
            return 0

        def one(m, _):
            total[...] += take(m, 1)
            return 0

        lax.fori_loop(0, fours, four, 0)
        lax.fori_loop(4 * fours, n, one, 0)
        store(total[...])


def joined_dot(lhs, rhs):
    return jnp.dot(
        jnp.concatenate(lhs, 1), jnp.concatenate(rhs, 0), preferred_element_type=F32
    )


def forward_body(first, flip, parts, number_ref, list_ref, tiles, source, out, total):
    col, row = lax.axis_index("col"), lax.axis_index("row")
    n = out.shape[0] // (2 * len(parts))

    def product(pieces):
        def locate(v):
            return v if first else v ^ (2 * row)

        return joined_dot([tiles[s] for s, _ in pieces], [source[locate(v)] for _, v in pieces])

    for place, part in enumerate(parts):
        for half in range(2):

            def block(i, _):
                def store(value):
                    out[(2 * place + half) * n + i] = value.astype(BF16)

                g = (col ^ (2 * (part * n + i) + flip)) * 2 + half
                sum_group(g, number_ref, list_ref, total, product, store)
                return 0

            lax.fori_loop(0, n, block, 0)


def forward(number, entries, tiles, source, first, flip, parts, after=()):
    edge, width = tiles.shape[-1], source.shape[-1]
    return run(
        functools.partial(forward_body, first, flip, parts),
        (number, entries, tiles, source),
        [SMEM, SMEM, VMEM, VMEM],
        [shape((len(parts) * number.shape[0] // 4, edge, width))],
        [pltpu.VMEM((edge, width), F32)],
        mib=16,
        after=after,
        cost=36 if parts == (0,) else 20,
    )[0]


def backward_body(n, number_ref, list_ref, tiles, *refs):
    pieces_in, (out, ranged, total) = refs[:n], refs[n:]
    mask, flips = lax.axis_index("row") * 2, lax.axis_index("col") * 2
    blocks, start = ranged.shape[0], 0
    for piece in pieces_in:
        ranged[start : start + piece.shape[0]] = piece[...]
        start += piece.shape[0]

    def product(pieces):
        def locate(u):
            x = u ^ flips
            return (x & 2) * (blocks // 4) + lax.shift_right_logical(x, 2) * 2 + (x & 1)

        return joined_dot([ranged[locate(u)] for _, u in pieces], [tiles[s] for s, _ in pieces])

    def block(i, _):
        def store(value):
            out[i] = value.astype(BF16)

        sum_group(i ^ mask, number_ref, list_ref, total, product, store)
        return 0

    lax.fori_loop(0, out.shape[0], block, 0)


def backward(number, entries, tiles, pieces, after=()):
    slots_n, edge, _ = tiles.shape
    _, width, _ = pieces[0].shape
    n, blocks = len(pieces), sum(x.shape[0] for x in pieces)
    return run(
        functools.partial(backward_body, n),
        (number, entries, tiles, *pieces),
        [SMEM, SMEM] + [VMEM] * (n + 1),
        [shape((number.shape[0], width, edge))],
        [pltpu.VMEM((blocks, width, edge), BF16), pltpu.VMEM((width, edge), F32)],
        mib=20,
        after=after,
    )[0]


def pair_sum_body(start, n, keep, come, *outs):
    for j in range(n):
        for half in range(2):
            i = half * n + j
            outs[j][half] = (keep[i].astype(F32) + come[start + i].astype(F32)).astype(BF16)


def pair_sum(keep, come, start):
    n = keep.shape[0] // 2
    return run(
        functools.partial(pair_sum_body, start, n),
        (keep, come),
        [VMEM] * 2,
        [shape((2, *keep.shape[1:]))] * n,
        mib=12,
    )


def tree(items):
    while len(items) > 1:
        rest = items[len(items) // 2 * 2 :]
        items = [a + b for a, b in zip(items[::2], items[1::2])] + rest
    return items[0]


def relay_body(n, *refs):
    for source, out in zip(refs[:n], refs[n:]):
        out[...] = source[...]


def relay(items, after):
    return run(
        functools.partial(relay_body, len(items)),
        tuple(items),
        [VMEM] * len(items),
        [shape(x.shape) for x in items],
        after=after,
    )


def choose_body(last, across, middle, out_two, out_three, *outs):
    ends = jnp.logical_or(position("col") == 0, position("col") == last)
    for half in range(2):
        outs[half][0] = jnp.where(ends, out_two[half], across[half])
        outs[2 + half][0] = jnp.where(ends, out_three[half], middle[half])


def choose(last, across, middle, out_two, out_three, after):
    return run(
        functools.partial(choose_body, last),
        (across, middle, out_two, out_three),
        [VMEM] * 4,
        [shape((1, *across.shape[1:]))] * 4,
        after=after,
    )


def agg_body(n, *refs):
    scale, outs = refs[n], refs[n + 1 :]
    for half, out in enumerate(outs):
        summed = tree([x[half].astype(F32) for x in refs[:n]])
        wide = repeat_lanes(scale[lax.axis_index("row") * 2 + half], summed.shape[1])
        out[...] = (summed * wide).astype(BF16)


def aggregate(parts, scale, after):
    return run(
        functools.partial(agg_body, len(parts)),
        (*parts, scale),
        [VMEM] * (len(parts) + 1),
        [shape(parts[0].shape[1:])] * 2,
        after=after,
    )


def first_body(start, n, *refs):
    scale, weight, agg, out = refs[2 * n], refs[2 * n + 1], refs[-2], refs[-1]
    row = lax.axis_index("row")
    if start:
        agg[: 2 * start] = refs[2 * n + 2][...]
        out[: 2 * start] = refs[2 * n + 3][...]
    for i in range(2 * n):
        block = 2 * start + i
        value = jnp.dot(refs[i][...], weight[...], preferred_element_type=F32)
        wide = repeat_lanes(scale[block ^ (2 * row)], value.shape[1])
        out[block] = (jax.nn.gelu(value) * wide).astype(BF16)
        agg[block] = refs[i][...]


def first_layer(aggs, scale, weight, before=(), after=()):
    n = len(aggs)
    start = before[0].shape[0] // 2 if before else 0
    return run(
        functools.partial(first_body, start, n),
        (*[x for pair in aggs for x in pair], scale, weight, *before),
        [VMEM] * (2 * n + 2 + len(before)),
        [shape((2 * (start + n), *aggs[0][0].shape))] * 2,
        mib=14,
        after=after,
    )


def second_body(*refs):
    scale, weight, out = refs[-3:]
    edge = refs[0].shape[1]
    for half in range(2):
        summed = tree([x[half].astype(F32) for x in refs[:-3]])
        wide = repeat_lanes(scale[lax.axis_index("row") * 2 + half], summed.shape[1])
        agg = (summed * wide).astype(BF16)
        value = jnp.dot(agg, weight[...], preferred_element_type=F32)
        out[half * edge : (half + 1) * edge, :] = value.astype(BF16)


def second_layer(parts, scale, weight):
    halves, edge, width = parts[0].shape
    return run(
        second_body,
        (*parts, scale, weight),
        [VMEM] * (2 + len(parts)),
        [shape((halves * edge, width))],
    )[0]


def grad_body(start, last, hidden_ref, aggs, outs, scale, w_first, w_second, *refs):
    row = lax.axis_index("row")
    core = lax.rem(lax.axis_index("col"), 2)
    first, second = refs[-2:]
    if start:
        first[...] = refs[0][...]
        second[...] = refs[1][...]
    else:
        first[...] = jnp.zeros_like(first)
        second[...] = jnp.zeros_like(second)

    def block(i, _):
        hidden, agg = hidden_ref[i], aggs[i]
        pre = jnp.dot(agg, w_first[...], preferred_element_type=F32)
        grad_hidden = lax.dot_general(
            hidden, w_second[...], (((0,), (1,)), ((), ())), preferred_element_type=F32
        )
        _, pullback = jax.vjp(jax.nn.gelu, pre)
        wide = repeat_lanes(scale[i ^ (2 * row)], pre.shape[1])
        grad_pre = pullback(grad_hidden * wide)[0].astype(BF16)
        first[...] += lax.dot_general(
            agg, grad_pre, (((0,), (0,)), ((), ())), preferred_element_type=F32
        )
        second[...] += lax.dot_general(
            outs[i], hidden, (((0,), (1,)), ((), ())), preferred_element_type=F32
        )
        return 0

    lax.fori_loop(start, aggs.shape[0], block, 0)
    if last:
        give, keep = refs[2:4]
        keep[...] = jnp.where(core == 0, first[...], second[...]).astype(BF16)
        give[...] = jnp.where(core == 0, second[...], first[...]).astype(BF16)


def weight_grads(start, hidden, aggs, outs, scale, w_first, w_second, before=(), after=()):
    dims = w_first.shape
    last = aggs.shape[0] == hidden.shape[0]
    return run(
        functools.partial(grad_body, start, last),
        (hidden, aggs, outs, scale, w_first, w_second, *before),
        [VMEM] * (6 + len(before)),
        [shape(dims)] * 2 if last else [shape(dims, F32)] * 2,
        [pltpu.VMEM(dims, F32)] * 2 if last else [],
        mib=26,
        after=after,
    )


def position(axis):
    if axis == "row":
        return lax.axis_index("row")
    return lax.shift_right_logical(lax.axis_index("col"), 1)


def split_body(n, axis, *refs):
    ins, outs = refs[:-n], refs[-n:]
    rows = ins[0].shape[0] // n
    for j in range(n):
        part = pl.ds(pl.multiple_of((position(axis) ^ j) * rows, rows), rows)
        outs[j][...] = tree([x[part, :].astype(F32) for x in ins]).astype(BF16)


def split_sum(items, n, axis, after=()):
    rows, width = items[0].shape
    return run(
        functools.partial(split_body, n, axis),
        tuple(items),
        [VMEM] * len(items),
        [shape((rows // n, width))] * n,
        after=after,
    )


def sum_body(n, *refs):
    refs[n][...] = tree([x[...].astype(F32) for x in refs[:n]]).astype(BF16)


def sum_parts(parts, after=()):
    return run(
        functools.partial(sum_body, len(parts)),
        tuple(parts),
        [VMEM] * len(parts),
        [shape(parts[0].shape)],
        after=after,
    )[0]


def join_body(n, axis, *refs):
    rows = refs[0].shape[0]
    for j in range(n):
        part = pl.ds(pl.multiple_of((position(axis) ^ j) * rows, rows), rows)
        refs[n][part, :] = refs[j][...]


def join(parts, axis):
    rows, width = parts[0].shape
    return run(
        functools.partial(join_body, len(parts), axis),
        tuple(parts),
        [VMEM] * len(parts),
        [shape((rows * len(parts), width))],
    )[0]


def select_body(mine, other, first, second):
    core = lax.rem(lax.axis_index("col"), 2)
    first[...] = jnp.where(core == 0, mine[...].astype(F32), other[...].astype(F32))
    second[...] = jnp.where(core == 0, other[...].astype(F32), mine[...].astype(F32))


def select(mine, other, after):
    return run(
        select_body, (mine, other), [VMEM] * 2, [shape(mine.shape, F32)] * 2, after=after
    )


COST = {
    scale_body: 36,
    prepare_body: 36,
    grad_body: 36,
    second_body: 36,
}


def per_device(features, degree, tile_vals, tile_slot, tile_count, w_first, w_second, cotangent):
    n_row, n_col = lax.axis_size("row"), lax.axis_size("col")
    line = n_col // 2
    piece, width = cotangent.shape
    tiles = tile_vals[0, 0]
    edge = tiles.shape[-1]
    local_cols = n_row * 2
    slots, count = tile_slot[0, 0], tile_count[0]

    def col_send(value, pairs):
        return lax.ppermute(
            value, "col", [(2 * a + k, 2 * b + k) for a, b in pairs for k in range(2)]
        )

    def line_flip(value, j):
        return col_send(value, [(a, a ^ j) for a in range(line)])

    def core_flip(value):
        return lax.ppermute(value, "col", [(a, a ^ 1) for a in range(n_col)])

    def row_flip(value, j):
        return lax.ppermute(value, "row", [(a, a ^ j) for a in range(n_row)])

    def scatter_line(own, behind, after=()):
        if line != 4:
            return [own[0]] + [line_flip(own[j], j) for j in range(1, line)], own[:2]
        to_three = col_send(own[3], [(0, 1), (3, 2)])
        to_two = col_send(behind, [(0, 1), (3, 2)])
        crossing = sum_parts([behind, to_three], own[:1])
        meeting = sum_parts([own[3], to_two], (crossing, *after))
        crossed = col_send(crossing, [(1, 2), (2, 1)])
        met = col_send(meeting, [(1, 2), (2, 1)])
        outward = sum_parts([own[1], crossed])
        return [own[0], line_flip(outward, 1), met], (meeting, outward)

    def gather_row(pair, behind):
        if n_row != 4:
            return [pair] + [[row_flip(x, j) for x in pair] for j in range(1, n_row)]
        x_first, y_second = row_flip(pair[0], 1), row_flip(pair[1], 2)
        x_second, y_first = row_flip(behind[1], 1), row_flip(behind[0], 2)
        diagonal = [row_flip(x_first, 2), row_flip(y_second, 1)]
        return [pair, [x_first, x_second], [y_first, y_second], diagonal]

    def gather_near(own):
        if line != 4:
            return []
        return [line_flip(own, 1), col_send(own, [(1, 2), (2, 1)])]

    def gather_far(own, near, middle, after, late):
        (across,) = relay([col_send(near, [(1, 2), (2, 1)])], after)
        out_two = col_send(middle, [(1, 0), (2, 3)])
        out_three = col_send(across, [(1, 0), (2, 3)])
        return [own, near, *choose(line - 1, across, middle, out_two, out_three, late)]

    halves = piece // edge
    scale, scaled = scale_kernel(degree[:, 0], cotangent, edge)
    early = gather_near(scaled)
    values = features[:, 0].reshape(local_cols, edge, width)
    first_in, number, entries, t_number, t_entries = prepare(
        count, slots, values, scale, 2 * n_col
    )

    def run_pass(source, first, after):
        sums = {}
        come = core_flip(forward(number, entries, tiles, source, first, 1, (1, 0), after))
        for place, part in enumerate((1, 0)):
            keep = forward(number, entries, tiles, source, first, 0, (part,), after)
            sums[part] = pair_sum(keep, come, place * line)
            after = sums[part][:1]
        return sums[0], sums[1]

    own_near, own_far = run_pass(first_in, True, ())
    own = (*own_near, *own_far)
    if early:
        early = relay(early, own_near[:1])
    parts, late = scatter_line(own, relay(own[2:3], own_near[:1])[0])
    if early:
        gathered = gather_far(scaled, *early, own_far[:1], late)
    else:
        gathered = [scaled] + [line_flip(scaled, j) for j in range(1, line)]
    ranged = gathered + [core_flip(g) for g in gathered]
    hidden = backward(t_number, t_entries, tiles, ranged)
    pair = aggregate(parts, scale, (hidden,))
    stacked = first_layer([pair], scale, w_first)
    spread = gather_row(pair, relay(pair, stacked[:1]))
    sums = weight_grads(0, hidden, *stacked, scale, w_first, w_second)
    for group in (spread[1:-1], spread[-1:]):
        start = stacked[0].shape[0]
        stacked = first_layer(group, scale, w_first, stacked, sums[:1])
        sums = weight_grads(start, hidden, *stacked, scale, w_first, w_second, sums)

    grad_give, grad_keep = sums
    own_near, own_far = run_pass(stacked[1], False, (grad_keep,))
    own = (*own_near, *own_far)
    split = split_sum([grad_keep, core_flip(grad_give)], n_row, "row", own_near[:1])
    moment = [split[0]] + [row_flip(split[j], j) for j in range(1, n_row)]
    if split[0].shape[0] % (16 * line) == 0:
        split = split_sum(moment, line, "line")
        moment = [split[0]] + [line_flip(split[j], j) for j in range(1, line)]
        summed = moment = sum_parts(moment)
        moment = join([moment] + [line_flip(moment, j) for j in range(1, line)], "line")
    else:
        moment = sum_parts(moment)
        moment = [moment] + [line_flip(moment, j) for j in range(1, line)]
        summed = moment = sum_parts(moment)
    (behind,) = relay(own[2:3], (summed,))
    parts, _ = scatter_line(own, behind, (moment,))
    moment = [moment] + [row_flip(moment, j) for j in range(1, n_row)]
    mine = join(moment, "row")
    logits = second_layer(parts, scale, w_second)
    return logits, *select(mine, core_flip(mine), (logits,))


def solution(mesh):
    return jax.shard_map(
        per_device,
        mesh=mesh,
        in_specs=(
            P(None, "col", None, None),
            P(None, "col", None),
            P("row", "col", None, None, None),
            P("row", "col", None),
            P("row", "col"),
            P(),
            P(),
            P(("row", "col"), None),
        ),
        out_specs=(P(("row", "col"), None), P(), P()),
        check_vma=False,
    )
```

```python
import functools

import jax
import jax.numpy as jnp
from jax import lax
from jax.experimental import pallas as pl
from jax.experimental.pallas import tpu as pltpu
from jax.sharding import PartitionSpec as P

F32 = jnp.float32
BF16 = jnp.bfloat16
MIB = 1024 * 1024
VMEM = pl.BlockSpec(memory_space=pltpu.VMEM)
SMEM = pl.BlockSpec(memory_space=pltpu.SMEM)
ANY = pl.BlockSpec(memory_space=pl.ANY)


def run(body, args, specs, outs, scratch=(), mib=8, after=(), out_specs=None):
    n, extra = len(args), len(after)

    def whole(*refs):
        body(*refs[:n], *refs[n + extra :])

    return pl.pallas_call(
        whole,
        out_shape=outs,
        in_specs=specs + [ANY] * extra,
        out_specs=out_specs or [VMEM] * len(outs),
        scratch_shapes=list(scratch),
        compiler_params=pltpu.CompilerParams(vmem_limit_bytes=mib * MIB),
        cost_estimate=pl.CostEstimate(
            flops=int(COST.get(getattr(body, "func", body), 0) * 1e9),
            bytes_accessed=0,
            transcendentals=0,
        ),
    )(*args, *after)


def shape(dims, dtype=BF16):
    return jax.ShapeDtypeStruct(dims, dtype)


def list_tiles(count, slot_ref, number_ref, list_ref, local_cols, by_row):
    groups, cap = number_ref.shape[0], list_ref.shape[0] // number_ref.shape[0]
    blank = slot_ref.shape[0] * 1024
    bits = local_cols.bit_length() - 1

    def clear(g, _):
        number_ref[g] = 0
        for j in range(cap):
            list_ref[g * cap + j] = blank
        return 0

    lax.fori_loop(0, groups, clear, 0)

    def place(s, _):
        p = slot_ref[s]
        u, v = lax.shift_right_logical(p, bits), p & (local_cols - 1)
        g, other = (u, v) if by_row else (v, u)
        n = number_ref[g]
        list_ref[g * cap + n] = s * 1024 + other
        number_ref[g] = n + 1
        return 0

    lax.fori_loop(0, count, place, 0)


def repeat_lanes(scale, width):
    return jnp.concatenate([scale] * (width // scale.shape[-1]), 1)


def scale_body(degree, cot, scale, out):
    edge, lanes = scale.shape[1:]
    width = cot.shape[1]
    for i in range(scale.shape[0]):
        part = degree[i // 2 : i // 2 + 1, i % 2 * edge : (i % 2 + 1) * edge]
        line = 1.0 / jnp.sqrt(part.astype(F32))
        scale[i] = jnp.broadcast_to(line, (lanes, edge)).T
    row = lax.axis_index("row")
    for e in range(2):
        value = cot[e * edge : (e + 1) * edge, :].astype(F32)
        out[e] = (value * repeat_lanes(scale[row * 2 + e], width)).T.astype(BF16)


def scale_kernel(degree, cotangent, edge):
    return run(
        scale_body,
        (degree, cotangent),
        [VMEM] * 2,
        [shape((2 * degree.shape[0], edge, 128), F32), shape((2, cotangent.shape[1], edge))],
    )


def prepare_body(count_ref, slot_ref, values, scale, out, *lists):
    local_cols = values.shape[0]
    list_tiles(count_ref[0], slot_ref, lists[0], lists[1], local_cols, True)
    list_tiles(count_ref[0], slot_ref, lists[2], lists[3], local_cols, False)

    def fill(i, _):
        wide = repeat_lanes(scale[i], values.shape[-1])
        out[i] = (values[i].astype(F32) * wide).astype(BF16)
        return 0

    lax.fori_loop(0, local_cols, fill, 0)


def prepare(count, slots, values, scale, block_rows):
    local_cols = values.shape[0]
    sizes = (block_rows, block_rows * local_cols, local_cols, block_rows * local_cols)
    return run(
        prepare_body,
        (count, slots, values, scale),
        [SMEM] * 2 + [VMEM] * 2,
        [shape(values.shape)] + [shape((n,), jnp.int32) for n in sizes],
        out_specs=[VMEM] + [SMEM] * 4,
        mib=12,
    )


def sum_large_group(g, number_ref, list_ref, total, product, store):
    cap = list_ref.shape[0] // number_ref.shape[0]
    n = number_ref[g]
    rest = jnp.where(n == 0, 0, ((n - 1) & 3) + 1)

    def take(start, width):
        entries = [list_ref[g * cap + start + j] for j in range(width)]
        return product([(lax.shift_right_logical(x, 10), x & 1023) for x in entries])

    @pl.when(n == 0)
    def _():
        total[...] = jnp.zeros_like(total)

    def exact(width):
        @pl.when(rest == width)
        def _():
            total[...] = take(0, width)

    for width in range(1, 5):
        exact(width)

    def four(m, _):
        total[...] += take(rest + 4 * m, 4)
        return 0

    lax.fori_loop(0, lax.shift_right_logical(n - rest, 2), four, 0)
    store(total[...])


def sum_group(g, number_ref, list_ref, total, product, store):
    cap = list_ref.shape[0] // number_ref.shape[0]
    n = number_ref[g]

    def take(start, width):
        entries = [list_ref[g * cap + start + j] for j in range(width)]
        return product([(lax.shift_right_logical(x, 10), x & 1023) for x in entries])

    def exact(width):
        @pl.when(n == width)
        def _():
            store(take(0, width))

    @pl.when(n == 0)
    def _():
        store(jnp.zeros_like(total))

    for width in range(1, 5):
        exact(width)

    @pl.when(n > 4)
    def _():
        total[...] = jnp.zeros_like(total)
        fours = lax.shift_right_logical(n, 2)

        def four(m, _):
            total[...] += take(4 * m, 4)
            return 0

        def one(m, _):
            total[...] += take(m, 1)
            return 0

        lax.fori_loop(0, fours, four, 0)
        lax.fori_loop(4 * fours, n, one, 0)
        store(total[...])


def joined_dot(lhs, rhs):
    return jnp.dot(
        jnp.concatenate(lhs, 1), jnp.concatenate(rhs, 0), preferred_element_type=F32
    )


def forward_body(first, flip, number_ref, list_ref, tiles, source, out, total):
    col, row = lax.axis_index("col"), lax.axis_index("row")
    line = out.shape[0] // 2

    def product(pieces):
        def locate(v):
            return v if first else v ^ (2 * row)

        return joined_dot([tiles[s] for s, _ in pieces], [source[locate(v)] for _, v in pieces])

    for half in range(2):

        def block(i, _):
            def store(value):
                out[half * line + i] = value.astype(BF16)

            g = (col ^ (2 * i + flip)) * 2 + half
            sum_group(g, number_ref, list_ref, total, product, store)
            return 0

        lax.fori_loop(0, line, block, 0)


def forward(number, entries, tiles, source, first, flip, after=()):
    slots_n, edge, _ = tiles.shape
    width = source.shape[-1]
    return run(
        functools.partial(forward_body, first, flip),
        (number, entries, tiles, source),
        [SMEM, SMEM, VMEM, VMEM],
        [shape((number.shape[0] // 2, edge, width))],
        [pltpu.VMEM((edge, width), F32)],
        mib=16,
        after=after,
    )[0]


def backward_body(n, number_ref, list_ref, tiles, *refs):
    pieces_in, (out, ranged, total) = refs[:n], refs[n:]
    mask, flips = lax.axis_index("row") * 2, lax.axis_index("col") * 2
    blocks, start = ranged.shape[0], 0
    for piece in pieces_in:
        ranged[start : start + piece.shape[0]] = piece[...]
        start += piece.shape[0]

    def product(pieces):
        def locate(u):
            x = u ^ flips
            return (x & 2) * (blocks // 4) + lax.shift_right_logical(x, 2) * 2 + (x & 1)

        return joined_dot([ranged[locate(u)] for _, u in pieces], [tiles[s] for s, _ in pieces])

    def block(i, _):
        def store(value):
            out[i] = value.astype(BF16)

        sum_large_group(i ^ mask, number_ref, list_ref, total, product, store)
        return 0

    lax.fori_loop(0, out.shape[0], block, 0)


def backward(number, entries, tiles, pieces, after=()):
    slots_n, edge, _ = tiles.shape
    _, width, _ = pieces[0].shape
    n, blocks = len(pieces), sum(x.shape[0] for x in pieces)
    return run(
        functools.partial(backward_body, n),
        (number, entries, tiles, *pieces),
        [SMEM, SMEM] + [VMEM] * (n + 1),
        [shape((number.shape[0], width, edge))],
        [pltpu.VMEM((blocks, width, edge), BF16), pltpu.VMEM((width, edge), F32)],
        mib=20,
        after=after,
    )[0]


def pair_sum_body(n, keep, come, *outs):
    for j in range(n):
        for half in range(2):
            i = half * n + j
            outs[j][half] = (keep[i].astype(F32) + come[i].astype(F32)).astype(BF16)


def pair_sum(keep, come, after=()):
    n = keep.shape[0] // 2
    return run(
        functools.partial(pair_sum_body, n),
        (keep, come),
        [VMEM] * 2,
        [shape((2, *keep.shape[1:]))] * n,
        mib=12,
        after=after,
    )


def tree(items):
    while len(items) > 1:
        rest = items[len(items) // 2 * 2 :]
        items = [a + b for a, b in zip(items[::2], items[1::2])] + rest
    return items[0]


def relay_body(n, *refs):
    for source, out in zip(refs[:n], refs[n:]):
        out[...] = source[...]


def relay(items, after):
    return run(
        functools.partial(relay_body, len(items)),
        tuple(items),
        [VMEM] * len(items),
        [shape(x.shape) for x in items],
        after=after,
    )


def choose_body(last, across, middle, out_two, out_three, *outs):
    ends = jnp.logical_or(position("col") == 0, position("col") == last)
    for half in range(2):
        outs[half][0] = jnp.where(ends, out_two[half], across[half])
        outs[2 + half][0] = jnp.where(ends, out_three[half], middle[half])


def choose(last, across, middle, out_two, out_three, after):
    return run(
        functools.partial(choose_body, last),
        (across, middle, out_two, out_three),
        [VMEM] * 4,
        [shape((1, *across.shape[1:]))] * 4,
        after=after,
    )


def agg_body(n, *refs):
    scale, outs = refs[n], refs[n + 1 :]
    for half, out in enumerate(outs):
        summed = tree([x[half].astype(F32) for x in refs[:n]])
        wide = repeat_lanes(scale[lax.axis_index("row") * 2 + half], summed.shape[1])
        out[...] = (summed * wide).astype(BF16)


def aggregate(parts, scale, after):
    return run(
        functools.partial(agg_body, len(parts)),
        (*parts, scale),
        [VMEM] * (len(parts) + 1),
        [shape(parts[0].shape[1:])] * 2,
        after=after,
    )


def first_body(start, n, *refs):
    scale, weight, agg, out = refs[2 * n], refs[2 * n + 1], refs[-2], refs[-1]
    row = lax.axis_index("row")
    if start:
        agg[: 2 * start] = refs[2 * n + 2][...]
        out[: 2 * start] = refs[2 * n + 3][...]
    for i in range(2 * n):
        block = 2 * start + i
        value = jnp.dot(refs[i][...], weight[...], preferred_element_type=F32)
        wide = repeat_lanes(scale[block ^ (2 * row)], value.shape[1])
        out[block] = (jax.nn.gelu(value) * wide).astype(BF16)
        agg[block] = refs[i][...]


def first_layer(aggs, scale, weight, before=(), after=()):
    n = len(aggs)
    start = before[0].shape[0] // 2 if before else 0
    return run(
        functools.partial(first_body, start, n),
        (*[x for pair in aggs for x in pair], scale, weight, *before),
        [VMEM] * (2 * n + 2 + len(before)),
        [shape((2 * (start + n), *aggs[0][0].shape))] * 2,
        mib=14,
        after=after,
    )


def second_body(*refs):
    scale, weight, out = refs[-3:]
    edge = refs[0].shape[1]
    for half in range(2):
        summed = tree([x[half].astype(F32) for x in refs[:-3]])
        wide = repeat_lanes(scale[lax.axis_index("row") * 2 + half], summed.shape[1])
        agg = (summed * wide).astype(BF16)
        value = jnp.dot(agg, weight[...], preferred_element_type=F32)
        out[half * edge : (half + 1) * edge, :] = value.astype(BF16)


def second_layer(parts, scale, weight, after):
    halves, edge, width = parts[0].shape
    return run(
        second_body,
        (*parts, scale, weight),
        [VMEM] * (2 + len(parts)),
        [shape((halves * edge, width))],
        after=after,
    )[0]


def grad_body(start, last, hidden_ref, aggs, outs, scale, w_first, w_second, *refs):
    row = lax.axis_index("row")
    core = lax.rem(lax.axis_index("col"), 2)
    first, second = refs[-2:]
    if start:
        first[...] = refs[0][...]
        second[...] = refs[1][...]
    else:
        first[...] = jnp.zeros_like(first)
        second[...] = jnp.zeros_like(second)

    def block(i, _):
        hidden, agg = hidden_ref[i], aggs[i]
        pre = jnp.dot(agg, w_first[...], preferred_element_type=F32)
        grad_hidden = lax.dot_general(
            hidden, w_second[...], (((0,), (1,)), ((), ())), preferred_element_type=F32
        )
        _, pullback = jax.vjp(jax.nn.gelu, pre)
        wide = repeat_lanes(scale[i ^ (2 * row)], pre.shape[1])
        grad_pre = pullback(grad_hidden * wide)[0].astype(BF16)
        first[...] += lax.dot_general(
            agg, grad_pre, (((0,), (0,)), ((), ())), preferred_element_type=F32
        )
        second[...] += lax.dot_general(
            outs[i], hidden, (((0,), (1,)), ((), ())), preferred_element_type=F32
        )
        return 0

    lax.fori_loop(start, aggs.shape[0], block, 0)
    if last:
        give, keep = refs[2:4]
        keep[...] = jnp.where(core == 0, first[...], second[...]).astype(BF16)
        give[...] = jnp.where(core == 0, second[...], first[...]).astype(BF16)


def weight_grads(start, hidden, aggs, outs, scale, w_first, w_second, before=(), after=()):
    dims = w_first.shape
    last = aggs.shape[0] == hidden.shape[0]
    return run(
        functools.partial(grad_body, start, last),
        (hidden, aggs, outs, scale, w_first, w_second, *before),
        [VMEM] * (6 + len(before)),
        [shape(dims)] * 2 if last else [shape(dims, F32)] * 2,
        [pltpu.VMEM(dims, F32)] * 2 if last else [],
        mib=26,
        after=after,
    )


def position(axis):
    if axis == "row":
        return lax.axis_index("row")
    return lax.shift_right_logical(lax.axis_index("col"), 1)


def split_body(n, axis, *refs):
    ins, outs = refs[:-n], refs[-n:]
    rows = ins[0].shape[0] // n
    for j in range(n):
        part = pl.ds(pl.multiple_of((position(axis) ^ j) * rows, rows), rows)
        outs[j][...] = tree([x[part, :].astype(F32) for x in ins]).astype(BF16)


def split_sum(items, n, axis, after=()):
    rows, width = items[0].shape
    return run(
        functools.partial(split_body, n, axis),
        tuple(items),
        [VMEM] * len(items),
        [shape((rows // n, width))] * n,
        after=after,
    )


def sum_body(n, *refs):
    refs[n][...] = tree([x[...].astype(F32) for x in refs[:n]]).astype(BF16)


def sum_parts(parts, after=()):
    return run(
        functools.partial(sum_body, len(parts)),
        tuple(parts),
        [VMEM] * len(parts),
        [shape(parts[0].shape)],
        after=after,
    )[0]


def join_body(n, axis, *refs):
    rows = refs[0].shape[0]
    for j in range(n):
        part = pl.ds(pl.multiple_of((position(axis) ^ j) * rows, rows), rows)
        refs[n][part, :] = refs[j][...]


def join(parts, axis):
    rows, width = parts[0].shape
    return run(
        functools.partial(join_body, len(parts), axis),
        tuple(parts),
        [VMEM] * len(parts),
        [shape((rows * len(parts), width))],
    )[0]


def select_body(mine, other, first, second):
    core = lax.rem(lax.axis_index("col"), 2)
    first[...] = jnp.where(core == 0, mine[...].astype(F32), other[...].astype(F32))
    second[...] = jnp.where(core == 0, other[...].astype(F32), mine[...].astype(F32))


def select(mine, other):
    return run(select_body, (mine, other), [VMEM] * 2, [shape(mine.shape, F32)] * 2)


COST = {
    scale_body: 36,
    prepare_body: 36,
    forward_body: 36,
    grad_body: 36,
    second_body: 36,
}


def per_device(features, degree, tile_vals, tile_slot, tile_count, w_first, w_second, cotangent):
    n_row, n_col = lax.axis_size("row"), lax.axis_size("col")
    line = n_col // 2
    piece, width = cotangent.shape
    tiles = tile_vals[0, 0]
    edge = tiles.shape[-1]
    local_cols = n_row * 2
    slots, count = tile_slot[0, 0], tile_count[0]

    def col_send(value, pairs):
        return lax.ppermute(
            value, "col", [(2 * a + k, 2 * b + k) for a, b in pairs for k in range(2)]
        )

    def line_flip(value, j):
        return col_send(value, [(a, a ^ j) for a in range(line)])

    def core_flip(value):
        return lax.ppermute(value, "col", [(a, a ^ 1) for a in range(n_col)])

    def row_flip(value, j):
        return lax.ppermute(value, "row", [(a, a ^ j) for a in range(n_row)])

    def scatter_line(own, behind, after=()):
        if line != 4:
            return [own[0]] + [line_flip(own[j], j) for j in range(1, line)], own[:2]
        to_three = col_send(own[3], [(0, 1), (3, 2)])
        to_two = col_send(behind, [(0, 1), (3, 2)])
        crossing = sum_parts([behind, to_three])
        meeting = sum_parts([own[3], to_two], (crossing, *after))
        crossed = col_send(crossing, [(1, 2), (2, 1)])
        met = col_send(meeting, [(1, 2), (2, 1)])
        outward = sum_parts([own[1], crossed])
        return [own[0], line_flip(outward, 1), met], (meeting, outward)

    def gather_row(pair, behind):
        if n_row != 4:
            return [pair] + [[row_flip(x, j) for x in pair] for j in range(1, n_row)]
        x_first, y_second = row_flip(pair[0], 1), row_flip(pair[1], 2)
        x_second, y_first = row_flip(behind[1], 1), row_flip(behind[0], 2)
        diagonal = [row_flip(x_first, 2), row_flip(y_second, 1)]
        return [pair, [x_first, x_second], [y_first, y_second], diagonal]

    def gather_near(own):
        if line != 4:
            return []
        return [line_flip(own, 1), col_send(own, [(1, 2), (2, 1)])]

    def gather_far(own, near, middle, after, late):
        (across,) = relay([col_send(near, [(1, 2), (2, 1)])], after)
        out_two = col_send(middle, [(1, 0), (2, 3)])
        out_three = col_send(across, [(1, 0), (2, 3)])
        return [own, near, *choose(line - 1, across, middle, out_two, out_three, late)]

    halves = piece // edge
    scale, scaled = scale_kernel(degree[:, 0], cotangent, edge)
    early = gather_near(scaled)
    values = features[:, 0].reshape(local_cols, edge, width)
    first_in, number, entries, t_number, t_entries = prepare(
        count, slots, values, scale, 2 * n_col
    )

    give = forward(number, entries, tiles, first_in, True, 1)
    keep = forward(number, entries, tiles, first_in, True, 0)
    if early:
        early = relay(early, (give,))
    own = pair_sum(keep, core_flip(give))
    parts, late = scatter_line(own, own[2])
    if early:
        gathered = gather_far(scaled, *early, (own[0],), late)
    else:
        gathered = [scaled] + [line_flip(scaled, j) for j in range(1, line)]
    ranged = gathered + [core_flip(g) for g in gathered]
    hidden = backward(t_number, t_entries, tiles, ranged)
    pair = aggregate(parts, scale, (hidden,))
    stacked = first_layer([pair], scale, w_first)
    spread = gather_row(pair, relay(pair, stacked[:1]))
    sums = weight_grads(0, hidden, *stacked, scale, w_first, w_second)
    for group in (spread[1:-1], spread[-1:]):
        start = stacked[0].shape[0]
        stacked = first_layer(group, scale, w_first, stacked, sums[:1])
        sums = weight_grads(start, hidden, *stacked, scale, w_first, w_second, sums)

    grad_give, grad_keep = sums
    give = forward(number, entries, tiles, stacked[1], False, 1, (grad_keep,))
    keep = forward(number, entries, tiles, stacked[1], False, 0)
    own = pair_sum(keep, core_flip(give))
    split = split_sum([grad_keep, core_flip(grad_give)], n_row, "row", own[:1])
    moment = [split[0]] + [row_flip(split[j], j) for j in range(1, n_row)]
    if split[0].shape[0] % (16 * line) == 0:
        split = split_sum(moment, line, "line")
        moment = sum_parts([split[0]] + [line_flip(split[j], j) for j in range(1, line)])
        moment = join([moment] + [line_flip(moment, j) for j in range(1, line)], "line")
    else:
        moment = sum_parts(moment)
        moment = sum_parts([moment] + [line_flip(moment, j) for j in range(1, line)])
    (behind,) = relay(own[2:3], (moment,))
    moment = [moment] + [row_flip(moment, j) for j in range(1, n_row)]
    mine = join(moment, "row")
    parts, _ = scatter_line(own, behind, (mine,))
    grad_first, grad_second = select(mine, core_flip(mine))
    logits = second_layer(parts, scale, w_second, (grad_second,))
    return logits, grad_first, grad_second


def solution(mesh):
    return jax.shard_map(
        per_device,
        mesh=mesh,
        in_specs=(
            P(None, "col", None, None),
            P(None, "col", None),
            P("row", "col", None, None, None),
            P("row", "col", None),
            P("row", "col"),
            P(),
            P(),
            P(("row", "col"), None),
        ),
        out_specs=(P(("row", "col"), None), P(), P()),
        check_vma=False,
    )
```

```python
import functools

import jax
import jax.numpy as jnp
from jax import lax
from jax.experimental import pallas as pl
from jax.experimental.pallas import tpu as pltpu
from jax.sharding import PartitionSpec as P

F32 = jnp.float32
BF16 = jnp.bfloat16
MIB = 1024 * 1024
VMEM = pl.BlockSpec(memory_space=pltpu.VMEM)
SMEM = pl.BlockSpec(memory_space=pltpu.SMEM)
ANY = pl.BlockSpec(memory_space=pl.ANY)


def run(body, args, specs, outs, scratch=(), mib=8, after=(), out_specs=None, cost=None):
    n, extra = len(args), len(after)
    cost = COST.get(getattr(body, "func", body), 0) if cost is None else cost

    def whole(*refs):
        body(*refs[:n], *refs[n + extra :])

    return pl.pallas_call(
        whole,
        out_shape=outs,
        in_specs=specs + [ANY] * extra,
        out_specs=out_specs or [VMEM] * len(outs),
        scratch_shapes=list(scratch),
        compiler_params=pltpu.CompilerParams(vmem_limit_bytes=mib * MIB),
        cost_estimate=pl.CostEstimate(
            flops=int(cost * 1e9),
            bytes_accessed=0,
            transcendentals=0,
        ),
    )(*args, *after)


def shape(dims, dtype=BF16):
    return jax.ShapeDtypeStruct(dims, dtype)


def list_tiles(count, slot_ref, number_ref, list_ref, local_cols, by_row):
    groups, cap = number_ref.shape[0], list_ref.shape[0] // number_ref.shape[0]
    blank = slot_ref.shape[0] * 1024
    bits = local_cols.bit_length() - 1

    def clear(g, _):
        number_ref[g] = 0
        for j in range(cap):
            list_ref[g * cap + j] = blank
        return 0

    lax.fori_loop(0, groups, clear, 0)

    def place(s, _):
        p = slot_ref[s]
        u, v = lax.shift_right_logical(p, bits), p & (local_cols - 1)
        g, other = (u, v) if by_row else (v, u)
        n = number_ref[g]
        list_ref[g * cap + n] = s * 1024 + other
        number_ref[g] = n + 1
        return 0

    lax.fori_loop(0, count, place, 0)


def repeat_lanes(scale, width):
    return jnp.concatenate([scale] * (width // scale.shape[-1]), 1)


def scale_body(degree, cot, scale, out):
    edge, lanes = scale.shape[1:]
    width = cot.shape[1]
    for i in range(scale.shape[0]):
        part = degree[i // 2 : i // 2 + 1, i % 2 * edge : (i % 2 + 1) * edge]
        line = 1.0 / jnp.sqrt(part.astype(F32))
        scale[i] = jnp.broadcast_to(line, (lanes, edge)).T
    row = lax.axis_index("row")
    for e in range(2):
        value = cot[e * edge : (e + 1) * edge, :].astype(F32)
        out[e] = (value * repeat_lanes(scale[row * 2 + e], width)).T.astype(BF16)


def scale_kernel(degree, cotangent, edge):
    return run(
        scale_body,
        (degree, cotangent),
        [VMEM] * 2,
        [shape((2 * degree.shape[0], edge, 128), F32), shape((2, cotangent.shape[1], edge))],
    )


def prepare_body(count_ref, slot_ref, values, scale, out, *lists):
    local_cols = values.shape[0]
    list_tiles(count_ref[0], slot_ref, lists[0], lists[1], local_cols, True)
    list_tiles(count_ref[0], slot_ref, lists[2], lists[3], local_cols, False)

    def fill(i, _):
        wide = repeat_lanes(scale[i], values.shape[-1])
        out[i] = (values[i].astype(F32) * wide).astype(BF16)
        return 0

    lax.fori_loop(0, local_cols, fill, 0)


def prepare(count, slots, values, scale, block_rows):
    local_cols = values.shape[0]
    sizes = (block_rows, block_rows * local_cols, local_cols, block_rows * local_cols)
    return run(
        prepare_body,
        (count, slots, values, scale),
        [SMEM] * 2 + [VMEM] * 2,
        [shape(values.shape)] + [shape((n,), jnp.int32) for n in sizes],
        out_specs=[VMEM] + [SMEM] * 4,
        mib=12,
    )


def sum_large_group(g, number_ref, list_ref, total, product, store):
    cap = list_ref.shape[0] // number_ref.shape[0]
    n = number_ref[g]
    rest = jnp.where(n == 0, 0, ((n - 1) & 3) + 1)

    def take(start, width):
        entries = [list_ref[g * cap + start + j] for j in range(width)]
        return product([(lax.shift_right_logical(x, 10), x & 1023) for x in entries])

    @pl.when(n == 0)
    def _():
        total[...] = jnp.zeros_like(total)

    def exact(width):
        @pl.when(rest == width)
        def _():
            total[...] = take(0, width)

    for width in range(1, 5):
        exact(width)

    def four(m, _):
        total[...] += take(rest + 4 * m, 4)
        return 0

    lax.fori_loop(0, lax.shift_right_logical(n - rest, 2), four, 0)
    store(total[...])


def sum_group(g, number_ref, list_ref, total, product, store):
    cap = list_ref.shape[0] // number_ref.shape[0]
    n = number_ref[g]

    def take(start, width):
        entries = [list_ref[g * cap + start + j] for j in range(width)]
        return product([(lax.shift_right_logical(x, 10), x & 1023) for x in entries])

    def exact(width):
        @pl.when(n == width)
        def _():
            store(take(0, width))

    @pl.when(n == 0)
    def _():
        store(jnp.zeros_like(total))

    for width in range(1, 5):
        exact(width)

    @pl.when(n > 4)
    def _():
        total[...] = jnp.zeros_like(total)
        fours = lax.shift_right_logical(n, 2)

        def four(m, _):
            total[...] += take(4 * m, 4)
            return 0

        def one(m, _):
            total[...] += take(m, 1)
            return 0

        lax.fori_loop(0, fours, four, 0)
        lax.fori_loop(4 * fours, n, one, 0)
        store(total[...])


def joined_dot(lhs, rhs):
    return jnp.dot(
        jnp.concatenate(lhs, 1), jnp.concatenate(rhs, 0), preferred_element_type=F32
    )


def forward_body(first, flip, parts, number_ref, list_ref, tiles, source, out, total):
    col, row = lax.axis_index("col"), lax.axis_index("row")
    n = out.shape[0] // (2 * len(parts))

    def product(pieces):
        def locate(v):
            return v if first else v ^ (2 * row)

        return joined_dot([tiles[s] for s, _ in pieces], [source[locate(v)] for _, v in pieces])

    for place, part in enumerate(parts):
        for half in range(2):

            def block(i, _):
                def store(value):
                    out[(2 * place + half) * n + i] = value.astype(BF16)

                g = (col ^ (2 * (part * n + i) + flip)) * 2 + half
                sum_group(g, number_ref, list_ref, total, product, store)
                return 0

            lax.fori_loop(0, n, block, 0)


def forward(number, entries, tiles, source, first, flip, parts, after=()):
    edge, width = tiles.shape[-1], source.shape[-1]
    return run(
        functools.partial(forward_body, first, flip, parts),
        (number, entries, tiles, source),
        [SMEM, SMEM, VMEM, VMEM],
        [shape((len(parts) * number.shape[0] // 4, edge, width))],
        [pltpu.VMEM((edge, width), F32)],
        mib=16,
        after=after,
        cost=36,
    )[0]


def backward_body(n, number_ref, list_ref, tiles, *refs):
    pieces_in, (out, ranged, total) = refs[:n], refs[n:]
    mask, flips = lax.axis_index("row") * 2, lax.axis_index("col") * 2
    blocks, start = ranged.shape[0], 0
    for piece in pieces_in:
        ranged[start : start + piece.shape[0]] = piece[...]
        start += piece.shape[0]

    def product(pieces):
        def locate(u):
            x = u ^ flips
            return (x & 2) * (blocks // 4) + lax.shift_right_logical(x, 2) * 2 + (x & 1)

        return joined_dot([ranged[locate(u)] for _, u in pieces], [tiles[s] for s, _ in pieces])

    def block(i, _):
        def store(value):
            out[i] = value.astype(BF16)

        sum_large_group(i ^ mask, number_ref, list_ref, total, product, store)
        return 0

    lax.fori_loop(0, out.shape[0], block, 0)


def backward(number, entries, tiles, pieces, after=()):
    slots_n, edge, _ = tiles.shape
    _, width, _ = pieces[0].shape
    n, blocks = len(pieces), sum(x.shape[0] for x in pieces)
    return run(
        functools.partial(backward_body, n),
        (number, entries, tiles, *pieces),
        [SMEM, SMEM] + [VMEM] * (n + 1),
        [shape((number.shape[0], width, edge))],
        [pltpu.VMEM((blocks, width, edge), BF16), pltpu.VMEM((width, edge), F32)],
        mib=20,
        after=after,
    )[0]


def pair_sum_body(start, n, keep, come, *outs):
    for j, out in enumerate(outs):
        for half in range(2):
            i = (j // n * 2 + half) * n + j % n
            out[half] = (keep[i].astype(F32) + come[start + i].astype(F32)).astype(BF16)


def pair_sum(keep, come, start):
    n = come.shape[0] // 4
    return run(
        functools.partial(pair_sum_body, start, n),
        (keep, come),
        [VMEM] * 2,
        [shape((2, *keep.shape[1:]))] * (keep.shape[0] // 2),
        mib=12,
    )


def tree(items):
    while len(items) > 1:
        rest = items[len(items) // 2 * 2 :]
        items = [a + b for a, b in zip(items[::2], items[1::2])] + rest
    return items[0]


def relay_body(n, *refs):
    for source, out in zip(refs[:n], refs[n:]):
        out[...] = source[...]


def relay(items, after):
    return run(
        functools.partial(relay_body, len(items)),
        tuple(items),
        [VMEM] * len(items),
        [shape(x.shape) for x in items],
        after=after,
    )


def choose_body(last, across, middle, out_two, out_three, *outs):
    ends = jnp.logical_or(position("col") == 0, position("col") == last)
    for half in range(2):
        outs[half][0] = jnp.where(ends, out_two[half], across[half])
        outs[2 + half][0] = jnp.where(ends, out_three[half], middle[half])


def choose(last, across, middle, out_two, out_three, after):
    return run(
        functools.partial(choose_body, last),
        (across, middle, out_two, out_three),
        [VMEM] * 4,
        [shape((1, *across.shape[1:]))] * 4,
        after=after,
    )


def agg_body(n, *refs):
    scale, outs = refs[n], refs[n + 1 :]
    for half, out in enumerate(outs):
        summed = tree([x[half].astype(F32) for x in refs[:n]])
        wide = repeat_lanes(scale[lax.axis_index("row") * 2 + half], summed.shape[1])
        out[...] = (summed * wide).astype(BF16)


def aggregate(parts, scale, after):
    return run(
        functools.partial(agg_body, len(parts)),
        (*parts, scale),
        [VMEM] * (len(parts) + 1),
        [shape(parts[0].shape[1:])] * 2,
        after=after,
    )


def first_body(start, n, *refs):
    scale, weight, agg, out = refs[2 * n], refs[2 * n + 1], refs[-2], refs[-1]
    row = lax.axis_index("row")
    if start:
        agg[: 2 * start] = refs[2 * n + 2][...]
        out[: 2 * start] = refs[2 * n + 3][...]
    for i in range(2 * n):
        block = 2 * start + i
        value = jnp.dot(refs[i][...], weight[...], preferred_element_type=F32)
        wide = repeat_lanes(scale[block ^ (2 * row)], value.shape[1])
        out[block] = (jax.nn.gelu(value) * wide).astype(BF16)
        agg[block] = refs[i][...]


def first_layer(aggs, scale, weight, before=(), after=()):
    n = len(aggs)
    start = before[0].shape[0] // 2 if before else 0
    return run(
        functools.partial(first_body, start, n),
        (*[x for pair in aggs for x in pair], scale, weight, *before),
        [VMEM] * (2 * n + 2 + len(before)),
        [shape((2 * (start + n), *aggs[0][0].shape))] * 2,
        mib=14,
        after=after,
    )


def second_body(*refs):
    scale, weight, out, mark = refs[-4:]
    edge = refs[0].shape[1]
    mark[...] = jnp.zeros_like(mark)
    for half in range(2):
        summed = tree([x[half].astype(F32) for x in refs[:-4]])
        wide = repeat_lanes(scale[lax.axis_index("row") * 2 + half], summed.shape[1])
        agg = (summed * wide).astype(BF16)
        value = jnp.dot(agg, weight[...], preferred_element_type=F32)
        out[half * edge : (half + 1) * edge, :] = value.astype(BF16)


def second_layer(parts, scale, weight):
    halves, edge, width = parts[0].shape
    return run(
        second_body,
        (*parts, scale, weight),
        [VMEM] * (2 + len(parts)),
        [shape((halves * edge, width)), shape((8, 128), F32)],
    )


def grad_body(start, last, hidden_ref, aggs, outs, scale, w_first, w_second, *refs):
    row = lax.axis_index("row")
    core = lax.rem(lax.axis_index("col"), 2)
    first, second = refs[-2:]
    if start:
        first[...] = refs[0][...]
        second[...] = refs[1][...]
    else:
        first[...] = jnp.zeros_like(first)
        second[...] = jnp.zeros_like(second)

    def block(i, _):
        hidden, agg = hidden_ref[i], aggs[i]
        pre = jnp.dot(agg, w_first[...], preferred_element_type=F32)
        grad_hidden = lax.dot_general(
            hidden, w_second[...], (((0,), (1,)), ((), ())), preferred_element_type=F32
        )
        _, pullback = jax.vjp(jax.nn.gelu, pre)
        wide = repeat_lanes(scale[i ^ (2 * row)], pre.shape[1])
        grad_pre = pullback(grad_hidden * wide)[0].astype(BF16)
        first[...] += lax.dot_general(
            agg, grad_pre, (((0,), (0,)), ((), ())), preferred_element_type=F32
        )
        second[...] += lax.dot_general(
            outs[i], hidden, (((0,), (1,)), ((), ())), preferred_element_type=F32
        )
        return 0

    lax.fori_loop(start, aggs.shape[0], block, 0)
    if last:
        give, keep = refs[2:4]
        keep[...] = jnp.where(core == 0, first[...], second[...]).astype(BF16)
        give[...] = jnp.where(core == 0, second[...], first[...]).astype(BF16)


def weight_grads(start, hidden, aggs, outs, scale, w_first, w_second, before=(), after=()):
    dims = w_first.shape
    last = aggs.shape[0] == hidden.shape[0]
    return run(
        functools.partial(grad_body, start, last),
        (hidden, aggs, outs, scale, w_first, w_second, *before),
        [VMEM] * (6 + len(before)),
        [shape(dims)] * 2 if last else [shape(dims, F32)] * 2,
        [pltpu.VMEM(dims, F32)] * 2 if last else [],
        mib=26,
        after=after,
    )


def position(axis):
    if axis == "row":
        return lax.axis_index("row")
    return lax.shift_right_logical(lax.axis_index("col"), 1)


def split_body(n, axis, *refs):
    ins, outs = refs[:-n], refs[-n:]
    rows = ins[0].shape[0] // n
    for j in range(n):
        part = pl.ds(pl.multiple_of((position(axis) ^ j) * rows, rows), rows)
        outs[j][...] = tree([x[part, :].astype(F32) for x in ins]).astype(BF16)


def split_sum(items, n, axis, after=()):
    rows, width = items[0].shape
    return run(
        functools.partial(split_body, n, axis),
        tuple(items),
        [VMEM] * len(items),
        [shape((rows // n, width))] * n,
        after=after,
    )


def sum_body(n, *refs):
    refs[n][...] = tree([x[...].astype(F32) for x in refs[:n]]).astype(BF16)


def sum_parts(parts, after=()):
    return run(
        functools.partial(sum_body, len(parts)),
        tuple(parts),
        [VMEM] * len(parts),
        [shape(parts[0].shape)],
        after=after,
    )[0]


def join_body(n, axis, *refs):
    rows = refs[0].shape[0]
    for j in range(n):
        part = pl.ds(pl.multiple_of((position(axis) ^ j) * rows, rows), rows)
        refs[n][part, :] = refs[j][...]


def join(parts, axis):
    rows, width = parts[0].shape
    return run(
        functools.partial(join_body, len(parts), axis),
        tuple(parts),
        [VMEM] * len(parts),
        [shape((rows * len(parts), width))],
    )[0]


def select_body(mine, other, first, second):
    core = lax.rem(lax.axis_index("col"), 2)
    first[...] = jnp.where(core == 0, mine[...].astype(F32), other[...].astype(F32))
    second[...] = jnp.where(core == 0, other[...].astype(F32), mine[...].astype(F32))


def select(mine, other, after):
    return run(
        select_body, (mine, other), [VMEM] * 2, [shape(mine.shape, F32)] * 2, after=after
    )


COST = {
    scale_body: 36,
    prepare_body: 36,
    grad_body: 36,
    second_body: 36,
}


def per_device(features, degree, tile_vals, tile_slot, tile_count, w_first, w_second, cotangent):
    n_row, n_col = lax.axis_size("row"), lax.axis_size("col")
    line = n_col // 2
    piece, width = cotangent.shape
    tiles = tile_vals[0, 0]
    edge = tiles.shape[-1]
    local_cols = n_row * 2
    slots, count = tile_slot[0, 0], tile_count[0]

    def col_send(value, pairs):
        return lax.ppermute(
            value, "col", [(2 * a + k, 2 * b + k) for a, b in pairs for k in range(2)]
        )

    def line_flip(value, j):
        return col_send(value, [(a, a ^ j) for a in range(line)])

    def core_flip(value):
        return lax.ppermute(value, "col", [(a, a ^ 1) for a in range(n_col)])

    def row_flip(value, j):
        return lax.ppermute(value, "row", [(a, a ^ j) for a in range(n_row)])

    def scatter_line(own, behind, after=()):
        if line != 4:
            return [own[0]] + [line_flip(own[j], j) for j in range(1, line)], own[:2]
        to_three = col_send(own[3], [(0, 1), (3, 2)])
        to_two = col_send(behind, [(0, 1), (3, 2)])
        crossing = sum_parts([behind, to_three], own[:1])
        meeting = sum_parts([own[3], to_two], (crossing, *after))
        crossed = col_send(crossing, [(1, 2), (2, 1)])
        met = col_send(meeting, [(1, 2), (2, 1)])
        outward = sum_parts([own[1], crossed])
        return [own[0], line_flip(outward, 1), met], (meeting, outward)

    def gather_row(pair, behind):
        if n_row != 4:
            return [pair] + [[row_flip(x, j) for x in pair] for j in range(1, n_row)]
        x_first, y_second = row_flip(pair[0], 1), row_flip(pair[1], 2)
        x_second, y_first = row_flip(behind[1], 1), row_flip(behind[0], 2)
        diagonal = [row_flip(x_first, 2), row_flip(y_second, 1)]
        return [pair, [x_first, x_second], [y_first, y_second], diagonal]

    def gather_near(own):
        if line != 4:
            return []
        return [line_flip(own, 1), col_send(own, [(1, 2), (2, 1)])]

    def gather_far(own, near, middle, after, late):
        out_two = col_send(middle, [(1, 0), (2, 3)])
        (across,) = relay([col_send(near, [(1, 2), (2, 1)])], (*after, out_two))
        out_three = col_send(across, [(1, 0), (2, 3)])
        return [own, near, *choose(line - 1, across, middle, out_two, out_three, late)]

    halves = piece // edge
    scale, scaled = scale_kernel(degree[:, 0], cotangent, edge)
    early = gather_near(scaled)
    values = features[:, 0].reshape(local_cols, edge, width)
    first_in, number, entries, t_number, t_entries = prepare(
        count, slots, values, scale, 2 * n_col
    )

    def run_pass(source, first, cuts, after):
        sums = {}
        give = forward(number, entries, tiles, source, first, 1, (1, 0), after)
        come = core_flip(give)
        for cut in cuts:
            keep = forward(number, entries, tiles, source, first, 0, cut, after)
            pieces = pair_sum(keep, come, 0 if 1 in cut else line)
            for place, part in enumerate(cut):
                sums[part] = pieces[place * line // 2 : (place + 1) * line // 2]
            after = pieces[:1]
        return give, (*sums[0], *sums[1])

    give, own = run_pass(first_in, True, ((1, 0),), ())
    if early:
        early = relay(early, (give,))
    parts, late = scatter_line(own, own[2])
    if early:
        gathered = gather_far(scaled, *early, own[:1], late)
    else:
        gathered = [scaled] + [line_flip(scaled, j) for j in range(1, line)]
    ranged = gathered + [core_flip(g) for g in gathered]
    hidden = backward(t_number, t_entries, tiles, ranged)
    pair = aggregate(parts, scale, (hidden,))
    stacked = first_layer([pair], scale, w_first)
    spread = gather_row(pair, relay(pair, stacked[:1]))
    sums = weight_grads(0, hidden, *stacked, scale, w_first, w_second)
    for group in (spread[1:-1], spread[-1:]):
        start = stacked[0].shape[0]
        stacked = first_layer(group, scale, w_first, stacked, sums[:1])
        sums = weight_grads(start, hidden, *stacked, scale, w_first, w_second, sums)

    grad_give, grad_keep = sums
    _, own = run_pass(stacked[1], False, ((1,), (0,)), (grad_keep,))
    split = split_sum([grad_keep, core_flip(grad_give)], n_row, "row", own[:1])
    moment = [split[0]] + [row_flip(split[j], j) for j in range(1, n_row)]
    if split[0].shape[0] % (16 * line) == 0:
        split = split_sum(moment, line, "line")
        moment = [split[0]] + [line_flip(split[j], j) for j in range(1, line)]
        summed = moment = sum_parts(moment)
        moment = join([moment] + [line_flip(moment, j) for j in range(1, line)], "line")
    else:
        moment = sum_parts(moment)
        moment = [moment] + [line_flip(moment, j) for j in range(1, line)]
        summed = moment = sum_parts(moment)
    (behind,) = relay(own[2:3], (summed,))
    parts, _ = scatter_line(own, behind, (moment,))
    moment = [moment] + [row_flip(moment, j) for j in range(1, n_row)]
    mine = join(moment, "row")
    logits, mark = second_layer(parts, scale, w_second)
    return logits, *select(mine, core_flip(mine), (mark,))


def solution(mesh):
    return jax.shard_map(
        per_device,
        mesh=mesh,
        in_specs=(
            P(None, "col", None, None),
            P(None, "col", None),
            P("row", "col", None, None, None),
            P("row", "col", None),
            P("row", "col"),
            P(),
            P(),
            P(("row", "col"), None),
        ),
        out_specs=(P(("row", "col"), None), P(), P()),
        check_vma=False,
    )
```

```python
import functools

import jax
import jax.numpy as jnp
from jax import lax
from jax.experimental import pallas as pl
from jax.experimental.pallas import tpu as pltpu
from jax.sharding import PartitionSpec as P

F32 = jnp.float32
BF16 = jnp.bfloat16
MIB = 1024 * 1024
VMEM = pl.BlockSpec(memory_space=pltpu.VMEM)
SMEM = pl.BlockSpec(memory_space=pltpu.SMEM)
ANY = pl.BlockSpec(memory_space=pl.ANY)


def run(body, args, specs, outs, scratch=(), mib=8, after=(), out_specs=None, cost=None):
    n, extra = len(args), len(after)
    cost = COST.get(getattr(body, "func", body), 0) if cost is None else cost

    def whole(*refs):
        body(*refs[:n], *refs[n + extra :])

    return pl.pallas_call(
        whole,
        out_shape=outs,
        in_specs=specs + [ANY] * extra,
        out_specs=out_specs or [VMEM] * len(outs),
        scratch_shapes=list(scratch),
        compiler_params=pltpu.CompilerParams(vmem_limit_bytes=mib * MIB),
        cost_estimate=pl.CostEstimate(
            flops=int(cost * 1e9),
            bytes_accessed=0,
            transcendentals=0,
        ),
    )(*args, *after)


def shape(dims, dtype=BF16):
    return jax.ShapeDtypeStruct(dims, dtype)


def list_tiles(count, slot_ref, number_ref, list_ref, local_cols, by_row):
    groups, cap = number_ref.shape[0], list_ref.shape[0] // number_ref.shape[0]
    blank = slot_ref.shape[0] * 1024
    bits = local_cols.bit_length() - 1

    def clear(g, _):
        number_ref[g] = 0
        for j in range(cap):
            list_ref[g * cap + j] = blank
        return 0

    lax.fori_loop(0, groups, clear, 0)

    def place(s, _):
        p = slot_ref[s]
        u, v = lax.shift_right_logical(p, bits), p & (local_cols - 1)
        g, other = (u, v) if by_row else (v, u)
        n = number_ref[g]
        list_ref[g * cap + n] = s * 1024 + other
        number_ref[g] = n + 1
        return 0

    lax.fori_loop(0, count, place, 0)


def repeat_lanes(scale, width):
    return jnp.concatenate([scale] * (width // scale.shape[-1]), 1)


def scale_body(degree, cot, scale, out):
    edge, lanes = scale.shape[1:]
    width = cot.shape[1]
    for i in range(scale.shape[0]):
        part = degree[i // 2 : i // 2 + 1, i % 2 * edge : (i % 2 + 1) * edge]
        line = 1.0 / jnp.sqrt(part.astype(F32))
        scale[i] = jnp.broadcast_to(line, (lanes, edge)).T
    row = lax.axis_index("row")
    for e in range(2):
        value = cot[e * edge : (e + 1) * edge, :].astype(F32)
        out[e] = (value * repeat_lanes(scale[row * 2 + e], width)).T.astype(BF16)


def scale_kernel(degree, cotangent, edge):
    return run(
        scale_body,
        (degree, cotangent),
        [VMEM] * 2,
        [shape((2 * degree.shape[0], edge, 128), F32), shape((2, cotangent.shape[1], edge))],
    )


def prepare_body(count_ref, slot_ref, values, scale, out, *lists):
    local_cols = values.shape[0]
    list_tiles(count_ref[0], slot_ref, lists[0], lists[1], local_cols, True)
    list_tiles(count_ref[0], slot_ref, lists[2], lists[3], local_cols, False)

    def fill(i, _):
        wide = repeat_lanes(scale[i], values.shape[-1])
        out[i] = (values[i].astype(F32) * wide).astype(BF16)
        return 0

    lax.fori_loop(0, local_cols, fill, 0)


def prepare(count, slots, values, scale, block_rows):
    local_cols = values.shape[0]
    sizes = (block_rows, block_rows * local_cols, local_cols, block_rows * local_cols)
    return run(
        prepare_body,
        (count, slots, values, scale),
        [SMEM] * 2 + [VMEM] * 2,
        [shape(values.shape)] + [shape((n,), jnp.int32) for n in sizes],
        out_specs=[VMEM] + [SMEM] * 4,
        mib=12,
    )


def sum_large_group(g, number_ref, list_ref, total, product, store):
    cap = list_ref.shape[0] // number_ref.shape[0]
    n = number_ref[g]
    rest = jnp.where(n == 0, 0, ((n - 1) & 3) + 1)

    def take(start, width):
        entries = [list_ref[g * cap + start + j] for j in range(width)]
        return product([(lax.shift_right_logical(x, 10), x & 1023) for x in entries])

    @pl.when(n == 0)
    def _():
        total[...] = jnp.zeros_like(total)

    def exact(width):
        @pl.when(rest == width)
        def _():
            total[...] = take(0, width)

    for width in range(1, 5):
        exact(width)

    def four(m, _):
        total[...] += take(rest + 4 * m, 4)
        return 0

    lax.fori_loop(0, lax.shift_right_logical(n - rest, 2), four, 0)
    store(total[...])


def sum_group(g, number_ref, list_ref, total, product, store):
    cap = list_ref.shape[0] // number_ref.shape[0]
    n = number_ref[g]

    def take(start, width):
        entries = [list_ref[g * cap + start + j] for j in range(width)]
        return product([(lax.shift_right_logical(x, 10), x & 1023) for x in entries])

    def exact(width):
        @pl.when(n == width)
        def _():
            store(take(0, width))

    @pl.when(n == 0)
    def _():
        store(jnp.zeros_like(total))

    for width in range(1, 5):
        exact(width)

    @pl.when(n > 4)
    def _():
        total[...] = jnp.zeros_like(total)
        fours = lax.shift_right_logical(n, 2)

        def four(m, _):
            total[...] += take(4 * m, 4)
            return 0

        def one(m, _):
            total[...] += take(m, 1)
            return 0

        lax.fori_loop(0, fours, four, 0)
        lax.fori_loop(4 * fours, n, one, 0)
        store(total[...])


def joined_dot(lhs, rhs):
    return jnp.dot(
        jnp.concatenate(lhs, 1), jnp.concatenate(rhs, 0), preferred_element_type=F32
    )


def forward_body(first, flip, parts, number_ref, list_ref, tiles, source, out, total):
    col, row = lax.axis_index("col"), lax.axis_index("row")
    n = out.shape[0] // (2 * len(parts))

    def product(pieces):
        def locate(v):
            return v if first else v ^ (2 * row)

        return joined_dot([tiles[s] for s, _ in pieces], [source[locate(v)] for _, v in pieces])

    for place, part in enumerate(parts):
        for half in range(2):

            def block(i, _):
                def store(value):
                    out[(2 * place + half) * n + i] = value.astype(BF16)

                g = (col ^ (2 * (part * n + i) + flip)) * 2 + half
                sum_group(g, number_ref, list_ref, total, product, store)
                return 0

            lax.fori_loop(0, n, block, 0)


def forward(number, entries, tiles, source, first, flip, parts, after=()):
    edge, width = tiles.shape[-1], source.shape[-1]
    return run(
        functools.partial(forward_body, first, flip, parts),
        (number, entries, tiles, source),
        [SMEM, SMEM, VMEM, VMEM],
        [shape((len(parts) * number.shape[0] // 4, edge, width))],
        [pltpu.VMEM((edge, width), F32)],
        mib=16,
        after=after,
        cost=36,
    )[0]


def backward_body(n, number_ref, list_ref, tiles, *refs):
    pieces_in, (out, ranged, total) = refs[:n], refs[n:]
    mask, flips = lax.axis_index("row") * 2, lax.axis_index("col") * 2
    blocks, start = ranged.shape[0], 0
    for piece in pieces_in:
        ranged[start : start + piece.shape[0]] = piece[...]
        start += piece.shape[0]

    def product(pieces):
        def locate(u):
            x = u ^ flips
            return (x & 2) * (blocks // 4) + lax.shift_right_logical(x, 2) * 2 + (x & 1)

        return joined_dot([ranged[locate(u)] for _, u in pieces], [tiles[s] for s, _ in pieces])

    def block(i, _):
        def store(value):
            out[i] = value.astype(BF16)

        sum_large_group(i ^ mask, number_ref, list_ref, total, product, store)
        return 0

    lax.fori_loop(0, out.shape[0], block, 0)


def backward(number, entries, tiles, pieces, after=()):
    slots_n, edge, _ = tiles.shape
    _, width, _ = pieces[0].shape
    n, blocks = len(pieces), sum(x.shape[0] for x in pieces)
    return run(
        functools.partial(backward_body, n),
        (number, entries, tiles, *pieces),
        [SMEM, SMEM] + [VMEM] * (n + 1),
        [shape((number.shape[0], width, edge))],
        [pltpu.VMEM((blocks, width, edge), BF16), pltpu.VMEM((width, edge), F32)],
        mib=20,
        after=after,
    )[0]


def pair_sum_body(start, n, keep, come, *outs):
    for j, out in enumerate(outs):
        for half in range(2):
            i = (j // n * 2 + half) * n + j % n
            out[half] = (keep[i].astype(F32) + come[start + i].astype(F32)).astype(BF16)


def pair_sum(keep, come, start):
    n = come.shape[0] // 4
    return run(
        functools.partial(pair_sum_body, start, n),
        (keep, come),
        [VMEM] * 2,
        [shape((2, *keep.shape[1:]))] * (keep.shape[0] // 2),
        mib=12,
    )


def tree(items):
    while len(items) > 1:
        rest = items[len(items) // 2 * 2 :]
        items = [a + b for a, b in zip(items[::2], items[1::2])] + rest
    return items[0]


def relay_body(n, *refs):
    for source, out in zip(refs[:n], refs[n:]):
        out[...] = source[...]


def relay(items, after):
    return run(
        functools.partial(relay_body, len(items)),
        tuple(items),
        [VMEM] * len(items),
        [shape(x.shape) for x in items],
        after=after,
    )


def choose_body(last, across, middle, out_two, out_three, *outs):
    ends = jnp.logical_or(position("col") == 0, position("col") == last)
    for half in range(2):
        outs[half][0] = jnp.where(ends, out_two[half], across[half])
        outs[2 + half][0] = jnp.where(ends, out_three[half], middle[half])


def choose(last, across, middle, out_two, out_three, after):
    return run(
        functools.partial(choose_body, last),
        (across, middle, out_two, out_three),
        [VMEM] * 4,
        [shape((1, *across.shape[1:]))] * 4,
        after=after,
    )


def agg_body(n, *refs):
    scale, outs = refs[n], refs[n + 1 :]
    for half, out in enumerate(outs):
        summed = tree([x[half].astype(F32) for x in refs[:n]])
        wide = repeat_lanes(scale[lax.axis_index("row") * 2 + half], summed.shape[1])
        out[...] = (summed * wide).astype(BF16)


def aggregate(parts, scale, after):
    return run(
        functools.partial(agg_body, len(parts)),
        (*parts, scale),
        [VMEM] * (len(parts) + 1),
        [shape(parts[0].shape[1:])] * 2,
        after=after,
    )


def first_body(start, n, *refs):
    scale, weight, agg, out = refs[2 * n], refs[2 * n + 1], refs[-2], refs[-1]
    row = lax.axis_index("row")
    if start:
        agg[: 2 * start] = refs[2 * n + 2][...]
        out[: 2 * start] = refs[2 * n + 3][...]
    for i in range(2 * n):
        block = 2 * start + i
        value = jnp.dot(refs[i][...], weight[...], preferred_element_type=F32)
        wide = repeat_lanes(scale[block ^ (2 * row)], value.shape[1])
        out[block] = (jax.nn.gelu(value) * wide).astype(BF16)
        agg[block] = refs[i][...]


def first_layer(aggs, scale, weight, before=(), after=()):
    n = len(aggs)
    start = before[0].shape[0] // 2 if before else 0
    return run(
        functools.partial(first_body, start, n),
        (*[x for pair in aggs for x in pair], scale, weight, *before),
        [VMEM] * (2 * n + 2 + len(before)),
        [shape((2 * (start + n), *aggs[0][0].shape))] * 2,
        mib=14,
        after=after,
    )


def second_body(*refs):
    scale, weight, out, mark = refs[-4:]
    edge = refs[0].shape[1]
    mark[...] = jnp.zeros_like(mark)
    for half in range(2):
        summed = tree([x[half].astype(F32) for x in refs[:-4]])
        wide = repeat_lanes(scale[lax.axis_index("row") * 2 + half], summed.shape[1])
        agg = (summed * wide).astype(BF16)
        value = jnp.dot(agg, weight[...], preferred_element_type=F32)
        out[half * edge : (half + 1) * edge, :] = value.astype(BF16)


def second_layer(parts, scale, weight):
    halves, edge, width = parts[0].shape
    return run(
        second_body,
        (*parts, scale, weight),
        [VMEM] * (2 + len(parts)),
        [shape((halves * edge, width)), shape((8, 128), F32)],
    )


def grad_body(start, last, hidden_ref, aggs, outs, scale, w_first, w_second, *refs):
    row = lax.axis_index("row")
    core = lax.rem(lax.axis_index("col"), 2)
    first, second = refs[-2:]
    if start:
        first[...] = refs[0][...]
        second[...] = refs[1][...]
    else:
        first[...] = jnp.zeros_like(first)
        second[...] = jnp.zeros_like(second)

    def block(i, _):
        hidden, agg = hidden_ref[i], aggs[i]
        pre = jnp.dot(agg, w_first[...], preferred_element_type=F32)
        grad_hidden = lax.dot_general(
            hidden, w_second[...], (((0,), (1,)), ((), ())), preferred_element_type=F32
        )
        _, pullback = jax.vjp(jax.nn.gelu, pre)
        wide = repeat_lanes(scale[i ^ (2 * row)], pre.shape[1])
        grad_pre = pullback(grad_hidden * wide)[0].astype(BF16)
        first[...] += lax.dot_general(
            agg, grad_pre, (((0,), (0,)), ((), ())), preferred_element_type=F32
        )
        second[...] += lax.dot_general(
            outs[i], hidden, (((0,), (1,)), ((), ())), preferred_element_type=F32
        )
        return 0

    lax.fori_loop(start, aggs.shape[0], block, 0)
    if last:
        give, keep = refs[2:4]
        keep[...] = jnp.where(core == 0, first[...], second[...]).astype(BF16)
        give[...] = jnp.where(core == 0, second[...], first[...]).astype(BF16)


def weight_grads(start, hidden, aggs, outs, scale, w_first, w_second, before=(), after=()):
    dims = w_first.shape
    last = aggs.shape[0] == hidden.shape[0]
    return run(
        functools.partial(grad_body, start, last),
        (hidden, aggs, outs, scale, w_first, w_second, *before),
        [VMEM] * (6 + len(before)),
        [shape(dims)] * 2 if last else [shape(dims, F32)] * 2,
        [pltpu.VMEM(dims, F32)] * 2 if last else [],
        mib=26,
        after=after,
    )


def position(axis):
    if axis == "row":
        return lax.axis_index("row")
    return lax.shift_right_logical(lax.axis_index("col"), 1)


def split_body(n, axis, *refs):
    ins, outs = refs[:-n], refs[-n:]
    rows = ins[0].shape[0] // n
    for j in range(n):
        part = pl.ds(pl.multiple_of((position(axis) ^ j) * rows, rows), rows)
        outs[j][...] = tree([x[part, :].astype(F32) for x in ins]).astype(BF16)


def split_sum(items, n, axis, after=()):
    rows, width = items[0].shape
    return run(
        functools.partial(split_body, n, axis),
        tuple(items),
        [VMEM] * len(items),
        [shape((rows // n, width))] * n,
        after=after,
    )


def sum_body(n, *refs):
    refs[n][...] = tree([x[...].astype(F32) for x in refs[:n]]).astype(BF16)


def sum_parts(parts, after=()):
    return run(
        functools.partial(sum_body, len(parts)),
        tuple(parts),
        [VMEM] * len(parts),
        [shape(parts[0].shape)],
        after=after,
    )[0]


def join_body(n, axis, *refs):
    rows = refs[0].shape[0]
    for j in range(n):
        part = pl.ds(pl.multiple_of((position(axis) ^ j) * rows, rows), rows)
        refs[n][part, :] = refs[j][...]


def join(parts, axis):
    rows, width = parts[0].shape
    return run(
        functools.partial(join_body, len(parts), axis),
        tuple(parts),
        [VMEM] * len(parts),
        [shape((rows * len(parts), width))],
    )[0]


def select_body(mine, other, first, second):
    core = lax.rem(lax.axis_index("col"), 2)
    first[...] = jnp.where(core == 0, mine[...].astype(F32), other[...].astype(F32))
    second[...] = jnp.where(core == 0, other[...].astype(F32), mine[...].astype(F32))


def select(mine, other, after):
    return run(
        select_body, (mine, other), [VMEM] * 2, [shape(mine.shape, F32)] * 2, after=after
    )


COST = {
    scale_body: 36,
    prepare_body: 36,
    grad_body: 36,
    second_body: 36,
}


def per_device(features, degree, tile_vals, tile_slot, tile_count, w_first, w_second, cotangent):
    n_row, n_col = lax.axis_size("row"), lax.axis_size("col")
    line = n_col // 2
    piece, width = cotangent.shape
    tiles = tile_vals[0, 0]
    edge = tiles.shape[-1]
    local_cols = n_row * 2
    slots, count = tile_slot[0, 0], tile_count[0]

    def col_send(value, pairs):
        return lax.ppermute(
            value, "col", [(2 * a + k, 2 * b + k) for a, b in pairs for k in range(2)]
        )

    def line_flip(value, j):
        return col_send(value, [(a, a ^ j) for a in range(line)])

    def core_flip(value):
        return lax.ppermute(value, "col", [(a, a ^ 1) for a in range(n_col)])

    def row_flip(value, j):
        return lax.ppermute(value, "row", [(a, a ^ j) for a in range(n_row)])

    def scatter_line(own, behind, after=()):
        if line != 4:
            return [own[0]] + [line_flip(own[j], j) for j in range(1, line)], own[:2]
        to_three = col_send(own[3], [(0, 1), (3, 2)])
        to_two = col_send(behind, [(0, 1), (3, 2)])
        crossing = sum_parts([behind, to_three], own[:1])
        meeting = sum_parts([own[3], to_two], (crossing, *after))
        crossed = col_send(crossing, [(1, 2), (2, 1)])
        met = col_send(meeting, [(1, 2), (2, 1)])
        outward = sum_parts([own[1], crossed])
        return [own[0], line_flip(outward, 1), met], (meeting, outward)

    def gather_row(pair, behind):
        if n_row != 4:
            return [pair] + [[row_flip(x, j) for x in pair] for j in range(1, n_row)]
        x_first, y_second = row_flip(pair[0], 1), row_flip(pair[1], 2)
        x_second, y_first = row_flip(behind[1], 1), row_flip(behind[0], 2)
        diagonal = [row_flip(x_first, 2), row_flip(y_second, 1)]
        return [pair, [x_first, x_second], [y_first, y_second], diagonal]

    def gather_near(own):
        if line != 4:
            return []
        return [line_flip(own, 1), col_send(own, [(1, 2), (2, 1)])]

    def gather_far(own, near, middle, after, late):
        out_two = col_send(middle, [(1, 0), (2, 3)])
        (across,) = relay([col_send(near, [(1, 2), (2, 1)])], (*after, out_two))
        out_three = col_send(across, [(1, 0), (2, 3)])
        return [own, near, *choose(line - 1, across, middle, out_two, out_three, late)]

    halves = piece // edge
    scale, scaled = scale_kernel(degree[:, 0], cotangent, edge)
    early = gather_near(scaled)
    values = features[:, 0].reshape(local_cols, edge, width)
    first_in, number, entries, t_number, t_entries = prepare(
        count, slots, values, scale, 2 * n_col
    )

    def run_pass(source, first, cuts, after):
        sums = {}
        give = forward(number, entries, tiles, source, first, 1, (1, 0), after)
        come = core_flip(give)
        for cut in cuts:
            keep = forward(number, entries, tiles, source, first, 0, cut, after)
            pieces = pair_sum(keep, come, 0 if 1 in cut else line)
            for place, part in enumerate(cut):
                sums[part] = pieces[place * line // 2 : (place + 1) * line // 2]
            after = pieces[:1]
        return give, (*sums[0], *sums[1])

    give, own = run_pass(first_in, True, ((1, 0),), ())
    if early:
        early = relay(early, (give,))
    parts, late = scatter_line(own, own[2])
    if early:
        gathered = gather_far(scaled, *early, own[:1], late)
    else:
        gathered = [scaled] + [line_flip(scaled, j) for j in range(1, line)]
    ranged = gathered + [core_flip(g) for g in gathered]
    hidden = backward(t_number, t_entries, tiles, ranged)
    pair = aggregate(parts, scale, (hidden,))
    stacked = first_layer([pair], scale, w_first)
    spread = gather_row(pair, relay(pair, stacked[:1]))
    sums = weight_grads(0, hidden, *stacked, scale, w_first, w_second)
    for group in (spread[1:-1], spread[-1:]):
        start = stacked[0].shape[0]
        stacked = first_layer(group, scale, w_first, stacked, sums[:1])
        sums = weight_grads(start, hidden, *stacked, scale, w_first, w_second, sums)

    grad_give, grad_keep = sums
    _, own = run_pass(stacked[1], False, ((1,), (0,)), (grad_keep,))
    split = split_sum([grad_keep, core_flip(grad_give)], n_row, "row", own[2:3])
    moment = [split[0]] + [row_flip(split[j], j) for j in range(1, n_row)]
    if split[0].shape[0] % (16 * line) == 0:
        split = split_sum(moment, line, "line")
        moment = [split[0]] + [line_flip(split[j], j) for j in range(1, line)]
        summed = moment = sum_parts(moment)
        moment = join([moment] + [line_flip(moment, j) for j in range(1, line)], "line")
    else:
        moment = sum_parts(moment)
        moment = [moment] + [line_flip(moment, j) for j in range(1, line)]
        summed = moment = sum_parts(moment)
    (behind,) = relay(own[2:3], (summed,))
    parts, _ = scatter_line(own, behind, (moment,))
    moment = [moment] + [row_flip(moment, j) for j in range(1, n_row)]
    mine = join(moment, "row")
    logits, mark = second_layer(parts, scale, w_second)
    return logits, *select(mine, core_flip(mine), (mark,))


def solution(mesh):
    return jax.shard_map(
        per_device,
        mesh=mesh,
        in_specs=(
            P(None, "col", None, None),
            P(None, "col", None),
            P("row", "col", None, None, None),
            P("row", "col", None),
            P("row", "col"),
            P(),
            P(),
            P(("row", "col"), None),
        ),
        out_specs=(P(("row", "col"), None), P(), P()),
        check_vma=False,
    )
```
